256 devices in a mesh: seq: 32 (over x, y, z_hi), head: 8 (over z_lo, core).
Axes of the slice: x: 4, y: 4, z: 8 (z_hi: 2, z_lo: 4; z = z_hi * 4 + z_lo), core: 2. Of those that a mesh axis runs over, the one named last changes fastest.
Arguments:
- query_rows: bfloat16 [8192, 3072], P('seq', 'head'), may hold values from -27 to 27
- key_rows: bfloat16 [8192, 3072], P('seq', 'head'), may hold values from -6 to 6
- value_rows: bfloat16 [8192, 3072], P('seq', 'head'), may hold values from -6 to 6
- rates: float32 [8192, 16], P('seq', 'head'), may hold values from 0.1 to 1
- fw_decay: float32 [32, 16], P('seq', 'head'), may hold values from 0 to 1
- fw_step: float32 [16], P('head'), may hold values from 0.03 to 0.15
- fast_gate: float32 [16, 192, 384], P('head'), may hold values from -0.4375 to 0.4375
- fast_up: float32 [16, 192, 384], P('head'), may hold values from -0.4375 to 0.4375
- fast_down: float32 [16, 384, 192], P('head'), may hold values from -0.3125 to 0.3125
- ttt_gain: float32 [3072], P('head'), may hold values from 0.1 to 1.9
- attn_gain: float32 [3072], P('head'), may hold values from 0.1 to 1.9
- out_proj: bfloat16 [3072, 3072], P('head'), may hold values from -0.109375 to 0.109375
Outputs:
- layer_out: bfloat16 [8192, 3072], P(('seq', 'head'))
The draws below stay inside these ranges and needn't reach their ends.
All inputs are finite; a program needn't handle non-finite values.
Results may differ from the reference program's by a relative error of at most 0.0053.
Values may be sent and summed in bfloat16 or wider, within the bound.
No kernel may reach another device: no remote copies, remote signals or barrier semaphores. Data moves between devices by JAX's collectives and lax.ppermute only.
A program may use at most 192 MiB of HBM per device.

```python
import math
import jax
import jax.numpy as jnp
from jax import lax

HEAD_DIM = 192
FAST_DIM = 384
BLOCK = 256
WINDOW = 2048
NS_STEPS = 5
ATTN_LANES = 16
WIDTH = 3072
SEGMENT_TALLY = 32
SEQLEN = 8192


def paired_rows(key):
    starting_level = jax.random.fold_in(key, 11)
    first_key, second_key = jax.random.split(starting_level, 2)
    queries = jax.random.truncated_normal(first_key, -6.0, 6.0, (SEQLEN, WIDTH), jnp.float32)
    keys_out = jax.random.truncated_normal(second_key, -6.0, 6.0, (SEQLEN, WIDTH), jnp.float32)
    return (queries, keys_out)


def draw_query_rows(key, part):
    return paired_rows(key)[0].astype(jnp.bfloat16)


def draw_key_rows(key, part):
    return paired_rows(key)[1].astype(jnp.bfloat16)


def draw_fw_decay(key, part):
    starting_level = jax.random.fold_in(key, 23)
    diversity_seed, master_seed, dispersion_seed, cluster_seed, loss_target_seed, quick_weight_seed = jax.random.split(starting_level, 6)
    share = 0.5
    slow_heads = jax.random.uniform(diversity_seed, (ATTN_LANES,)) < share
    total_log = jnp.exp(jax.random.uniform(master_seed, (ATTN_LANES,), minval=math.log(0.2), maxval=math.log(1.0)))
    factor = jnp.exp(jax.random.uniform(dispersion_seed, (SEGMENT_TALLY, ATTN_LANES), minval=math.log(0.5), maxval=math.log(2.0)))
    lasting_decay_factor = jnp.exp(-total_log[None, :] * factor / SEGMENT_TALLY)
    fast_keep = jnp.exp(jax.random.uniform(quick_weight_seed, (SEGMENT_TALLY, ATTN_LANES), minval=math.log(0.05), maxval=math.log(0.3)))
    cluster_sets = jax.random.uniform(cluster_seed, (SEGMENT_TALLY, ATTN_LANES)) < 2.0 / SEGMENT_TALLY
    cluster_loss = jax.random.uniform(loss_target_seed, (SEGMENT_TALLY, ATTN_LANES), minval=0.5, maxval=0.8)
    lasting_decay_factor = lasting_decay_factor * jnp.where(cluster_sets, cluster_loss, 1.0)
    return jnp.where(slow_heads[None, :], lasting_decay_factor, fast_keep).astype(jnp.float32)


def level_of(key, shape, cuts, smallest, top_value):
    loudness, own = 1.0, jax.random.fold_in(key, 6)
    for dim, blocks in cuts:
        draws = jnp.exp(jax.random.uniform(jax.random.fold_in(own, dim), (blocks,), jnp.float32, smallest / len(cuts), top_value / len(cuts)))
        loudness = loudness * jnp.repeat(draws, shape[dim] // blocks).reshape([-1 if axis == dim else 1 for axis in range(len(shape))])
    return loudness


def bell_draw(stream_key, shape, scale, most, pieces=(), kind=jnp.bfloat16):
    level = level_of(stream_key, shape, pieces, -0.22, 0.18) if pieces else 1.0
    entries = jax.random.normal(stream_key, shape, jnp.float32) * scale * level
    return jnp.minimum(jnp.maximum(entries, -most), most).astype(kind)


def setup_inputs(seed: int = 0) -> dict:
    arg_keys = jax.random.split(jax.random.key(seed), 13)
    return {
        "query_rows": draw_query_rows(jax.random.fold_in(arg_keys[12], 71), 0),
        "key_rows": draw_key_rows(jax.random.fold_in(arg_keys[12], 71), 0),
        "value_rows": bell_draw(arg_keys[2], (SEQLEN, WIDTH), 1.0, 6.0, ((0, 32), (1, 8))),
        "rates": jnp.clip(jnp.exp(math.log(1.0) - 2.3025851 * jax.random.uniform(arg_keys[3], (SEQLEN, ATTN_LANES), jnp.float32) ** level_of(arg_keys[3], (SEQLEN, ATTN_LANES), ((0, 32), (1, 8)), -0.2, 0.2)), 0.1, 1.0),
        "fw_decay": draw_fw_decay(jax.random.fold_in(arg_keys[12], 71), 0),
        "fw_step": jnp.clip(jnp.exp(math.log(0.15) - 1.609438 * jax.random.uniform(arg_keys[5], (ATTN_LANES,), jnp.float32) ** level_of(arg_keys[5], (ATTN_LANES,), ((0, 8),), -0.2, 0.2)), 0.03, 0.15),
        "fast_gate": bell_draw(arg_keys[6], (ATTN_LANES, HEAD_DIM, FAST_DIM), HEAD_DIM ** -0.5, 0.4375, ((0, 8),), jnp.float32),
        "fast_up": bell_draw(arg_keys[7], (ATTN_LANES, HEAD_DIM, FAST_DIM), HEAD_DIM ** -0.5, 0.4375, ((0, 8),), jnp.float32),
        "fast_down": bell_draw(arg_keys[8], (ATTN_LANES, FAST_DIM, HEAD_DIM), FAST_DIM ** -0.5, 0.3125, ((0, 8),), jnp.float32),
        "ttt_gain": jnp.clip(1.0 + 0.18 * jax.random.normal(arg_keys[9], (WIDTH,), jnp.float32), 0.1, 1.9),
        "attn_gain": jnp.clip(1.0 + 0.18 * jax.random.normal(arg_keys[10], (WIDTH,), jnp.float32), 0.1, 1.9),
        "out_proj": bell_draw(arg_keys[11], (WIDTH, WIDTH), WIDTH ** -0.5, 0.109375, ((0, 8),)),
    }


FULL_PRECISION = lax.Precision.HIGHEST
coef_a = 3.4445
coef_b = -4.775
coef_c = 2.0315

def matmul(left_mat, right_mat):
    return jnp.dot(left_mat, right_mat, precision=FULL_PRECISION, preferred_element_type=jnp.float32)

def rms_rows(values):
    return values * lax.rsqrt(lax.optimization_barrier(jnp.mean(values * values, axis=-1, keepdims=True)) + 1e-06)

def silu_slope(pre_act):
    sigmoid_z = jax.nn.sigmoid(pre_act)
    return sigmoid_z * (1.0 + pre_act * (1.0 - sigmoid_z))

def orthogonalize(gradient):
    current = gradient / (jnp.sqrt(jnp.sum(gradient * gradient)) + 1e-07)
    for sweep_id in range(NS_STEPS):
        gram_mat = matmul(current, current.T)
        poly_mat = coef_b * gram_mat + coef_c * matmul(gram_mat, gram_mat)
        current = coef_a * current + matmul(poly_mat, current)
    return current

def fast_apply(inputs, gate_mat, up_mat, down_mat):
    return matmul(jax.nn.silu(matmul(inputs, gate_mat)) * matmul(inputs, up_mat), down_mat)

def fast_update(key_norm, targets, token_rates, gate_mat, up_mat, down_mat, step_size):
    pre_gate = matmul(key_norm, gate_mat)
    pre_up = matmul(key_norm, up_mat)
    active = jax.nn.silu(pre_gate)
    middle = active * pre_up
    out_grad = -token_rates[:, None] * targets
    grad_down = matmul(middle.T, out_grad)
    mid_grad = matmul(out_grad, down_mat.T)
    grad_gate = matmul(key_norm.T, mid_grad * pre_up * silu_slope(pre_gate))
    grad_up = matmul(key_norm.T, mid_grad * active)
    return (-step_size * orthogonalize(grad_gate), -step_size * orthogonalize(grad_up), -step_size * orthogonalize(grad_down.T).T)

def window_attention(query_head, key_head, value_head, allowed, scale):
    scores = lax.dot_general(query_head, key_head, (((1,), (1,)), ((), ())), preferred_element_type=jnp.float32) * scale
    scores = jnp.where(allowed, scores, -jnp.inf)
    row_max = lax.optimization_barrier(jnp.max(scores, axis=-1, keepdims=True))
    weights = jnp.exp(scores - row_max)
    row_total = lax.optimization_barrier(jnp.sum(weights, axis=-1, keepdims=True))
    return jnp.dot(weights.astype(jnp.bfloat16), value_head, preferred_element_type=jnp.float32) / row_total

def split_heads(rows_mat, head_count):
    return rows_mat.reshape(rows_mat.shape[0], head_count, -1).transpose(1, 0, 2)

def reference(query_rows, key_rows, value_rows, rates, fw_decay, fw_step, fast_gate, fast_up, fast_down, ttt_gain, attn_gain, out_proj):
    scale = 1.0 / math.sqrt(HEAD_DIM)
    key_pad = jnp.concatenate([jnp.zeros((WINDOW, WIDTH), key_rows.dtype), key_rows], axis=0)
    value_pad = jnp.concatenate([jnp.zeros((WINDOW, WIDTH), value_rows.dtype), value_rows], axis=0)
    query_pos = jnp.arange(BLOCK, dtype=jnp.int32)[:, None]
    key_cols = jnp.arange(WINDOW + BLOCK, dtype=jnp.int32)[None, :]
    gain_ttt = ttt_gain.reshape(ATTN_LANES, 1, HEAD_DIM)
    gain_attn = attn_gain.reshape(ATTN_LANES, 1, HEAD_DIM)

    def block_step(states, block_id):
        state_gate, state_up, state_down = states
        start = (block_id * BLOCK).astype(jnp.int32)
        queries = lax.dynamic_slice_in_dim(query_rows, start, BLOCK, 0)
        keys_here = lax.dynamic_slice_in_dim(key_rows, start, BLOCK, 0)
        values_here = lax.dynamic_slice_in_dim(value_rows, start, BLOCK, 0)
        rates_here = lax.dynamic_slice_in_dim(rates, start, BLOCK, 0)
        window_keys = lax.dynamic_slice_in_dim(key_pad, start, WINDOW + BLOCK, 0)
        window_values = lax.dynamic_slice_in_dim(value_pad, start, WINDOW + BLOCK, 0)
        token_pos = start + query_pos
        key_pos = start - WINDOW + key_cols
        allowed = (key_pos <= token_pos) & (key_pos > token_pos - WINDOW) & (key_pos >= 0)
        attended = jax.vmap(window_attention, (0, 0, 0, None, None))(split_heads(queries, ATTN_LANES), split_heads(window_keys, ATTN_LANES), split_heads(window_values, ATTN_LANES), allowed, scale)
        query_norm = rms_rows(split_heads(queries, ATTN_LANES).astype(jnp.float32))
        key_norm = rms_rows(split_heads(keys_here, ATTN_LANES).astype(jnp.float32))
        applied = jax.vmap(fast_apply)(query_norm, fast_gate + state_gate, fast_up + state_up, fast_down + state_down)
        upd_gate, upd_up, upd_down = jax.vmap(fast_update)(key_norm, split_heads(values_here, ATTN_LANES).astype(jnp.float32), rates_here.T, fast_gate, fast_up, fast_down, fw_step)
        retention = fw_decay[block_id][:, None, None]
        new_states = (retention * state_gate + upd_gate, retention * state_up + upd_up, retention * state_down + upd_down)
        mixed = rms_rows(applied) * gain_ttt + rms_rows(attended) * gain_attn
        mixed = mixed.transpose(1, 0, 2).reshape(BLOCK, WIDTH).astype(jnp.bfloat16)
        return (new_states, mixed)
    init = (jnp.zeros((ATTN_LANES, HEAD_DIM, FAST_DIM), jnp.float32), jnp.zeros((ATTN_LANES, HEAD_DIM, FAST_DIM), jnp.float32), jnp.zeros((ATTN_LANES, FAST_DIM, HEAD_DIM), jnp.float32))
    final_states, mixed = lax.scan(block_step, init, jnp.arange(SEGMENT_TALLY, dtype=jnp.int32))
    mixed = mixed.reshape(SEQLEN, WIDTH)
    return jnp.dot(mixed, out_proj, preferred_element_type=jnp.float32).astype(jnp.bfloat16)
```

```python
import functools
import math

import jax
import jax.numpy as jnp
from jax import lax
from jax.experimental import pallas as pl
from jax.experimental.pallas import tpu as pltpu
from jax.sharding import Mesh, PartitionSpec as P

F32 = jnp.float32
BF16 = jnp.bfloat16
HD = 192
FD = 384
BLK = 256
WIDTH = 3072
NS_STEPS = 5
PAIRS = 16
CHUNK = 108
CROWS = 112
PAY = 400
COEF = (3.4445, -4.775, 2.0315)
VMEM_CAP = 32 * 1024 * 1024
VM = pl.BlockSpec(memory_space=pltpu.VMEM)
SM = pl.BlockSpec(memory_space=pltpu.SMEM)


def call(body, outs, ins, flops, nbytes, trans=0, scratch=(), in_specs=None):
    return pl.pallas_call(
        body,
        out_shape=outs,
        in_specs=in_specs or [VM] * len(ins),
        out_specs=jax.tree.map(lambda _: VM, outs),
        scratch_shapes=list(scratch),
        compiler_params=pltpu.CompilerParams(vmem_limit_bytes=VMEM_CAP),
        cost_estimate=pl.CostEstimate(flops=flops, bytes_accessed=nbytes, transcendentals=trans),
    )(*ins)


def nn(a, b):
    return lax.dot_general(a, b, (((1,), (0,)), ((), ())), preferred_element_type=F32)


def nt(a, b):
    return lax.dot_general(a, b, (((1,), (1,)), ((), ())), preferred_element_type=F32)


def split(x):
    hi = x.astype(BF16)
    return hi, (x - hi.astype(F32)).astype(BF16)


def nn3(a, b):
    return nn(a[0], b[0]) + (nn(a[0], b[1]) + nn(a[1], b[0]))


def nt3(a, b):
    return nt(a[0], b[0]) + (nt(a[0], b[1]) + nt(a[1], b[0]))


def three(x):
    hi = x.astype(BF16).astype(F32)
    mid = (x - hi).astype(BF16).astype(F32)
    low = x - hi - mid
    row = lax.broadcasted_iota(jnp.int32, x.shape, 0)
    return jnp.where(row == 0, hi, jnp.where(row == 1, mid, jnp.where(row == 2, low, 0.0)))


def pick(ref, zh):
    return jnp.where(zh == 0, ref[:, :HD], ref[:, HD:])


def pack_body(q_ref, k_ref, v_ref, r_ref, d_ref, own_ref, send_ref):
    zh = lax.axis_index("zh")
    for out_ref, who in ((own_ref, zh), (send_ref, 1 - zh)):
        out_ref[0:BLK, 0:HD] = pick(k_ref, who)
        out_ref[0:BLK, HD:] = pick(v_ref, who)
        q = pick(q_ref, who)
        out_ref[BLK : BLK + 128, 0:HD] = q[0:128]
        out_ref[BLK : BLK + 128, HD:] = q[128:256]
        rate = jnp.where(who == 0, r_ref[:, 0:1], r_ref[:, 1:2])
        rate_row = jnp.broadcast_to(rate, (BLK, 128)).T[0:16, :]
        decay = jnp.where(who == 0, d_ref[0, 0], d_ref[0, 1])
        row = jnp.concatenate([rate_row, jnp.full((16, 128), decay, F32)], axis=1)
        out_ref[384:400, :] = three(row).astype(BF16)


def tail(pay_ref):
    rows = pay_ref[384:400, :].astype(F32)
    return rows[0:1] + rows[1:2] + rows[2:3]


def queries(pay_ref):
    both = pay_ref[BLK : BLK + 128, :]
    return jnp.concatenate([both[:, :HD], both[:, HD:]], axis=0)


def fast_updates(pay_ref, g_ref, u_ref, d_ref, step_ref, work_ref):
    zh = lax.axis_index("zh")
    k = pay_ref[0:BLK, 0:HD]
    v = pay_ref[0:BLK, HD:]
    kf = k.astype(F32)
    rk = lax.rsqrt(jnp.mean(kf * kf, axis=1, keepdims=True) + 1e-6)
    rate = jnp.broadcast_to(tail(pay_ref)[:, :BLK], (128, BLK)).T[:, 0:1]
    gh, gl = split(g_ref[zh])
    uh, ul = split(u_ref[zh])
    dh, dl = split(d_ref[zh])
    pre_gate = rk * (nn(k, gh) + nn(k, gl))
    pre_up = rk * (nn(k, uh) + nn(k, ul))
    back = -rate * (nt(v, dh) + nt(v, dl))
    sig = jax.nn.sigmoid(pre_gate)
    act = pre_gate * sig
    mid_h, mid_l = split(-rate * (act * pre_up))
    gate_h, gate_l = split(rk * (back * pre_up * (sig * (1.0 + pre_gate * (1.0 - sig)))))
    up_h, up_l = split(rk * (back * act))
    kt = k.T
    vt = v.T
    work_ref[0] = nn(kt, gate_h) + nn(kt, gate_l)
    work_ref[1] = nn(kt, up_h) + nn(kt, up_l)
    work_ref[2] = nn(vt, mid_h) + nn(vt, mid_l)
    for i in range(3):
        grad = work_ref[i]
        norm = jnp.sqrt(jnp.sum(grad * grad, keepdims=True)) + 1e-7
        work_ref[i] = grad / norm

    def sweep(_, carry):
        for i in range(3):
            x = work_ref[i]
            xs = split(x)
            gram = nt3(xs, xs)
            gs = split(gram)
            poly = COEF[1] * gram + COEF[2] * nn3(gs, gs)
            work_ref[i] = COEF[0] * x + nn3(split(poly), xs)
        return carry

    lax.fori_loop(0, NS_STEPS, sweep, 0)
    return -step_ref[zh]


def first_body(pay_ref, g_ref, u_ref, d_ref, step_ref, upd_ref, work_ref):
    scale = fast_updates(pay_ref, g_ref, u_ref, d_ref, step_ref, work_ref)
    for i in range(3):
        upd_ref[i] = scale * work_ref[i]


def second_body(own_ref, pay_ref, upd_ref, g_ref, u_ref, d_ref, step_ref, even_ref, send_ref, work_ref, flat_ref):
    scale = fast_updates(pay_ref, g_ref, u_ref, d_ref, step_ref, work_ref)
    zh = lax.axis_index("zh")
    mine = tail(own_ref)[:, BLK:]
    theirs = tail(pay_ref)[:, BLK:]
    keep_even = jnp.where(zh == 0, mine, theirs)
    keep_odd = jnp.where(zh == 0, theirs, mine)
    flat_ref[PAIRS * CHUNK :, :] = jnp.zeros((64, 128), F32)
    for i in range(3):
        other = scale * work_ref[i]
        own = upd_ref[i]
        even = jnp.where(zh == 0, own, other)
        odd = jnp.where(zh == 0, other, own)
        even_ref[i] = even
        for j in range(3):
            cols = slice(j * 128, (j + 1) * 128)
            flat_ref[(3 * i + j) * HD : (3 * i + j + 1) * HD, :] = keep_odd * even[:, cols] + odd[:, cols]
    keep = three(jnp.broadcast_to(keep_even * keep_odd, (16, 128)))[0:4]
    for c in range(PAIRS):
        send_ref[c] = jnp.concatenate([flat_ref[c * CHUNK : (c + 1) * CHUNK, :], keep], axis=0).astype(BF16)


def scan_body(in_ref, out_ref):
    run = jnp.zeros((CROWS, 128), F32)
    for j in range(PAIRS):
        out_ref[j] = run.astype(BF16)
        if j < PAIRS - 1:
            here = in_ref[j].astype(F32)
            keep = here[CHUNK : CHUNK + 1] + here[CHUNK + 1 : CHUNK + 2] + here[CHUNK + 2 : CHUNK + 3]
            run = keep * run + here


def attend_body(own_ref, recv_ref, pair_ref, w1_ref, w2_ref, w3_ref, w4_ref, gain_ref, out_ref, score_ref):
    zh = lax.axis_index("zh")
    pair = lax.axis_index("x") * 4 + lax.axis_index("y")
    scale = 1.0 / math.sqrt(HD)
    wins = (pair_ref, w1_ref, w2_ref, w3_ref, w4_ref)
    q_own = queries(own_ref)
    q_recv = queries(recv_ref)
    gain = jnp.where(zh == 0, gain_ref[:, :HD], gain_ref[:, HD:])
    row = lax.broadcasted_iota(jnp.int32, (BLK, BLK), 0)
    col = lax.broadcasted_iota(jnp.int32, (BLK, BLK), 1)

    def rows_of(parity):
        slot = zh if parity == 0 else 1 - zh
        return pl.ds(pl.multiple_of(slot * BLK, BLK), BLK)

    for parity in range(2):
        q = jnp.where(zh == parity, q_own, q_recv)
        blocks = [(o, e) for o in (4, 3, 2, 1, 0) for e in (0, 1)]
        blocks = blocks[:9] if parity == 0 else blocks[1:]
        top = None
        for n, (o, e) in enumerate(blocks):
            k = wins[o][rows_of(e), 0:HD]
            s = nt(q, k) * scale
            if n == 0:
                s = jnp.where(col > row, s, -1e30)
            if n == 8:
                s = jnp.where(col <= row, s, -1e30)
            if o > 0:
                s = s + jnp.where(pair >= o, 0.0, -1e30)
            score_ref[n] = s
            top = s if top is None else jnp.maximum(top, s)
        top = jnp.max(top, axis=1, keepdims=True)
        total = None
        acc = None
        for n, (o, e) in enumerate(blocks):
            w = jnp.exp(score_ref[n] - top)
            total = w if total is None else total + w
            part = nn(w.astype(BF16), wins[o][rows_of(e), HD:])
            acc = part if acc is None else acc + part
        att = acc / jnp.sum(total, axis=1, keepdims=True)
        norm = lax.rsqrt(jnp.mean(att * att, axis=1, keepdims=True) + 1e-6)
        out_ref[parity] = att * norm * gain


def apply_body(pre_ref, even_ref, own_ref, recv_ref, g_ref, u_ref, d_ref, gain_ref, att_ref, out_ref, flat_ref):
    zh = lax.axis_index("zh")
    for c in range(PAIRS):
        flat_ref[c * CHUNK : (c + 1) * CHUNK, :] = pre_ref[c].astype(F32)[0:CHUNK]
    keep = jnp.where(zh == 0, tail(own_ref)[:, BLK : BLK + 1], tail(recv_ref)[:, BLK : BLK + 1])
    gain = jnp.where(zh == 0, gain_ref[:, :HD], gain_ref[:, HD:])
    q_own = queries(own_ref)
    q_recv = queries(recv_ref)
    base = (g_ref[zh], u_ref[zh], d_ref[zh].T)
    for parity in range(2):
        q = jnp.where(zh == parity, q_own, q_recv)
        qf = q.astype(F32)
        rq = lax.rsqrt(jnp.mean(qf * qf, axis=1, keepdims=True) + 1e-6)
        mats = []
        for i in range(3):
            state = jnp.concatenate(
                [flat_ref[(3 * i + j) * HD : (3 * i + j + 1) * HD, :] for j in range(3)], axis=1
            )
            if parity == 1:
                state = keep * state + even_ref[i]
            mats.append(split(base[i] + state))
        gate = rq * (nn(q, mats[0][0]) + nn(q, mats[0][1]))
        up = rq * (nn(q, mats[1][0]) + nn(q, mats[1][1]))
        applied = nt3(split(gate * jax.nn.sigmoid(gate) * up), mats[2])
        norm = lax.rsqrt(jnp.mean(applied * applied, axis=1, keepdims=True) + 1e-6)
        mixed = (applied * norm * gain + att_ref[parity]).astype(BF16)
        for c in range(2):
            for z in range(4):
                out_ref[c * 2 + parity, (z % 2) * 32 : (z % 2) * 32 + 32, (z // 2) * HD : (z // 2 + 1) * HD] = mixed[
                    z * 64 + c * 32 : z * 64 + c * 32 + 32
                ]


def project_body(mix_ref, own_ref, other_ref, out_ref):
    core = lax.axis_index("c")
    total = None
    for w_ref, which in ((own_ref, core), (other_ref, 1 - core)):
        for zh in range(2):
            part = mix_ref[which * 2 + zh]
            part = jnp.concatenate([part[:, :HD], part[:, HD:]], axis=0)
            part = nn(part, w_ref[zh * HD : (zh + 1) * HD, :])
            total = part if total is None else total + part
    out_ref[...] = total.astype(BF16)


def local(q, k, v, rates, decay, step, gate, up, down, ttt_gain, attn_gain, proj):
    sds = jax.ShapeDtypeStruct
    pay = sds((PAY, FD), BF16)
    own, send = call(
        pack_body, (pay, pay), (q, k, v, rates, decay), 0, 2_000_000, in_specs=[VM, VM, VM, VM, SM]
    )
    recv = lax.ppermute(send, "zh", [(0, 1), (1, 0)])
    proj_other = lax.ppermute(proj, "c", [(0, 1), (1, 0)])
    mats = sds((3, HD, FD), F32)
    work = pltpu.VMEM((3, HD, FD), F32)
    flat = pltpu.VMEM((PAIRS * CHUNK + 64, 128), F32)
    upd = call(
        first_body,
        mats,
        (own, gate, up, down, step),
        6_000_000_000,
        3_000_000,
        in_specs=[VM] * 4 + [SM],
        scratch=[work],
    )
    pair_kv = jnp.concatenate([own[:BLK], recv[:BLK]], axis=0)
    wins = [
        lax.ppermute(pair_kv, ("x", "y"), [(i, i + o) for i in range(PAIRS - o)]) for o in (1, 2, 3, 4)
    ]
    even, outgoing = call(
        second_body,
        (mats, sds((PAIRS, CROWS, 128), BF16)),
        (own, recv, upd, gate, up, down, step),
        6_000_000_000,
        4_000_000,
        in_specs=[VM] * 6 + [SM],
        scratch=[work, flat],
    )
    pieces = lax.all_to_all(outgoing, ("x", "y"), 0, 0, tiled=True)
    sums = call(scan_body, sds((PAIRS, CROWS, 128), BF16), (pieces,), 500_000, 1_000_000)
    prefix = lax.all_to_all(sums, ("x", "y"), 0, 0, tiled=True)
    att = call(
        attend_body,
        sds((2, BLK, HD), F32),
        (own, recv, pair_kv, *wins, attn_gain.reshape(1, FD)),
        1_000_000_000,
        3_000_000,
        1_200_000,
        scratch=[pltpu.VMEM((9, BLK, BLK), F32)],
    )
    mixed = call(
        apply_body,
        sds((4, 64, FD), BF16),
        (prefix, even, own, recv, gate, up, down, ttt_gain.reshape(1, FD), att),
        600_000_000,
        5_000_000,
        scratch=[flat],
    )
    mixed = lax.all_to_all(mixed, ("c", "zh"), 0, 0, tiled=True)
    tile = 512
    partial = pl.pallas_call(
        project_body,
        out_shape=sds((128, WIDTH), BF16),
        grid=(WIDTH // tile,),
        in_specs=[
            pl.BlockSpec((4, 64, FD), lambda i: (0, 0, 0)),
            pl.BlockSpec((FD, tile), lambda i: (0, i)),
            pl.BlockSpec((FD, tile), lambda i: (0, i)),
        ],
        out_specs=pl.BlockSpec((128, tile), lambda i: (0, i)),
        compiler_params=pltpu.CompilerParams(vmem_limit_bytes=VMEM_CAP),
        cost_estimate=pl.CostEstimate(flops=600_000_000, bytes_accessed=6_000_000, transcendentals=0),
    )(mixed, proj, proj_other)
    parts = lax.all_to_all(partial.reshape(4, 32, WIDTH), "zl", 0, 0, tiled=True)
    return jnp.sum(parts.astype(F32), axis=0).astype(BF16)


def solution(mesh):
    fine = Mesh(mesh.devices.reshape(4, 4, 2, 4, 2), ("x", "y", "zh", "zl", "c"))
    seq = ("x", "y", "zh")
    head = ("zl", "c")
    in_specs = (
        P(seq, head),
        P(seq, head),
        P(seq, head),
        P(seq, head),
        P(seq, head),
        P(head),
        P(head, None, None),
        P(head, None, None),
        P(head, None, None),
        P(head),
        P(head),
        P(head, None),
    )
    out_specs = P(("x", "y", "zh", "zl", "c"), None)
    return jax.shard_map(local, mesh=fine, in_specs=in_specs, out_specs=out_specs, check_vma=False)
```

```python
import functools
import math

import jax
import jax.numpy as jnp
from jax import lax
from jax.experimental import pallas as pl
from jax.experimental.pallas import tpu as pltpu
from jax.sharding import Mesh, PartitionSpec as P

F32 = jnp.float32
BF16 = jnp.bfloat16
HD = 192
FD = 384
BLK = 256
WIDTH = 3072
NS_STEPS = 5
PAIRS = 16
CHUNK = 108
CROWS = 112
PAY = 400
COEF = (3.4445, -4.775, 2.0315)
VMEM_CAP = 60 * 1024 * 1024


class Lazy:
    def __init__(self, copy, ref):
        self.copy, self.ref = copy, ref

    def get(self):
        if self.copy is not None:
            self.copy.wait()
            self.copy = None
        return self.ref


def call(body, outs, ins, flops, nbytes, trans=0, scratch=(), mine=()):
    outs = list(outs)
    n_in, n_out = len(ins), len(outs)
    shapes = [a.shape[1:] if i in mine else a.shape for i, a in enumerate(ins)]

    def kernel(*refs):
        in_refs, out_refs = refs[:n_in], refs[n_in : n_in + n_out]
        rest = refs[n_in + n_out :]
        in_vm, out_vm = rest[:n_in], rest[n_in : n_in + n_out]
        in_sem, out_sem, extra = rest[n_in + n_out], rest[n_in + n_out + 1], rest[n_in + n_out + 2 :]
        zh = lax.axis_index("zh")
        lazy = []
        for i in range(n_in):
            src = in_refs[i].at[zh] if i in mine else in_refs[i]
            copy = pltpu.make_async_copy(src, in_vm[i], in_sem.at[i])
            copy.start()
            lazy.append(Lazy(copy, in_vm[i]))
        copies = [pltpu.make_async_copy(out_vm[i], out_refs[i], out_sem.at[i]) for i in range(n_out)]
        body(*lazy, *out_vm, *extra)
        for copy in copies:
            copy.start()
        for item in lazy:
            item.get()
        for copy in copies:
            copy.wait()

    any_spec = pl.BlockSpec(memory_space=pltpu.MemorySpace.HBM)
    return pl.pallas_call(
        kernel,
        out_shape=outs,
        in_specs=[any_spec] * n_in,
        out_specs=[any_spec] * n_out,
        scratch_shapes=[pltpu.VMEM(sh, a.dtype) for sh, a in zip(shapes, ins)]
        + [pltpu.VMEM(o.shape, o.dtype) for o in outs]
        + [pltpu.SemaphoreType.DMA((n_in,)), pltpu.SemaphoreType.DMA((n_out,))]
        + list(scratch),
        compiler_params=pltpu.CompilerParams(vmem_limit_bytes=VMEM_CAP),
        cost_estimate=pl.CostEstimate(flops=flops, bytes_accessed=nbytes, transcendentals=trans),
    )(*ins)


def nn(a, b):
    return lax.dot_general(a, b, (((1,), (0,)), ((), ())), preferred_element_type=F32)


def nt(a, b):
    return lax.dot_general(a, b, (((1,), (1,)), ((), ())), preferred_element_type=F32)


def split(x):
    hi = x.astype(BF16)
    return hi, (x - hi.astype(F32)).astype(BF16)


def nn3(a, b):
    return nn(a[0], b[0]) + (nn(a[0], b[1]) + nn(a[1], b[0]))


def nt3(a, b):
    return nt(a[0], b[0]) + (nt(a[0], b[1]) + nt(a[1], b[0]))


def three(x):
    hi = x.astype(BF16).astype(F32)
    mid = (x - hi).astype(BF16).astype(F32)
    low = x - hi - mid
    row = lax.broadcasted_iota(jnp.int32, x.shape, 0)
    return jnp.where(row == 0, hi, jnp.where(row == 1, mid, jnp.where(row == 2, low, 0.0)))


def pick(ref, who):
    return jnp.where(who == 0, ref[:, :HD], ref[:, HD:])


def one_of(row, who):
    return jnp.where(who == 0, row[0:1], row[1:2])


def fill(out_ref, q, k, v, rate_row, decay):
    out_ref[0:BLK, 0:HD] = k
    out_ref[0:BLK, HD:] = v
    out_ref[BLK : BLK + 128, 0:HD] = q[0:128]
    out_ref[BLK : BLK + 128, HD:] = q[128:256]
    row = jnp.concatenate([rate_row, jnp.broadcast_to(decay, (1, 128))], axis=1)
    out_ref[384:400, :] = three(jnp.broadcast_to(row, (16, FD))).astype(BF16)


def pack_body(q, k, v, r, d, send_ref):
    who = 1 - lax.axis_index("zh")
    fill(
        send_ref,
        pick(q.get(), who),
        pick(k.get(), who),
        pick(v.get(), who),
        one_of(r.get()[...], who),
        jnp.where(who == 0, d.get()[:, 0:1], d.get()[:, 1:2]),
    )


def tail(pay_ref):
    rows = pay_ref[384:400, :].astype(F32)
    return rows[0:1] + rows[1:2] + rows[2:3]


def queries(pay_ref):
    both = pay_ref[BLK : BLK + 128, :]
    return jnp.concatenate([both[:, :HD], both[:, HD:]], axis=0)


def orthogonalize(mats):
    norms = [jnp.sqrt(jnp.sum(m * m, keepdims=True)) + 1e-7 for m in mats]
    mats = [m / n for m, n in zip(mats, norms)]
    for _ in range(NS_STEPS):
        parts = [split(x) for x in mats]
        grams = []
        for hi, lo in parts:
            cross = nt(hi, lo)
            grams.append(nt(hi, hi) + (cross + cross.T))
        polys = []
        for gram in grams:
            hi, lo = split(gram)
            cross = nn(hi, lo)
            polys.append(split(COEF[1] * gram + COEF[2] * (nn(hi, hi) + (cross + cross.T))))
        mats = [COEF[0] * x + nn3(p, s) for x, p, s in zip(mats, polys, parts)]
    return mats


def fast_updates(k, v, rate_row, g, u, dt, step):
    kf = k.astype(F32)
    rk = lax.rsqrt(jnp.mean(kf * kf, axis=1, keepdims=True) + 1e-6)
    rate = jnp.broadcast_to(rate_row, (128, BLK)).T[:, 0:1]
    gh, gl = split(g.get()[...])
    pre_gate = rk * (nn(k, gh) + nn(k, gl))
    uh, ul = split(u.get()[...])
    pre_up = rk * (nn(k, uh) + nn(k, ul))
    dh, dl = split(dt.get()[...])
    back = -rate * (nn(v, dh) + nn(v, dl))
    sig = jax.nn.sigmoid(pre_gate)
    act = pre_gate * sig
    mid_h, mid_l = split(-rate * (act * pre_up))
    gate_h, gate_l = split(rk * (back * pre_up * (sig * (1.0 + pre_gate * (1.0 - sig)))))
    up_h, up_l = split(rk * (back * act))
    kt = k.T
    vt = v.T
    grads = [
        nn(kt, gate_h) + nn(kt, gate_l),
        nn(kt, up_h) + nn(kt, up_l),
        nn(vt, mid_h) + nn(vt, mid_l),
    ]
    row = step.get()[...]
    scale = -jnp.where(lax.axis_index("zh") == 0, row[:, 0:1], row[:, 1:2])
    return [scale * x for x in orthogonalize(grads)]


def first_body(q, k, v, r, d, g, u, dt, step, upd_ref, own_ref):
    zh = lax.axis_index("zh")
    key = pick(k.get(), zh)
    value = pick(v.get(), zh)
    rate_row = one_of(r.get()[...], zh)
    fill(own_ref, pick(q.get(), zh), key, value, rate_row, jnp.where(zh == 0, d.get()[:, 0:1], d.get()[:, 1:2]))
    for i, x in enumerate(fast_updates(key, value, rate_row, g, u, dt, step)):
        upd_ref[i] = x


def join_body(own_ref, recv_ref, out_ref, sem):
    copies = [
        pltpu.make_async_copy(ref.at[0:BLK], out_ref.at[i * BLK : (i + 1) * BLK], sem.at[i])
        for i, ref in enumerate((own_ref, recv_ref))
    ]
    for copy in copies:
        copy.start()
    for copy in copies:
        copy.wait()


def second_body(pay, g, u, dt, step, own, upd, even_ref, send_ref, flat_ref):
    pay_ref = pay.get()
    others = fast_updates(
        pay_ref[0:BLK, 0:HD], pay_ref[0:BLK, HD:], tail(pay_ref)[:, :BLK], g, u, dt, step
    )
    zh = lax.axis_index("zh")
    upd_ref = upd.get()
    mine = tail(own.get())[:, BLK:]
    theirs = tail(pay_ref)[:, BLK:]
    keep_even = jnp.where(zh == 0, mine, theirs)
    keep_odd = jnp.where(zh == 0, theirs, mine)
    flat_ref[PAIRS * CHUNK :, :] = jnp.zeros((64, 128), F32)
    for i in range(3):
        other = others[i]
        own_upd = upd_ref[i]
        even = jnp.where(zh == 0, own_upd, other)
        odd = jnp.where(zh == 0, other, own_upd)
        even_ref[i] = even
        for j in range(3):
            cols = slice(j * 128, (j + 1) * 128)
            flat_ref[(3 * i + j) * HD : (3 * i + j + 1) * HD, :] = keep_odd * even[:, cols] + odd[:, cols]
    keep = three(jnp.broadcast_to(keep_even * keep_odd, (16, 128)))[0:4]
    for c in range(PAIRS):
        send_ref[c] = jnp.concatenate([flat_ref[c * CHUNK : (c + 1) * CHUNK, :], keep], axis=0).astype(BF16)


def scan_body(pieces, out_ref):
    in_ref = pieces.get()
    run = jnp.zeros((CROWS, 128), F32)
    for j in range(PAIRS):
        out_ref[j] = run.astype(BF16)
        if j < PAIRS - 1:
            here = in_ref[j].astype(F32)
            keep = here[CHUNK : CHUNK + 1] + here[CHUNK + 1 : CHUNK + 2] + here[CHUNK + 2 : CHUNK + 3]
            run = keep * run + here


def attend_body(own, recv, pair_kv, w1, w2, w3, w4, gain_in, out_ref, score_ref):
    zh = lax.axis_index("zh")
    pair = lax.axis_index("x") * 4 + lax.axis_index("y")
    scale = 1.0 / math.sqrt(HD)
    q_own = queries(own.get())
    q_recv = queries(recv.get())
    gain_ref = gain_in.get()
    wins = [w.get() for w in (pair_kv, w1, w2, w3, w4)]
    gain = jnp.where(zh == 0, gain_ref[:, :HD], gain_ref[:, HD:])
    row = lax.broadcasted_iota(jnp.int32, (BLK, BLK), 0)
    col = lax.broadcasted_iota(jnp.int32, (BLK, BLK), 1)

    def rows_of(parity):
        slot = zh if parity == 0 else 1 - zh
        return pl.ds(pl.multiple_of(slot * BLK, BLK), BLK)

    for parity in range(2):
        q = jnp.where(zh == parity, q_own, q_recv)
        blocks = [(o, e) for o in (4, 3, 2, 1, 0) for e in (0, 1)]
        blocks = blocks[:9] if parity == 0 else blocks[1:]
        top = None
        for n, (o, e) in enumerate(blocks):
            k = wins[o][rows_of(e), 0:HD]
            s = nt(q, k) * scale
            if n == 0:
                s = jnp.where(col > row, s, -1e30)
            if n == 8:
                s = jnp.where(col <= row, s, -1e30)
            if o > 0:
                s = s + jnp.where(pair >= o, 0.0, -1e30)
            score_ref[n] = s
            top = s if top is None else jnp.maximum(top, s)
        top = jnp.max(top, axis=1, keepdims=True)
        total = None
        acc = None
        for n, (o, e) in enumerate(blocks):
            w = jnp.exp(score_ref[n] - top)
            total = w if total is None else total + w
            part = nn(w.astype(BF16), wins[o][rows_of(e), HD:])
            acc = part if acc is None else acc + part
        att = acc / jnp.sum(total, axis=1, keepdims=True)
        norm = lax.rsqrt(jnp.mean(att * att, axis=1, keepdims=True) + 1e-6)
        out_ref[parity] = att * norm * gain


def apply_body(pre, even, own, recv, g, u, dt, gain_in, att, out_ref, flat_ref):
    zh = lax.axis_index("zh")
    pre_ref, even_ref, own_ref, recv_ref, gain_ref, att_ref = [
        x.get() for x in (pre, even, own, recv, gain_in, att)
    ]
    for c in range(PAIRS):
        flat_ref[c * CHUNK : (c + 1) * CHUNK, :] = pre_ref[c].astype(F32)[0:CHUNK]
    keep = jnp.where(zh == 0, tail(own_ref)[:, BLK : BLK + 1], tail(recv_ref)[:, BLK : BLK + 1])
    gain = jnp.where(zh == 0, gain_ref[:, :HD], gain_ref[:, HD:])
    q_own = queries(own_ref)
    q_recv = queries(recv_ref)
    base = [x.get()[...] for x in (g, u, dt)]
    for parity in range(2):
        q = jnp.where(zh == parity, q_own, q_recv)
        qf = q.astype(F32)
        rq = lax.rsqrt(jnp.mean(qf * qf, axis=1, keepdims=True) + 1e-6)
        mats = []
        for i in range(3):
            state = jnp.concatenate(
                [flat_ref[(3 * i + j) * HD : (3 * i + j + 1) * HD, :] for j in range(3)], axis=1
            )
            if parity == 1:
                state = keep * state + even_ref[i]
            mats.append(split(base[i] + state))
        gate = rq * (nn(q, mats[0][0]) + nn(q, mats[0][1]))
        up = rq * (nn(q, mats[1][0]) + nn(q, mats[1][1]))
        applied = nt3(split(gate * jax.nn.sigmoid(gate) * up), mats[2])
        norm = lax.rsqrt(jnp.mean(applied * applied, axis=1, keepdims=True) + 1e-6)
        mixed = (applied * norm * gain + att_ref[parity]).astype(BF16)
        for c in range(2):
            for z in range(4):
                out_ref[c * 2 + parity, (z % 2) * 32 : (z % 2) * 32 + 32, (z // 2) * HD : (z // 2 + 1) * HD] = mixed[
                    z * 64 + c * 32 : z * 64 + c * 32 + 32
                ]


def project_body(mix_ref, own_ref, other_ref, out_ref):
    core = lax.axis_index("c")
    total = None
    for w_ref, which in ((own_ref, core), (other_ref, 1 - core)):
        for zh in range(2):
            part = mix_ref[which * 2 + zh]
            part = jnp.concatenate([part[:, :HD], part[:, HD:]], axis=0)
            part = nn(part, w_ref[zh * HD : (zh + 1) * HD, :])
            total = part if total is None else total + part
    out_ref[...] = total.astype(BF16)


def total_body(parts, out_ref):
    ref = parts.get()
    out_ref[...] = sum(ref[i].astype(F32) for i in range(4)).astype(BF16)


def local(q, k, v, rates, decay, step, gate, up, down, ttt_gain, attn_gain, proj):
    sds = jax.ShapeDtypeStruct
    pay = sds((PAY, FD), BF16)
    rates = rates.T
    down = jnp.swapaxes(down, 1, 2)
    step = step.reshape(1, 2)
    (send,) = call(pack_body, [pay], (q, k, v, rates, decay), 0, 1_000_000)
    recv = lax.ppermute(send, "zh", [(0, 1), (1, 0)])
    proj_other = lax.ppermute(proj, "c", [(0, 1), (1, 0)])
    mats = sds((3, HD, FD), F32)
    flat = pltpu.VMEM((PAIRS * CHUNK + 64, 128), F32)
    upd, own = call(
        first_body,
        [mats, pay],
        (q, k, v, rates, decay, gate, up, down, step),
        6_000_000_000,
        3_000_000,
        mine=(5, 6, 7),
    )
    pair_kv = pl.pallas_call(
        join_body,
        out_shape=sds((2 * BLK, FD), BF16),
        in_specs=[pl.BlockSpec(memory_space=pltpu.MemorySpace.HBM)] * 2,
        out_specs=pl.BlockSpec(memory_space=pltpu.MemorySpace.HBM),
        scratch_shapes=[pltpu.SemaphoreType.DMA((2,))],
        compiler_params=pltpu.CompilerParams(vmem_limit_bytes=VMEM_CAP),
        cost_estimate=pl.CostEstimate(flops=0, bytes_accessed=800_000, transcendentals=0),
    )(own, recv)
    wins = [
        lax.ppermute(pair_kv, ("x", "y"), [(i, i + o) for i in range(PAIRS - o)]) for o in (1, 2, 3, 4)
    ]
    even, outgoing = call(
        second_body,
        [mats, sds((PAIRS, CROWS, 128), BF16)],
        (recv, gate, up, down, step, own, upd),
        6_000_000_000,
        4_000_000,
        scratch=[flat],
        mine=(1, 2, 3),
    )
    outgoing, *wins = lax.optimization_barrier((outgoing, *wins))
    pieces = lax.all_to_all(outgoing, ("x", "y"), 0, 0, tiled=True)
    (sums,) = call(scan_body, [sds((PAIRS, CROWS, 128), BF16)], (pieces,), 500_000, 1_000_000)
    prefix = lax.all_to_all(sums, ("x", "y"), 0, 0, tiled=True)
    (att,) = call(
        attend_body,
        [sds((2, BLK, HD), F32)],
        (own, recv, pair_kv, *wins, attn_gain.reshape(1, FD)),
        1_000_000_000,
        3_000_000,
        1_200_000,
        scratch=[pltpu.VMEM((9, BLK, BLK), F32)],
    )
    (mixed,) = call(
        apply_body,
        [sds((4, 64, FD), BF16)],
        (prefix, even, own, recv, gate, up, down, ttt_gain.reshape(1, FD), att),
        600_000_000,
        5_000_000,
        scratch=[flat],
        mine=(4, 5, 6),
    )
    mixed = lax.all_to_all(mixed, ("c", "zh"), 0, 0, tiled=True)
    tile = 512
    partial = pl.pallas_call(
        project_body,
        out_shape=sds((128, WIDTH), BF16),
        grid=(WIDTH // tile,),
        in_specs=[
            pl.BlockSpec((4, 64, FD), lambda i: (0, 0, 0)),
            pl.BlockSpec((FD, tile), lambda i: (0, i)),
            pl.BlockSpec((FD, tile), lambda i: (0, i)),
        ],
        out_specs=pl.BlockSpec((128, tile), lambda i: (0, i)),
        compiler_params=pltpu.CompilerParams(vmem_limit_bytes=VMEM_CAP),
        cost_estimate=pl.CostEstimate(flops=600_000_000, bytes_accessed=6_000_000, transcendentals=0),
    )(mixed, proj, proj_other)
    parts = lax.all_to_all(partial.reshape(4, 32, WIDTH), "zl", 0, 0, tiled=True)
    (result,) = call(total_body, [sds((32, WIDTH), BF16)], (parts,), 400_000, 1_000_000)
    return result


def solution(mesh):
    fine = Mesh(mesh.devices.reshape(4, 4, 2, 4, 2), ("x", "y", "zh", "zl", "c"))
    seq = ("x", "y", "zh")
    head = ("zl", "c")
    in_specs = (
        P(seq, head),
        P(seq, head),
        P(seq, head),
        P(seq, head),
        P(seq, head),
        P(head),
        P(head, None, None),
        P(head, None, None),
        P(head, None, None),
        P(head),
        P(head),
        P(head, None),
    )
    out_specs = P(("x", "y", "zh", "zl", "c"), None)
    return jax.shard_map(local, mesh=fine, in_specs=in_specs, out_specs=out_specs, check_vma=False)
```

```python
import functools
import math

import jax
import jax.numpy as jnp
from jax import lax
from jax.experimental import pallas as pl
from jax.experimental.pallas import tpu as pltpu
from jax.sharding import Mesh, PartitionSpec as P

F32 = jnp.float32
BF16 = jnp.bfloat16
HD = 192
FD = 384
BLK = 256
WIDTH = 3072
NS_STEPS = 5
PAIRS = 16
CHUNK = 108
CROWS = 112
PAY = 400
COEF = (3.4445, -4.775, 2.0315)
VMEM_CAP = 60 * 1024 * 1024
SMALL = 12 * 1024 * 1024


class Lazy:
    def __init__(self, copy, ref):
        self.copy, self.ref = copy, ref

    def get(self):
        if self.copy is not None:
            self.copy.wait()
            self.copy = None
        return self.ref


def call(body, outs, ins, flops, nbytes, trans=0, scratch=(), mine=(), cap=VMEM_CAP):
    outs = list(outs)
    n_in, n_out = len(ins), len(outs)
    shapes = [a.shape[1:] if i in mine else a.shape for i, a in enumerate(ins)]

    def kernel(*refs):
        in_refs, out_refs = refs[:n_in], refs[n_in : n_in + n_out]
        rest = refs[n_in + n_out :]
        in_vm, out_vm = rest[:n_in], rest[n_in : n_in + n_out]
        in_sem, out_sem, extra = rest[n_in + n_out], rest[n_in + n_out + 1], rest[n_in + n_out + 2 :]
        zh = lax.axis_index("zh")
        lazy = []
        for i in range(n_in):
            src = in_refs[i].at[zh] if i in mine else in_refs[i]
            copy = pltpu.make_async_copy(src, in_vm[i], in_sem.at[i])
            copy.start()
            lazy.append(Lazy(copy, in_vm[i]))
        copies = [pltpu.make_async_copy(out_vm[i], out_refs[i], out_sem.at[i]) for i in range(n_out)]
        body(*lazy, *out_vm, *extra)
        for copy in copies:
            copy.start()
        for item in lazy:
            item.get()
        for copy in copies:
            copy.wait()

    any_spec = pl.BlockSpec(memory_space=pltpu.MemorySpace.HBM)
    return pl.pallas_call(
        kernel,
        out_shape=outs,
        in_specs=[any_spec] * n_in,
        out_specs=[any_spec] * n_out,
        scratch_shapes=[pltpu.VMEM(sh, a.dtype) for sh, a in zip(shapes, ins)]
        + [pltpu.VMEM(o.shape, o.dtype) for o in outs]
        + [pltpu.SemaphoreType.DMA((n_in,)), pltpu.SemaphoreType.DMA((n_out,))]
        + list(scratch),
        compiler_params=pltpu.CompilerParams(vmem_limit_bytes=cap),
        cost_estimate=pl.CostEstimate(flops=flops, bytes_accessed=nbytes, transcendentals=trans),
    )(*ins)


def nn(a, b):
    return lax.dot_general(a, b, (((1,), (0,)), ((), ())), preferred_element_type=F32)


def nt(a, b):
    return lax.dot_general(a, b, (((1,), (1,)), ((), ())), preferred_element_type=F32)


def split(x):
    hi = x.astype(BF16)
    return hi, (x - hi.astype(F32)).astype(BF16)


def nn3(a, b):
    return nn(a[0], b[0]) + (nn(a[0], b[1]) + nn(a[1], b[0]))


def nt3(a, b):
    return nt(a[0], b[0]) + (nt(a[0], b[1]) + nt(a[1], b[0]))


def three(x):
    hi = x.astype(BF16).astype(F32)
    mid = (x - hi).astype(BF16).astype(F32)
    low = x - hi - mid
    row = lax.broadcasted_iota(jnp.int32, x.shape, 0)
    return jnp.where(row == 0, hi, jnp.where(row == 1, mid, jnp.where(row == 2, low, 0.0)))


def pick(ref, who):
    return jnp.where(who == 0, ref[:, :HD], ref[:, HD:])


def one_of(row, who):
    return jnp.where(who == 0, row[0:1], row[1:2])


def fill(out_ref, q, k, v, rate_row, decay):
    out_ref[0:BLK, 0:HD] = k
    out_ref[0:BLK, HD:] = v
    out_ref[BLK : BLK + 128, 0:HD] = q[0:128]
    out_ref[BLK : BLK + 128, HD:] = q[128:256]
    row = jnp.concatenate([rate_row, jnp.broadcast_to(decay, (1, 128))], axis=1)
    out_ref[384:400, :] = three(jnp.broadcast_to(row, (16, FD))).astype(BF16)


def pack_body(q, k, v, r, d, send_ref):
    who = 1 - lax.axis_index("zh")
    fill(
        send_ref,
        pick(q.get(), who),
        pick(k.get(), who),
        pick(v.get(), who),
        one_of(r.get()[...], who),
        jnp.where(who == 0, d.get()[:, 0:1], d.get()[:, 1:2]),
    )


def tail(pay_ref):
    rows = pay_ref[384:400, :].astype(F32)
    return rows[0:1] + rows[1:2] + rows[2:3]


def queries(pay_ref):
    both = pay_ref[BLK : BLK + 128, :]
    return jnp.concatenate([both[:, :HD], both[:, HD:]], axis=0)


def orthogonalize(mats):
    norms = [jnp.sqrt(jnp.sum(m * m, keepdims=True)) + 1e-7 for m in mats]
    mats = [m / n for m, n in zip(mats, norms)]
    for _ in range(NS_STEPS):
        parts = [split(x) for x in mats]
        grams = []
        for hi, lo in parts:
            cross = nt(hi, lo)
            grams.append(nt(hi, hi) + (cross + cross.T))
        polys = []
        for gram in grams:
            hi, lo = split(gram)
            cross = nn(hi, lo)
            polys.append(split(COEF[1] * gram + COEF[2] * (nn(hi, hi) + (cross + cross.T))))
        mats = [COEF[0] * x + nn3(p, s) for x, p, s in zip(mats, polys, parts)]
    return mats


def fast_updates(k, v, rate_row, g, u, dt, step):
    kf = k.astype(F32)
    rk = lax.rsqrt(jnp.mean(kf * kf, axis=1, keepdims=True) + 1e-6)
    rate = jnp.broadcast_to(rate_row, (128, BLK)).T[:, 0:1]
    gh, gl = split(g.get()[...])
    pre_gate = rk * (nn(k, gh) + nn(k, gl))
    uh, ul = split(u.get()[...])
    pre_up = rk * (nn(k, uh) + nn(k, ul))
    dh, dl = split(dt.get()[...])
    back = -rate * (nn(v, dh) + nn(v, dl))
    sig = jax.nn.sigmoid(pre_gate)
    act = pre_gate * sig
    mid_h, mid_l = split(-rate * (act * pre_up))
    gate_h, gate_l = split(rk * (back * pre_up * (sig * (1.0 + pre_gate * (1.0 - sig)))))
    up_h, up_l = split(rk * (back * act))
    kt = k.T
    vt = v.T
    grads = [
        nn(kt, gate_h) + nn(kt, gate_l),
        nn(kt, up_h) + nn(kt, up_l),
        nn(vt, mid_h) + nn(vt, mid_l),
    ]
    row = step.get()[...]
    scale = -jnp.where(lax.axis_index("zh") == 0, row[:, 0:1], row[:, 1:2])
    return [scale * x for x in orthogonalize(grads)]


def first_body(q, k, v, r, d, g, u, dt, step, upd_ref, own_ref):
    zh = lax.axis_index("zh")
    key = pick(k.get(), zh)
    value = pick(v.get(), zh)
    rate_row = one_of(r.get()[...], zh)
    fill(own_ref, pick(q.get(), zh), key, value, rate_row, jnp.where(zh == 0, d.get()[:, 0:1], d.get()[:, 1:2]))
    for i, x in enumerate(fast_updates(key, value, rate_row, g, u, dt, step)):
        upd_ref[i] = x


def join_body(own, recv, out_ref):
    out_ref[0:BLK] = own.get()[0:BLK]
    out_ref[BLK:] = recv.get()[0:BLK]


def second_body(pay, g, u, dt, step, own, upd, even_ref, send_ref, flat_ref):
    pay_ref = pay.get()
    others = fast_updates(
        pay_ref[0:BLK, 0:HD], pay_ref[0:BLK, HD:], tail(pay_ref)[:, :BLK], g, u, dt, step
    )
    zh = lax.axis_index("zh")
    upd_ref = upd.get()
    mine = tail(own.get())[:, BLK:]
    theirs = tail(pay_ref)[:, BLK:]
    keep_even = jnp.where(zh == 0, mine, theirs)
    keep_odd = jnp.where(zh == 0, theirs, mine)
    flat_ref[PAIRS * CHUNK :, :] = jnp.zeros((64, 128), F32)
    for i in range(3):
        other = others[i]
        own_upd = upd_ref[i]
        even = jnp.where(zh == 0, own_upd, other)
        odd = jnp.where(zh == 0, other, own_upd)
        even_ref[i] = even
        for j in range(3):
            cols = slice(j * 128, (j + 1) * 128)
            flat_ref[(3 * i + j) * HD : (3 * i + j + 1) * HD, :] = keep_odd * even[:, cols] + odd[:, cols]
    keep = three(jnp.broadcast_to(keep_even * keep_odd, (16, 128)))[0:4]
    for c in range(PAIRS):
        send_ref[c] = jnp.concatenate([flat_ref[c * CHUNK : (c + 1) * CHUNK, :], keep], axis=0).astype(BF16)


def scan_body(pieces, out_ref):
    in_ref = pieces.get()
    run = jnp.zeros((CROWS, 128), F32)
    for j in range(PAIRS):
        out_ref[j] = run.astype(BF16)
        if j < PAIRS - 1:
            here = in_ref[j].astype(F32)
            keep = here[CHUNK : CHUNK + 1] + here[CHUNK + 1 : CHUNK + 2] + here[CHUNK + 2 : CHUNK + 3]
            run = keep * run + here


def attend_body(own, recv, pair_kv, w1, w2, w3, w4, gain_in, out_ref, score_ref):
    zh = lax.axis_index("zh")
    pair = lax.axis_index("x") * 4 + lax.axis_index("y")
    scale = 1.0 / math.sqrt(HD)
    q_own = queries(own.get())
    q_recv = queries(recv.get())
    gain_ref = gain_in.get()
    wins = [w.get() for w in (pair_kv, w1, w2, w3, w4)]
    gain = jnp.where(zh == 0, gain_ref[:, :HD], gain_ref[:, HD:])
    row = lax.broadcasted_iota(jnp.int32, (BLK, BLK), 0)
    col = lax.broadcasted_iota(jnp.int32, (BLK, BLK), 1)

    def rows_of(parity):
        slot = zh if parity == 0 else 1 - zh
        return pl.ds(pl.multiple_of(slot * BLK, BLK), BLK)

    for parity in range(2):
        q = jnp.where(zh == parity, q_own, q_recv)
        blocks = [(o, e) for o in (4, 3, 2, 1, 0) for e in (0, 1)]
        blocks = blocks[:9] if parity == 0 else blocks[1:]
        top = None
        for n, (o, e) in enumerate(blocks):
            k = wins[o][rows_of(e), 0:HD]
            s = nt(q, k) * scale
            if n == 0:
                s = jnp.where(col > row, s, -1e30)
            if n == 8:
                s = jnp.where(col <= row, s, -1e30)
            if o > 0:
                s = s + jnp.where(pair >= o, 0.0, -1e30)
            score_ref[n] = s
            top = s if top is None else jnp.maximum(top, s)
        top = jnp.max(top, axis=1, keepdims=True)
        total = None
        acc = None
        for n, (o, e) in enumerate(blocks):
            w = jnp.exp(score_ref[n] - top)
            total = w if total is None else total + w
            part = nn(w.astype(BF16), wins[o][rows_of(e), HD:])
            acc = part if acc is None else acc + part
        att = acc / jnp.sum(total, axis=1, keepdims=True)
        norm = lax.rsqrt(jnp.mean(att * att, axis=1, keepdims=True) + 1e-6)
        out_ref[parity] = att * norm * gain


def apply_body(pre, even, own, recv, g, u, dt, gain_in, att, out_ref, flat_ref):
    zh = lax.axis_index("zh")
    pre_ref, even_ref, own_ref, recv_ref, gain_ref, att_ref = [
        x.get() for x in (pre, even, own, recv, gain_in, att)
    ]
    for c in range(PAIRS):
        flat_ref[c * CHUNK : (c + 1) * CHUNK, :] = pre_ref[c].astype(F32)[0:CHUNK]
    keep = jnp.where(zh == 0, tail(own_ref)[:, BLK : BLK + 1], tail(recv_ref)[:, BLK : BLK + 1])
    gain = jnp.where(zh == 0, gain_ref[:, :HD], gain_ref[:, HD:])
    q_own = queries(own_ref)
    q_recv = queries(recv_ref)
    base = [x.get()[...] for x in (g, u, dt)]
    for parity in range(2):
        q = jnp.where(zh == parity, q_own, q_recv)
        qf = q.astype(F32)
        rq = lax.rsqrt(jnp.mean(qf * qf, axis=1, keepdims=True) + 1e-6)
        mats = []
        for i in range(3):
            state = jnp.concatenate(
                [flat_ref[(3 * i + j) * HD : (3 * i + j + 1) * HD, :] for j in range(3)], axis=1
            )
            if parity == 1:
                state = keep * state + even_ref[i]
            mats.append(split(base[i] + state))
        gate = rq * (nn(q, mats[0][0]) + nn(q, mats[0][1]))
        up = rq * (nn(q, mats[1][0]) + nn(q, mats[1][1]))
        applied = nt3(split(gate * jax.nn.sigmoid(gate) * up), mats[2])
        norm = lax.rsqrt(jnp.mean(applied * applied, axis=1, keepdims=True) + 1e-6)
        mixed = (applied * norm * gain + att_ref[parity]).astype(BF16)
        for c in range(2):
            for z in range(4):
                out_ref[c * 2 + parity, (z % 2) * 32 : (z % 2) * 32 + 32, (z // 2) * HD : (z // 2 + 1) * HD] = mixed[
                    z * 64 + c * 32 : z * 64 + c * 32 + 32
                ]


def project_body(mix_ref, own_ref, other_ref, out_ref):
    core = lax.axis_index("c")
    total = None
    for w_ref, which in ((own_ref, core), (other_ref, 1 - core)):
        for zh in range(2):
            part = mix_ref[which * 2 + zh]
            part = jnp.concatenate([part[:, :HD], part[:, HD:]], axis=0)
            part = nn(part, w_ref[zh * HD : (zh + 1) * HD, :])
            total = part if total is None else total + part
    out_ref[...] = total.astype(BF16)


def total_body(parts, out_ref):
    ref = parts.get()
    out_ref[...] = sum(ref[i].astype(F32) for i in range(4)).astype(BF16)


def local(q, k, v, rates, decay, step, gate, up, down, ttt_gain, attn_gain, proj):
    sds = jax.ShapeDtypeStruct
    pay = sds((PAY, FD), BF16)
    rates = rates.T
    down = jnp.swapaxes(down, 1, 2)
    step = step.reshape(1, 2)
    (send,) = call(pack_body, [pay], (q, k, v, rates, decay), 0, 1_000_000)
    recv = lax.ppermute(send, "zh", [(0, 1), (1, 0)])
    proj_other = lax.ppermute(proj, "c", [(0, 1), (1, 0)])
    mats = sds((3, HD, FD), F32)
    flat = pltpu.VMEM((PAIRS * CHUNK + 64, 128), F32)
    upd, own = call(
        first_body,
        [mats, pay],
        (q, k, v, rates, decay, gate, up, down, step),
        6_000_000_000,
        3_000_000,
        mine=(5, 6, 7),
    )
    (pair_kv,) = call(join_body, [sds((2 * BLK, FD), BF16)], (own, recv), 0, 800_000)
    wins = [
        lax.ppermute(pair_kv, ("x", "y"), [(i, i + o) for i in range(PAIRS - o)]) for o in (1, 2, 3, 4)
    ]
    even, outgoing = call(
        second_body,
        [mats, sds((PAIRS, CROWS, 128), BF16)],
        (recv, gate, up, down, step, own, upd),
        6_000_000_000,
        4_000_000,
        scratch=[flat],
        mine=(1, 2, 3),
    )
    outgoing, wins[1], wins[3] = lax.optimization_barrier((outgoing, wins[1], wins[3]))
    pieces = lax.all_to_all(outgoing, ("x", "y"), 0, 0, tiled=True)
    (sums,) = call(scan_body, [sds((PAIRS, CROWS, 128), BF16)], (pieces,), 500_000, 1_000_000, cap=SMALL)
    prefix = lax.all_to_all(sums, ("x", "y"), 0, 0, tiled=True)
    (att,) = call(
        attend_body,
        [sds((2, BLK, HD), F32)],
        (own, recv, pair_kv, *wins, attn_gain.reshape(1, FD)),
        1_000_000_000,
        3_000_000,
        1_200_000,
        scratch=[pltpu.VMEM((9, BLK, BLK), F32)],
    )
    (mixed,) = call(
        apply_body,
        [sds((4, 64, FD), BF16)],
        (prefix, even, own, recv, gate, up, down, ttt_gain.reshape(1, FD), att),
        600_000_000,
        5_000_000,
        scratch=[flat],
        mine=(4, 5, 6),
    )
    mixed = lax.all_to_all(mixed, ("c", "zh"), 0, 0, tiled=True)
    tile = 512
    partial = pl.pallas_call(
        project_body,
        out_shape=sds((128, WIDTH), BF16),
        grid=(WIDTH // tile,),
        in_specs=[
            pl.BlockSpec((4, 64, FD), lambda i: (0, 0, 0)),
            pl.BlockSpec((FD, tile), lambda i: (0, i)),
            pl.BlockSpec((FD, tile), lambda i: (0, i)),
        ],
        out_specs=pl.BlockSpec((128, tile), lambda i: (0, i)),
        compiler_params=pltpu.CompilerParams(vmem_limit_bytes=SMALL),
        cost_estimate=pl.CostEstimate(flops=600_000_000, bytes_accessed=6_000_000, transcendentals=0),
    )(mixed, proj, proj_other)
    parts = lax.all_to_all(partial.reshape(4, 32, WIDTH), "zl", 0, 0, tiled=True)
    (result,) = call(total_body, [sds((32, WIDTH), BF16)], (parts,), 400_000, 1_000_000, cap=SMALL)
    return result


def solution(mesh):
    fine = Mesh(mesh.devices.reshape(4, 4, 2, 4, 2), ("x", "y", "zh", "zl", "c"))
    seq = ("x", "y", "zh")
    head = ("zl", "c")
    in_specs = (
        P(seq, head),
        P(seq, head),
        P(seq, head),
        P(seq, head),
        P(seq, head),
        P(head),
        P(head, None, None),
        P(head, None, None),
        P(head, None, None),
        P(head),
        P(head),
        P(head, None),
    )
    out_specs = P(("x", "y", "zh", "zl", "c"), None)
    return jax.shard_map(local, mesh=fine, in_specs=in_specs, out_specs=out_specs, check_vma=False)
```

```python
import functools
import math

import jax
import jax.numpy as jnp
from jax import lax
from jax.experimental import pallas as pl
from jax.experimental.pallas import tpu as pltpu
from jax.sharding import Mesh, PartitionSpec as P

F32 = jnp.float32
BF16 = jnp.bfloat16
HD = 192
FD = 384
BLK = 256
WIDTH = 3072
NS_STEPS = 5
PAIRS = 16
CHUNK = 108
CROWS = 112
PAY = 400
COEF = (3.4445, -4.775, 2.0315)
VMEM_CAP = 60 * 1024 * 1024
SMALL = 12 * 1024 * 1024


class Lazy:
    def __init__(self, copy, ref):
        self.copy, self.ref = copy, ref

    def get(self):
        if self.copy is not None:
            self.copy.wait()
            self.copy = None
        return self.ref


def call(body, outs, ins, flops, nbytes, trans=0, scratch=(), mine=(), cap=VMEM_CAP):
    outs = list(outs)
    n_in, n_out = len(ins), len(outs)
    shapes = [a.shape[1:] if i in mine else a.shape for i, a in enumerate(ins)]

    def kernel(*refs):
        in_refs, out_refs = refs[:n_in], refs[n_in : n_in + n_out]
        rest = refs[n_in + n_out :]
        in_vm, out_vm = rest[:n_in], rest[n_in : n_in + n_out]
        in_sem, out_sem, extra = rest[n_in + n_out], rest[n_in + n_out + 1], rest[n_in + n_out + 2 :]
        zh = lax.axis_index("zh")
        lazy = []
        for i in range(n_in):
            src = in_refs[i].at[zh] if i in mine else in_refs[i]
            copy = pltpu.make_async_copy(src, in_vm[i], in_sem.at[i])
            copy.start()
            lazy.append(Lazy(copy, in_vm[i]))
        copies = [pltpu.make_async_copy(out_vm[i], out_refs[i], out_sem.at[i]) for i in range(n_out)]
        body(*lazy, *out_vm, *extra)
        for copy in copies:
            copy.start()
        for item in lazy:
            item.get()
        for copy in copies:
            copy.wait()

    any_spec = pl.BlockSpec(memory_space=pltpu.MemorySpace.HBM)
    return pl.pallas_call(
        kernel,
        out_shape=outs,
        in_specs=[any_spec] * n_in,
        out_specs=[any_spec] * n_out,
        scratch_shapes=[pltpu.VMEM(sh, a.dtype) for sh, a in zip(shapes, ins)]
        + [pltpu.VMEM(o.shape, o.dtype) for o in outs]
        + [pltpu.SemaphoreType.DMA((n_in,)), pltpu.SemaphoreType.DMA((n_out,))]
        + list(scratch),
        compiler_params=pltpu.CompilerParams(vmem_limit_bytes=cap),
        cost_estimate=pl.CostEstimate(flops=flops, bytes_accessed=nbytes, transcendentals=trans),
    )(*ins)


def nn(a, b):
    return lax.dot_general(a, b, (((1,), (0,)), ((), ())), preferred_element_type=F32)


def nt(a, b):
    return lax.dot_general(a, b, (((1,), (1,)), ((), ())), preferred_element_type=F32)


def split(x):
    hi = x.astype(BF16)
    return hi, (x - hi.astype(F32)).astype(BF16)


def nn3(a, b):
    return nn(a[0], b[0]) + (nn(a[0], b[1]) + nn(a[1], b[0]))


def nt3(a, b):
    return nt(a[0], b[0]) + (nt(a[0], b[1]) + nt(a[1], b[0]))


def three(x):
    hi = x.astype(BF16).astype(F32)
    mid = (x - hi).astype(BF16).astype(F32)
    low = x - hi - mid
    row = lax.broadcasted_iota(jnp.int32, x.shape, 0)
    return jnp.where(row == 0, hi, jnp.where(row == 1, mid, jnp.where(row == 2, low, 0.0)))


def pick(ref, who):
    return jnp.where(who == 0, ref[:, :HD], ref[:, HD:])


def one_of(row, who):
    return jnp.where(who == 0, row[0:1], row[1:2])


def fill(out_ref, q, k, v, rate_row, decay):
    out_ref[0:BLK, 0:HD] = k
    out_ref[0:BLK, HD:] = v
    out_ref[BLK : BLK + 128, 0:HD] = q[0:128]
    out_ref[BLK : BLK + 128, HD:] = q[128:256]
    row = jnp.concatenate([rate_row, jnp.broadcast_to(decay, (1, 128))], axis=1)
    out_ref[384:400, :] = three(jnp.broadcast_to(row, (16, FD))).astype(BF16)


def pack_body(q, k, v, r, d, send_ref):
    who = 1 - lax.axis_index("zh")
    fill(
        send_ref,
        pick(q.get(), who),
        pick(k.get(), who),
        pick(v.get(), who),
        one_of(r.get()[...], who),
        jnp.where(who == 0, d.get()[:, 0:1], d.get()[:, 1:2]),
    )


def tail(pay_ref):
    rows = pay_ref[384:400, :].astype(F32)
    return rows[0:1] + rows[1:2] + rows[2:3]


def queries(pay_ref):
    both = pay_ref[BLK : BLK + 128, :]
    return jnp.concatenate([both[:, :HD], both[:, HD:]], axis=0)


def orthogonalize(mats):
    norms = [jnp.sqrt(jnp.sum(m * m, keepdims=True)) + 1e-7 for m in mats]
    mats = [m / n for m, n in zip(mats, norms)]
    for _ in range(NS_STEPS):
        parts = [split(x) for x in mats]
        grams = []
        for hi, lo in parts:
            cross = nt(hi, lo)
            grams.append(nt(hi, hi) + (cross + cross.T))
        polys = []
        for gram in grams:
            hi, lo = split(gram)
            cross = nn(hi, lo)
            polys.append(split(COEF[1] * gram + COEF[2] * (nn(hi, hi) + (cross + cross.T))))
        mats = [COEF[0] * x + nn3(p, s) for x, p, s in zip(mats, polys, parts)]
    return mats


def fast_updates(k, v, rate_row, g, u, dt, step):
    kf = k.astype(F32)
    rk = lax.rsqrt(jnp.mean(kf * kf, axis=1, keepdims=True) + 1e-6)
    rate = jnp.broadcast_to(rate_row, (128, BLK)).T[:, 0:1]
    gh, gl = split(g.get()[...])
    pre_gate = rk * (nn(k, gh) + nn(k, gl))
    uh, ul = split(u.get()[...])
    pre_up = rk * (nn(k, uh) + nn(k, ul))
    dh, dl = split(dt.get()[...])
    back = -rate * (nn(v, dh) + nn(v, dl))
    sig = jax.nn.sigmoid(pre_gate)
    act = pre_gate * sig
    mid_h, mid_l = split(-rate * (act * pre_up))
    gate_h, gate_l = split(rk * (back * pre_up * (sig * (1.0 + pre_gate * (1.0 - sig)))))
    up_h, up_l = split(rk * (back * act))
    kt = k.T
    vt = v.T
    grads = [
        nn(kt, gate_h) + nn(kt, gate_l),
        nn(kt, up_h) + nn(kt, up_l),
        nn(vt, mid_h) + nn(vt, mid_l),
    ]
    row = step.get()[...]
    scale = -jnp.where(lax.axis_index("zh") == 0, row[:, 0:1], row[:, 1:2])
    return [scale * x for x in orthogonalize(grads)]


def first_body(q, k, v, r, d, g, u, dt, step, upd_ref, own_ref):
    zh = lax.axis_index("zh")
    key = pick(k.get(), zh)
    value = pick(v.get(), zh)
    rate_row = one_of(r.get()[...], zh)
    fill(own_ref, pick(q.get(), zh), key, value, rate_row, jnp.where(zh == 0, d.get()[:, 0:1], d.get()[:, 1:2]))
    for i, x in enumerate(fast_updates(key, value, rate_row, g, u, dt, step)):
        upd_ref[i] = x


def join_body(own, recv, out_ref):
    out_ref[0:BLK] = own.get()[0:BLK]
    out_ref[BLK:] = recv.get()[0:BLK]


def second_body(pay, g, u, dt, step, own, upd, even_ref, send_ref, flat_ref):
    pay_ref = pay.get()
    others = fast_updates(
        pay_ref[0:BLK, 0:HD], pay_ref[0:BLK, HD:], tail(pay_ref)[:, :BLK], g, u, dt, step
    )
    zh = lax.axis_index("zh")
    upd_ref = upd.get()
    mine = tail(own.get())[:, BLK:]
    theirs = tail(pay_ref)[:, BLK:]
    keep_even = jnp.where(zh == 0, mine, theirs)
    keep_odd = jnp.where(zh == 0, theirs, mine)
    flat_ref[PAIRS * CHUNK :, :] = jnp.zeros((64, 128), F32)
    for i in range(3):
        other = others[i]
        own_upd = upd_ref[i]
        even = jnp.where(zh == 0, own_upd, other)
        odd = jnp.where(zh == 0, other, own_upd)
        even_ref[i] = even
        for j in range(3):
            cols = slice(j * 128, (j + 1) * 128)
            flat_ref[(3 * i + j) * HD : (3 * i + j + 1) * HD, :] = keep_odd * even[:, cols] + odd[:, cols]
    keep = three(jnp.broadcast_to(keep_even * keep_odd, (16, 128)))[0:4]
    for c in range(PAIRS):
        send_ref[c] = jnp.concatenate([flat_ref[c * CHUNK : (c + 1) * CHUNK, :], keep], axis=0).astype(BF16)


def scan_body(pieces, out_ref):
    in_ref = pieces.get()
    run = jnp.zeros((CROWS, 128), F32)
    for j in range(PAIRS):
        out_ref[j] = run.astype(BF16)
        if j < PAIRS - 1:
            here = in_ref[j].astype(F32)
            keep = here[CHUNK : CHUNK + 1] + here[CHUNK + 1 : CHUNK + 2] + here[CHUNK + 2 : CHUNK + 3]
            run = keep * run + here


def scores_of(q, keys, blocks, score_ref, rows_of, pair):
    row = lax.broadcasted_iota(jnp.int32, (BLK, BLK), 0)
    col = lax.broadcasted_iota(jnp.int32, (BLK, BLK), 1)
    top = None
    for n, (o, e, kind) in enumerate(blocks):
        s = nt(q, keys[o][rows_of(e), 0:HD]) * (1.0 / math.sqrt(HD))
        if kind == "oldest":
            s = jnp.where(col > row, s, -1e30)
        if kind == "newest":
            s = jnp.where(col <= row, s, -1e30)
        if o > 0:
            s = s + jnp.where(pair >= o, 0.0, -1e30)
        score_ref[n] = s
        top = s if top is None else jnp.maximum(top, s)
    return jnp.max(top, axis=1, keepdims=True)


def weighted(values, blocks, score_ref, rows_of, top):
    total = None
    acc = None
    for n, (o, e, _) in enumerate(blocks):
        w = jnp.exp(score_ref[n] - top)
        total = w if total is None else total + w
        part = nn(w.astype(BF16), values[o][rows_of(e), HD:])
        acc = part if acc is None else acc + part
    return jnp.sum(total, axis=1, keepdims=True), acc


def window_blocks(parity, offsets):
    blocks = [(o, e) for o in (4, 3, 2, 1, 0) for e in (0, 1)][parity : parity + 9]
    kinds = ["oldest"] + ["inner"] * 7 + ["newest"]
    return [(o, e, kind) for (o, e), kind in zip(blocks, kinds) if o in offsets]


def ordered_rows(zh):
    def rows_of(parity):
        slot = zh if parity == 0 else 1 - zh
        return pl.ds(pl.multiple_of(slot * BLK, BLK), BLK)

    return rows_of


def pair_index():
    return lax.axis_index("x") * 4 + lax.axis_index("y")


def attend_first_body(own, recv, pair_kv, w2, w4, acc_ref, stat_ref, score_ref):
    zh = lax.axis_index("zh")
    q_own = queries(own.get())
    q_recv = queries(recv.get())
    wins = {0: pair_kv.get(), 2: w2.get(), 4: w4.get()}
    rows_of = ordered_rows(zh)
    lane = lax.broadcasted_iota(jnp.int32, (BLK, 128), 1)
    for parity in range(2):
        q = jnp.where(zh == parity, q_own, q_recv)
        blocks = window_blocks(parity, wins)
        scores = score_ref.at[parity]
        top = scores_of(q, wins, blocks, scores, rows_of, pair_index())
        total, acc = weighted(wins, blocks, scores, rows_of, top)
        acc_ref[parity] = acc
        stat_ref[parity] = jnp.where(lane < 64, top, total)


def attend_second_body(own, recv, w1, w3, acc_in, stat, gain_in, out_ref, score_ref):
    zh = lax.axis_index("zh")
    q_own = queries(own.get())
    q_recv = queries(recv.get())
    gain_ref = gain_in.get()
    wins = {1: w1.get(), 3: w3.get()}
    gain = jnp.where(zh == 0, gain_ref[:, :HD], gain_ref[:, HD:])
    rows_of = ordered_rows(zh)
    stats = stat.get()
    before = acc_in.get()
    for parity in range(2):
        q = jnp.where(zh == parity, q_own, q_recv)
        blocks = window_blocks(parity, wins)
        scores = score_ref.at[parity]
        old_top = stats[parity, :, 0:1]
        top = jnp.maximum(old_top, scores_of(q, wins, blocks, scores, rows_of, pair_index()))
        total, acc = weighted(wins, blocks, scores, rows_of, top)
        rescale = jnp.exp(old_top - top)
        total = total + rescale * stats[parity, :, 64:65]
        att = (acc + rescale * before[parity]) / total
        norm = lax.rsqrt(jnp.mean(att * att, axis=1, keepdims=True) + 1e-6)
        out_ref[parity] = att * norm * gain


def apply_body(pre, even, own, recv, g, u, dt, gain_in, att, out_ref, flat_ref):
    zh = lax.axis_index("zh")
    pre_ref, even_ref, own_ref, recv_ref, gain_ref, att_ref = [
        x.get() for x in (pre, even, own, recv, gain_in, att)
    ]
    for c in range(PAIRS):
        flat_ref[c * CHUNK : (c + 1) * CHUNK, :] = pre_ref[c].astype(F32)[0:CHUNK]
    keep = jnp.where(zh == 0, tail(own_ref)[:, BLK : BLK + 1], tail(recv_ref)[:, BLK : BLK + 1])
    gain = jnp.where(zh == 0, gain_ref[:, :HD], gain_ref[:, HD:])
    q_own = queries(own_ref)
    q_recv = queries(recv_ref)
    base = [x.get()[...] for x in (g, u, dt)]
    for parity in range(2):
        q = jnp.where(zh == parity, q_own, q_recv)
        qf = q.astype(F32)
        rq = lax.rsqrt(jnp.mean(qf * qf, axis=1, keepdims=True) + 1e-6)
        mats = []
        for i in range(3):
            state = jnp.concatenate(
                [flat_ref[(3 * i + j) * HD : (3 * i + j + 1) * HD, :] for j in range(3)], axis=1
            )
            if parity == 1:
                state = keep * state + even_ref[i]
            mats.append(split(base[i] + state))
        gate = rq * (nn(q, mats[0][0]) + nn(q, mats[0][1]))
        up = rq * (nn(q, mats[1][0]) + nn(q, mats[1][1]))
        applied = nt3(split(gate * jax.nn.sigmoid(gate) * up), mats[2])
        norm = lax.rsqrt(jnp.mean(applied * applied, axis=1, keepdims=True) + 1e-6)
        mixed = (applied * norm * gain + att_ref[parity]).astype(BF16)
        for c in range(2):
            for z in range(4):
                out_ref[c * 2 + parity, (z % 2) * 32 : (z % 2) * 32 + 32, (z // 2) * HD : (z // 2 + 1) * HD] = mixed[
                    z * 64 + c * 32 : z * 64 + c * 32 + 32
                ]


def project_body(mix_ref, own_ref, other_ref, out_ref):
    core = lax.axis_index("c")
    total = None
    for w_ref, which in ((own_ref, core), (other_ref, 1 - core)):
        for zh in range(2):
            part = mix_ref[which * 2 + zh]
            part = jnp.concatenate([part[:, :HD], part[:, HD:]], axis=0)
            part = nn(part, w_ref[zh * HD : (zh + 1) * HD, :])
            total = part if total is None else total + part
    out_ref[...] = total.astype(BF16)


def total_body(parts, out_ref):
    ref = parts.get()
    out_ref[...] = sum(ref[i].astype(F32) for i in range(4)).astype(BF16)


def local(q, k, v, rates, decay, step, gate, up, down, ttt_gain, attn_gain, proj):
    sds = jax.ShapeDtypeStruct
    pay = sds((PAY, FD), BF16)
    rates = rates.T
    down = jnp.swapaxes(down, 1, 2)
    step = step.reshape(1, 2)
    (send,) = call(pack_body, [pay], (q, k, v, rates, decay), 0, 1_000_000)
    recv = lax.ppermute(send, "zh", [(0, 1), (1, 0)])
    proj_other = lax.ppermute(proj, "c", [(0, 1), (1, 0)])
    mats = sds((3, HD, FD), F32)
    flat = pltpu.VMEM((PAIRS * CHUNK + 64, 128), F32)
    upd, own = call(
        first_body,
        [mats, pay],
        (q, k, v, rates, decay, gate, up, down, step),
        6_000_000_000,
        3_000_000,
        mine=(5, 6, 7),
    )
    (pair_kv,) = call(join_body, [sds((2 * BLK, FD), BF16)], (own, recv), 0, 800_000)
    wins = [
        lax.ppermute(pair_kv, ("x", "y"), [(i, i + o) for i in range(PAIRS - o)]) for o in (1, 2, 3, 4)
    ]
    even, outgoing = call(
        second_body,
        [mats, sds((PAIRS, CROWS, 128), BF16)],
        (recv, gate, up, down, step, own, upd),
        6_000_000_000,
        4_000_000,
        scratch=[flat],
        mine=(1, 2, 3),
    )
    pieces = lax.all_to_all(outgoing, ("x", "y"), 0, 0, tiled=True)
    acc, stat = call(
        attend_first_body,
        [sds((2, BLK, HD), F32), sds((2, BLK, 128), F32)],
        (own, recv, pair_kv, wins[1], wins[3]),
        30000000000,
        2_000_000,
        600_000,
        scratch=[pltpu.VMEM((2, 5, BLK, BLK), F32)],
    )
    pieces, acc = lax.optimization_barrier((pieces, acc))
    (sums,) = call(scan_body, [sds((PAIRS, CROWS, 128), BF16)], (pieces,), 500_000, 1_000_000, cap=SMALL)
    prefix = lax.all_to_all(sums, ("x", "y"), 0, 0, tiled=True)
    (att,) = call(
        attend_second_body,
        [sds((2, BLK, HD), F32)],
        (own, recv, wins[0], wins[2], acc, stat, attn_gain.reshape(1, FD)),
        500_000_000,
        2_000_000,
        600_000,
        scratch=[pltpu.VMEM((2, 4, BLK, BLK), F32)],
    )
    (mixed,) = call(
        apply_body,
        [sds((4, 64, FD), BF16)],
        (prefix, even, own, recv, gate, up, down, ttt_gain.reshape(1, FD), att),
        600_000_000,
        5_000_000,
        scratch=[flat],
        mine=(4, 5, 6),
    )
    mixed = lax.all_to_all(mixed, ("c", "zh"), 0, 0, tiled=True)
    tile = 512
    partial = pl.pallas_call(
        project_body,
        out_shape=sds((128, WIDTH), BF16),
        grid=(WIDTH // tile,),
        in_specs=[
            pl.BlockSpec((4, 64, FD), lambda i: (0, 0, 0)),
            pl.BlockSpec((FD, tile), lambda i: (0, i)),
            pl.BlockSpec((FD, tile), lambda i: (0, i)),
        ],
        out_specs=pl.BlockSpec((128, tile), lambda i: (0, i)),
        compiler_params=pltpu.CompilerParams(vmem_limit_bytes=SMALL),
        cost_estimate=pl.CostEstimate(flops=600_000_000, bytes_accessed=6_000_000, transcendentals=0),
    )(mixed, proj, proj_other)
    parts = lax.all_to_all(partial.reshape(4, 32, WIDTH), "zl", 0, 0, tiled=True)
    (result,) = call(total_body, [sds((32, WIDTH), BF16)], (parts,), 400_000, 1_000_000, cap=SMALL)
    return result


def solution(mesh):
    fine = Mesh(mesh.devices.reshape(4, 4, 2, 4, 2), ("x", "y", "zh", "zl", "c"))
    seq = ("x", "y", "zh")
    head = ("zl", "c")
    in_specs = (
        P(seq, head),
        P(seq, head),
        P(seq, head),
        P(seq, head),
        P(seq, head),
        P(head),
        P(head, None, None),
        P(head, None, None),
        P(head, None, None),
        P(head),
        P(head),
        P(head, None),
    )
    out_specs = P(("x", "y", "zh", "zl", "c"), None)
    return jax.shard_map(local, mesh=fine, in_specs=in_specs, out_specs=out_specs, check_vma=False)
```

```python
import functools
import math

import jax
import jax.numpy as jnp
from jax import lax
from jax.experimental import pallas as pl
from jax.experimental.pallas import tpu as pltpu
from jax.sharding import Mesh, PartitionSpec as P

F32 = jnp.float32
BF16 = jnp.bfloat16
HD = 192
FD = 384
BLK = 256
WIDTH = 3072
NS_STEPS = 5
PAIRS = 16
CHUNK = 108
CROWS = 112
PAY = 272
COEF = (3.4445, -4.775, 2.0315)
VMEM_CAP = 60 * 1024 * 1024
SMALL = 12 * 1024 * 1024


class Lazy:
    def __init__(self, copy, ref):
        self.copy, self.ref = copy, ref

    def get(self):
        if self.copy is not None:
            self.copy.wait()
            self.copy = None
        return self.ref


def call(body, outs, ins, flops, nbytes, trans=0, scratch=(), mine=(), cap=VMEM_CAP):
    outs = list(outs)
    n_in, n_out = len(ins), len(outs)
    shapes = [a.shape[1:] if i in mine else a.shape for i, a in enumerate(ins)]

    def kernel(*refs):
        in_refs, out_refs = refs[:n_in], refs[n_in : n_in + n_out]
        rest = refs[n_in + n_out :]
        in_vm, out_vm = rest[:n_in], rest[n_in : n_in + n_out]
        in_sem, out_sem, extra = rest[n_in + n_out], rest[n_in + n_out + 1], rest[n_in + n_out + 2 :]
        zh = lax.axis_index("zh")
        lazy = []
        for i in range(n_in):
            src = in_refs[i].at[zh] if i in mine else in_refs[i]
            copy = pltpu.make_async_copy(src, in_vm[i], in_sem.at[i])
            copy.start()
            lazy.append(Lazy(copy, in_vm[i]))
        copies = [pltpu.make_async_copy(out_vm[i], out_refs[i], out_sem.at[i]) for i in range(n_out)]
        body(*lazy, *out_vm, *extra)
        for copy in copies:
            copy.start()
        for item in lazy:
            item.get()
        for copy in copies:
            copy.wait()

    any_spec = pl.BlockSpec(memory_space=pltpu.MemorySpace.HBM)
    return pl.pallas_call(
        kernel,
        out_shape=outs,
        in_specs=[any_spec] * n_in,
        out_specs=[any_spec] * n_out,
        scratch_shapes=[pltpu.VMEM(sh, a.dtype) for sh, a in zip(shapes, ins)]
        + [pltpu.VMEM(o.shape, o.dtype) for o in outs]
        + [pltpu.SemaphoreType.DMA((n_in,)), pltpu.SemaphoreType.DMA((n_out,))]
        + list(scratch),
        compiler_params=pltpu.CompilerParams(vmem_limit_bytes=cap),
        cost_estimate=pl.CostEstimate(flops=flops, bytes_accessed=nbytes, transcendentals=trans),
    )(*ins)


def nn(a, b):
    return lax.dot_general(a, b, (((1,), (0,)), ((), ())), preferred_element_type=F32)


def nt(a, b):
    return lax.dot_general(a, b, (((1,), (1,)), ((), ())), preferred_element_type=F32)


def split(x):
    hi = x.astype(BF16)
    return hi, (x - hi.astype(F32)).astype(BF16)


def nn3(a, b):
    return nn(a[0], b[0]) + (nn(a[0], b[1]) + nn(a[1], b[0]))


def nt3(a, b):
    return nt(a[0], b[0]) + (nt(a[0], b[1]) + nt(a[1], b[0]))


def three(x):
    hi = x.astype(BF16).astype(F32)
    mid = (x - hi).astype(BF16).astype(F32)
    low = x - hi - mid
    row = lax.broadcasted_iota(jnp.int32, x.shape, 0)
    return jnp.where(row == 0, hi, jnp.where(row == 1, mid, jnp.where(row == 2, low, 0.0)))


def pick(ref, who):
    return jnp.where(who == 0, ref[:, :HD], ref[:, HD:])


def one_of(row, who):
    return jnp.where(who == 0, row[0:1], row[1:2])


def fill(out_ref, k, v, rate_row, decay):
    out_ref[0:BLK, 0:HD] = k
    out_ref[0:BLK, HD:] = v
    row = jnp.concatenate([rate_row, jnp.broadcast_to(decay, (1, 128))], axis=1)
    out_ref[BLK:PAY, :] = three(jnp.broadcast_to(row, (16, FD))).astype(BF16)


def fold_queries(out_ref, q):
    out_ref[:, 0:HD] = q[0:128]
    out_ref[:, HD:] = q[128:256]


def pack_body(k, v, r, d, q, send_ref, query_ref):
    who = 1 - lax.axis_index("zh")
    fill(
        send_ref,
        pick(k.get(), who),
        pick(v.get(), who),
        one_of(r.get()[...], who),
        jnp.where(who == 0, d.get()[:, 0:1], d.get()[:, 1:2]),
    )
    fold_queries(query_ref, pick(q.get(), who))


def tail(pay_ref):
    rows = pay_ref[BLK:PAY, :].astype(F32)
    return rows[0:1] + rows[1:2] + rows[2:3]


def queries(ref):
    both = ref[...]
    return jnp.concatenate([both[:, :HD], both[:, HD:]], axis=0)


def orthogonalize(mats):
    norms = [jnp.sqrt(jnp.sum(m * m, keepdims=True)) + 1e-7 for m in mats]
    mats = [m / n for m, n in zip(mats, norms)]
    for _ in range(NS_STEPS):
        parts = [split(x) for x in mats]
        grams = []
        for hi, lo in parts:
            cross = nt(hi, lo)
            grams.append(nt(hi, hi) + (cross + cross.T))
        polys = []
        for gram in grams:
            hi, lo = split(gram)
            cross = nn(hi, lo)
            polys.append(split(COEF[1] * gram + COEF[2] * (nn(hi, hi) + (cross + cross.T))))
        mats = [COEF[0] * x + nn3(p, s) for x, p, s in zip(mats, polys, parts)]
    return mats


def fast_updates(k, v, rate_row, g, u, dt, step):
    kf = k.astype(F32)
    rk = lax.rsqrt(jnp.mean(kf * kf, axis=1, keepdims=True) + 1e-6)
    rate = jnp.broadcast_to(rate_row, (128, BLK)).T[:, 0:1]
    gh, gl = split(g.get()[...])
    pre_gate = rk * (nn(k, gh) + nn(k, gl))
    uh, ul = split(u.get()[...])
    pre_up = rk * (nn(k, uh) + nn(k, ul))
    dh, dl = split(dt.get()[...])
    back = -rate * (nn(v, dh) + nn(v, dl))
    sig = jax.nn.sigmoid(pre_gate)
    act = pre_gate * sig
    mid_h, mid_l = split(-rate * (act * pre_up))
    gate_h, gate_l = split(rk * (back * pre_up * (sig * (1.0 + pre_gate * (1.0 - sig)))))
    up_h, up_l = split(rk * (back * act))
    kt = k.T
    vt = v.T
    grads = [
        nn(kt, gate_h) + nn(kt, gate_l),
        nn(kt, up_h) + nn(kt, up_l),
        nn(vt, mid_h) + nn(vt, mid_l),
    ]
    row = step.get()[...]
    scale = -jnp.where(lax.axis_index("zh") == 0, row[:, 0:1], row[:, 1:2])
    return [scale * x for x in orthogonalize(grads)]


def first_body(k, v, r, d, g, u, dt, step, q, upd_ref, own_ref, query_ref):
    zh = lax.axis_index("zh")
    key = pick(k.get(), zh)
    value = pick(v.get(), zh)
    rate_row = one_of(r.get()[...], zh)
    fill(own_ref, key, value, rate_row, jnp.where(zh == 0, d.get()[:, 0:1], d.get()[:, 1:2]))
    for i, x in enumerate(fast_updates(key, value, rate_row, g, u, dt, step)):
        upd_ref[i] = x
    fold_queries(query_ref, pick(q.get(), zh))


def relay_body(pair_kv, shifted, two_ref, three_ref):
    y = lax.axis_index("y")
    here = pair_kv.get()[...]
    before = shifted.get()[...]
    two_ref[...] = jnp.where(y < 2, here, before)
    three_ref[...] = jnp.where(y < 1, here, before)


def join_body(own, recv, out_ref):
    out_ref[0:BLK] = own.get()[0:BLK]
    out_ref[BLK:] = recv.get()[0:BLK]


def second_body(pay, g, u, dt, step, own, upd, even_ref, send_ref, flat_ref):
    pay_ref = pay.get()
    others = fast_updates(
        pay_ref[0:BLK, 0:HD], pay_ref[0:BLK, HD:], tail(pay_ref)[:, :BLK], g, u, dt, step
    )
    zh = lax.axis_index("zh")
    upd_ref = upd.get()
    mine = tail(own.get())[:, BLK:]
    theirs = tail(pay_ref)[:, BLK:]
    keep_even = jnp.where(zh == 0, mine, theirs)
    keep_odd = jnp.where(zh == 0, theirs, mine)
    flat_ref[PAIRS * CHUNK :, :] = jnp.zeros((64, 128), F32)
    for i in range(3):
        other = others[i]
        own_upd = upd_ref[i]
        even = jnp.where(zh == 0, own_upd, other)
        odd = jnp.where(zh == 0, other, own_upd)
        even_ref[i] = even
        for j in range(3):
            cols = slice(j * 128, (j + 1) * 128)
            flat_ref[(3 * i + j) * HD : (3 * i + j + 1) * HD, :] = keep_odd * even[:, cols] + odd[:, cols]
    keep = three(jnp.broadcast_to(keep_even * keep_odd, (16, 128)))[0:4]
    for c in range(PAIRS):
        send_ref[c] = jnp.concatenate([flat_ref[c * CHUNK : (c + 1) * CHUNK, :], keep], axis=0).astype(BF16)


def scan_body(pieces, out_ref):
    in_ref = pieces.get()
    run = jnp.zeros((CROWS, 128), F32)
    for j in range(PAIRS):
        out_ref[j] = run.astype(BF16)
        if j < PAIRS - 1:
            here = in_ref[j].astype(F32)
            keep = here[CHUNK : CHUNK + 1] + here[CHUNK + 1 : CHUNK + 2] + here[CHUNK + 2 : CHUNK + 3]
            run = keep * run + here


def scores_of(q, keys, blocks, score_ref, rows_of, pair):
    row = lax.broadcasted_iota(jnp.int32, (BLK, BLK), 0)
    col = lax.broadcasted_iota(jnp.int32, (BLK, BLK), 1)
    top = None
    for n, (o, e, kind) in enumerate(blocks):
        s = nt(q, keys[o][rows_of(e), 0:HD]) * (1.0 / math.sqrt(HD))
        if kind == "oldest":
            s = jnp.where(col > row, s, -1e30)
        if kind == "newest":
            s = jnp.where(col <= row, s, -1e30)
        if o > 0:
            s = s + jnp.where(pair >= o, 0.0, -1e30)
        score_ref[n] = s
        top = s if top is None else jnp.maximum(top, s)
    return jnp.max(top, axis=1, keepdims=True)


def weighted(values, blocks, score_ref, rows_of, top):
    total = None
    acc = None
    for n, (o, e, _) in enumerate(blocks):
        w = jnp.exp(score_ref[n] - top)
        total = w if total is None else total + w
        part = nn(w.astype(BF16), values[o][rows_of(e), HD:])
        acc = part if acc is None else acc + part
    return jnp.sum(total, axis=1, keepdims=True), acc


def window_blocks(parity, offsets):
    blocks = [(o, e) for o in (4, 3, 2, 1, 0) for e in (0, 1)][parity : parity + 9]
    kinds = ["oldest"] + ["inner"] * 7 + ["newest"]
    return [(o, e, kind) for (o, e), kind in zip(blocks, kinds) if o in offsets]


def ordered_rows(zh):
    def rows_of(parity):
        slot = zh if parity == 0 else 1 - zh
        return pl.ds(pl.multiple_of(slot * BLK, BLK), BLK)

    return rows_of


def pair_index():
    return lax.axis_index("x") * 4 + lax.axis_index("y")


def attend_first_body(own, recv, pair_kv, shifted, w1, acc_ref, stat_ref, score_ref):
    zh = lax.axis_index("zh")
    q_own = queries(own.get())
    q_recv = queries(recv.get())
    wins = {0: pair_kv.get(), 4: shifted.get(), 1: w1.get()}
    rows_of = ordered_rows(zh)
    lane = lax.broadcasted_iota(jnp.int32, (BLK, 128), 1)
    for parity in range(2):
        q = jnp.where(zh == parity, q_own, q_recv)
        blocks = window_blocks(parity, wins)
        scores = score_ref.at[parity]
        top = scores_of(q, wins, blocks, scores, rows_of, pair_index())
        total, acc = weighted(wins, blocks, scores, rows_of, top)
        acc_ref[parity] = acc
        stat_ref[parity] = jnp.where(lane < 64, top, total)


def attend_second_body(own, recv, w2, w3, acc_in, stat, gain_in, out_ref, score_ref):
    zh = lax.axis_index("zh")
    q_own = queries(own.get())
    q_recv = queries(recv.get())
    gain_ref = gain_in.get()
    wins = {2: w2.get(), 3: w3.get()}
    gain = jnp.where(zh == 0, gain_ref[:, :HD], gain_ref[:, HD:])
    rows_of = ordered_rows(zh)
    stats = stat.get()
    before = acc_in.get()
    for parity in range(2):
        q = jnp.where(zh == parity, q_own, q_recv)
        blocks = window_blocks(parity, wins)
        scores = score_ref.at[parity]
        old_top = stats[parity, :, 0:1]
        top = jnp.maximum(old_top, scores_of(q, wins, blocks, scores, rows_of, pair_index()))
        total, acc = weighted(wins, blocks, scores, rows_of, top)
        rescale = jnp.exp(old_top - top)
        total = total + rescale * stats[parity, :, 64:65]
        att = (acc + rescale * before[parity]) / total
        norm = lax.rsqrt(jnp.mean(att * att, axis=1, keepdims=True) + 1e-6)
        out_ref[parity] = att * norm * gain


def apply_body(pre, even, own, recv, q_mine, q_theirs, g, u, dt, gain_in, att, out_ref, flat_ref):
    zh = lax.axis_index("zh")
    pre_ref, even_ref, own_ref, recv_ref, gain_ref, att_ref = [
        x.get() for x in (pre, even, own, recv, gain_in, att)
    ]
    for c in range(PAIRS):
        flat_ref[c * CHUNK : (c + 1) * CHUNK, :] = pre_ref[c].astype(F32)[0:CHUNK]
    keep = jnp.where(zh == 0, tail(own_ref)[:, BLK : BLK + 1], tail(recv_ref)[:, BLK : BLK + 1])
    gain = jnp.where(zh == 0, gain_ref[:, :HD], gain_ref[:, HD:])
    q_own = queries(q_mine.get())
    q_recv = queries(q_theirs.get())
    base = [x.get()[...] for x in (g, u, dt)]
    for parity in range(2):
        q = jnp.where(zh == parity, q_own, q_recv)
        qf = q.astype(F32)
        rq = lax.rsqrt(jnp.mean(qf * qf, axis=1, keepdims=True) + 1e-6)
        mats = []
        for i in range(3):
            state = jnp.concatenate(
                [flat_ref[(3 * i + j) * HD : (3 * i + j + 1) * HD, :] for j in range(3)], axis=1
            )
            if parity == 1:
                state = keep * state + even_ref[i]
            mats.append(split(base[i] + state))
        gate = rq * (nn(q, mats[0][0]) + nn(q, mats[0][1]))
        up = rq * (nn(q, mats[1][0]) + nn(q, mats[1][1]))
        applied = nt3(split(gate * jax.nn.sigmoid(gate) * up), mats[2])
        norm = lax.rsqrt(jnp.mean(applied * applied, axis=1, keepdims=True) + 1e-6)
        mixed = (applied * norm * gain + att_ref[parity]).astype(BF16)
        for c in range(2):
            for z in range(4):
                out_ref[c * 2 + parity, (z % 2) * 32 : (z % 2) * 32 + 32, (z // 2) * HD : (z // 2 + 1) * HD] = mixed[
                    z * 64 + c * 32 : z * 64 + c * 32 + 32
                ]


def project_body(mix_ref, own_ref, other_ref, out_ref):
    core = lax.axis_index("c")
    total = None
    for w_ref, which in ((own_ref, core), (other_ref, 1 - core)):
        for zh in range(2):
            part = mix_ref[which * 2 + zh]
            part = jnp.concatenate([part[:, :HD], part[:, HD:]], axis=0)
            part = nn(part, w_ref[zh * HD : (zh + 1) * HD, :])
            total = part if total is None else total + part
    out_ref[...] = total.astype(BF16)


def total_body(parts, out_ref):
    ref = parts.get()
    out_ref[...] = sum(ref[i].astype(F32) for i in range(4)).astype(BF16)


def local(q, k, v, rates, decay, step, gate, up, down, ttt_gain, attn_gain, proj):
    sds = jax.ShapeDtypeStruct
    pay = sds((PAY, FD), BF16)
    rates = rates.T
    down = jnp.swapaxes(down, 1, 2)
    step = step.reshape(1, 2)
    folded = sds((128, FD), BF16)
    send, send_q = call(pack_body, [pay, folded], (k, v, rates, decay, q), 0, 1_000_000)
    recv = lax.ppermute(send, "zh", [(0, 1), (1, 0)])
    proj_other = lax.ppermute(proj, "c", [(0, 1), (1, 0)])
    mats = sds((3, HD, FD), F32)
    flat = pltpu.VMEM((PAIRS * CHUNK + 64, 128), F32)
    upd, own, own_q = call(
        first_body,
        [mats, pay, folded],
        (k, v, rates, decay, gate, up, down, step, q),
        6_000_000_000,
        3_000_000,
        mine=(4, 5, 6),
    )
    (pair_kv,) = call(join_body, [sds((2 * BLK, FD), BF16)], (own, recv), 0, 800_000)
    shifted = lax.ppermute(pair_kv, "x", [(i, i + 1) for i in range(3)])
    w1 = lax.ppermute(pair_kv, ("x", "y"), [(i, i + 1) for i in range(PAIRS - 1)])
    even, outgoing = call(
        second_body,
        [mats, sds((PAIRS, CROWS, 128), BF16)],
        (recv, gate, up, down, step, own, upd),
        6_000_000_000,
        4_000_000,
        scratch=[flat],
        mine=(1, 2, 3),
    )
    window = sds((2 * BLK, FD), BF16)
    two, three_back = call(relay_body, [window, window], (pair_kv, shifted), 0, 1_000_000)
    outgoing, two, three_back, send_q = lax.optimization_barrier((outgoing, two, three_back, send_q))
    w2 = lax.ppermute(two, "y", [(i, (i + 2) % 4) for i in range(4)])
    w3 = lax.ppermute(three_back, "y", [(i, (i + 3) % 4) for i in range(4)])
    recv_q = lax.ppermute(send_q, "zh", [(0, 1), (1, 0)])
    pieces = lax.all_to_all(outgoing, ("x", "y"), 0, 0, tiled=True)
    acc, stat = call(
        attend_first_body,
        [sds((2, BLK, HD), F32), sds((2, BLK, 128), F32)],
        (own_q, recv_q, pair_kv, shifted, w1),
        30_000_000_000,
        2_000_000,
        600_000,
        scratch=[pltpu.VMEM((2, 5, BLK, BLK), F32)],
    )
    pieces, acc = lax.optimization_barrier((pieces, acc))
    (sums,) = call(scan_body, [sds((PAIRS, CROWS, 128), BF16)], (pieces,), 500_000, 1_000_000, cap=SMALL)
    prefix = lax.all_to_all(sums, ("x", "y"), 0, 0, tiled=True)
    (att,) = call(
        attend_second_body,
        [sds((2, BLK, HD), F32)],
        (own_q, recv_q, w2, w3, acc, stat, attn_gain.reshape(1, FD)),
        500_000_000,
        2_000_000,
        600_000,
        scratch=[pltpu.VMEM((2, 4, BLK, BLK), F32)],
    )
    (mixed,) = call(
        apply_body,
        [sds((4, 64, FD), BF16)],
        (prefix, even, own, recv, own_q, recv_q, gate, up, down, ttt_gain.reshape(1, FD), att),
        600_000_000,
        5_000_000,
        scratch=[flat],
        mine=(6, 7, 8),
    )
    mixed = lax.all_to_all(mixed, ("c", "zh"), 0, 0, tiled=True)
    tile = 512
    partial = pl.pallas_call(
        project_body,
        out_shape=sds((128, WIDTH), BF16),
        grid=(WIDTH // tile,),
        in_specs=[
            pl.BlockSpec((4, 64, FD), lambda i: (0, 0, 0)),
            pl.BlockSpec((FD, tile), lambda i: (0, i)),
            pl.BlockSpec((FD, tile), lambda i: (0, i)),
        ],
        out_specs=pl.BlockSpec((128, tile), lambda i: (0, i)),
        compiler_params=pltpu.CompilerParams(vmem_limit_bytes=SMALL),
        cost_estimate=pl.CostEstimate(flops=600_000_000, bytes_accessed=6_000_000, transcendentals=0),
    )(mixed, proj, proj_other)
    parts = lax.all_to_all(partial.reshape(4, 32, WIDTH), "zl", 0, 0, tiled=True)
    (result,) = call(total_body, [sds((32, WIDTH), BF16)], (parts,), 400_000, 1_000_000, cap=SMALL)
    return result


def solution(mesh):
    fine = Mesh(mesh.devices.reshape(4, 4, 2, 4, 2), ("x", "y", "zh", "zl", "c"))
    seq = ("x", "y", "zh")
    head = ("zl", "c")
    in_specs = (
        P(seq, head),
        P(seq, head),
        P(seq, head),
        P(seq, head),
        P(seq, head),
        P(head),
        P(head, None, None),
        P(head, None, None),
        P(head, None, None),
        P(head),
        P(head),
        P(head, None),
    )
    out_specs = P(("x", "y", "zh", "zl", "c"), None)
    return jax.shard_map(local, mesh=fine, in_specs=in_specs, out_specs=out_specs, check_vma=False)
```

```python
import functools
import math

import jax
import jax.numpy as jnp
from jax import lax
from jax.experimental import pallas as pl
from jax.experimental.pallas import tpu as pltpu
from jax.sharding import Mesh, PartitionSpec as P

F32 = jnp.float32
BF16 = jnp.bfloat16
HD = 192
FD = 384
BLK = 256
WIDTH = 3072
NS_STEPS = 5
PAIRS = 16
CHUNK = 108
CROWS = 112
PAY = 272
COEF = (3.4445, -4.775, 2.0315)
VMEM_CAP = 60 * 1024 * 1024
SMALL = 12 * 1024 * 1024


class Lazy:
    def __init__(self, copy, ref):
        self.copy, self.ref = copy, ref

    def get(self):
        if self.copy is not None:
            self.copy.wait()
            self.copy = None
        return self.ref


def call(body, outs, ins, flops, nbytes, trans=0, scratch=(), mine=(), cap=VMEM_CAP):
    outs = list(outs)
    n_in, n_out = len(ins), len(outs)
    shapes = [a.shape[1:] if i in mine else a.shape for i, a in enumerate(ins)]

    def kernel(*refs):
        in_refs, out_refs = refs[:n_in], refs[n_in : n_in + n_out]
        rest = refs[n_in + n_out :]
        in_vm, out_vm = rest[:n_in], rest[n_in : n_in + n_out]
        in_sem, out_sem, extra = rest[n_in + n_out], rest[n_in + n_out + 1], rest[n_in + n_out + 2 :]
        zh = lax.axis_index("zh")
        lazy = []
        for i in range(n_in):
            src = in_refs[i].at[zh] if i in mine else in_refs[i]
            copy = pltpu.make_async_copy(src, in_vm[i], in_sem.at[i])
            copy.start()
            lazy.append(Lazy(copy, in_vm[i]))
        copies = [pltpu.make_async_copy(out_vm[i], out_refs[i], out_sem.at[i]) for i in range(n_out)]
        body(*lazy, *out_vm, *extra)
        for copy in copies:
            copy.start()
        for item in lazy:
            item.get()
        for copy in copies:
            copy.wait()

    any_spec = pl.BlockSpec(memory_space=pltpu.MemorySpace.HBM)
    return pl.pallas_call(
        kernel,
        out_shape=outs,
        in_specs=[any_spec] * n_in,
        out_specs=[any_spec] * n_out,
        scratch_shapes=[pltpu.VMEM(sh, a.dtype) for sh, a in zip(shapes, ins)]
        + [pltpu.VMEM(o.shape, o.dtype) for o in outs]
        + [pltpu.SemaphoreType.DMA((n_in,)), pltpu.SemaphoreType.DMA((n_out,))]
        + list(scratch),
        compiler_params=pltpu.CompilerParams(vmem_limit_bytes=cap),
        cost_estimate=pl.CostEstimate(flops=flops, bytes_accessed=nbytes, transcendentals=trans),
    )(*ins)


def nn(a, b):
    return lax.dot_general(a, b, (((1,), (0,)), ((), ())), preferred_element_type=F32)


def nt(a, b):
    return lax.dot_general(a, b, (((1,), (1,)), ((), ())), preferred_element_type=F32)


def split(x):
    hi = x.astype(BF16)
    return hi, (x - hi.astype(F32)).astype(BF16)


def nn3(a, b):
    return nn(a[0], b[0]) + (nn(a[0], b[1]) + nn(a[1], b[0]))


def nt3(a, b):
    return nt(a[0], b[0]) + (nt(a[0], b[1]) + nt(a[1], b[0]))


def three(x):
    hi = x.astype(BF16).astype(F32)
    mid = (x - hi).astype(BF16).astype(F32)
    low = x - hi - mid
    row = lax.broadcasted_iota(jnp.int32, x.shape, 0)
    return jnp.where(row == 0, hi, jnp.where(row == 1, mid, jnp.where(row == 2, low, 0.0)))


def pick(ref, who):
    return jnp.where(who == 0, ref[:, :HD], ref[:, HD:])


def one_of(row, who):
    return jnp.where(who == 0, row[0:1], row[1:2])


def fill(out_ref, k, v, rate_row, decay):
    out_ref[0:BLK, 0:HD] = k
    out_ref[0:BLK, HD:] = v
    row = jnp.concatenate([rate_row, jnp.broadcast_to(decay, (1, 128))], axis=1)
    out_ref[BLK:PAY, :] = three(jnp.broadcast_to(row, (16, FD))).astype(BF16)


def fold_queries(out_ref, q):
    out_ref[:, 0:HD] = q[0:128]
    out_ref[:, HD:] = q[128:256]


def pack_body(k, v, r, d, q, send_ref, query_ref):
    who = 1 - lax.axis_index("zh")
    fill(
        send_ref,
        pick(k.get(), who),
        pick(v.get(), who),
        one_of(r.get()[...], who),
        jnp.where(who == 0, d.get()[:, 0:1], d.get()[:, 1:2]),
    )
    fold_queries(query_ref, pick(q.get(), who))


def tail(pay_ref):
    rows = pay_ref[BLK:PAY, :].astype(F32)
    return rows[0:1] + rows[1:2] + rows[2:3]


def queries(ref):
    both = ref[...]
    return jnp.concatenate([both[:, :HD], both[:, HD:]], axis=0)


def orthogonalize(mats):
    norms = [jnp.sqrt(jnp.sum(m * m, keepdims=True)) + 1e-7 for m in mats]
    mats = [m / n for m, n in zip(mats, norms)]
    for _ in range(NS_STEPS):
        parts = [split(x) for x in mats]
        grams = []
        for hi, lo in parts:
            cross = nt(hi, lo)
            grams.append(nt(hi, hi) + (cross + cross.T))
        polys = []
        for gram in grams:
            hi, lo = split(gram)
            cross = nn(hi, lo)
            polys.append(split(COEF[1] * gram + COEF[2] * (nn(hi, hi) + (cross + cross.T))))
        mats = [COEF[0] * x + nn3(p, s) for x, p, s in zip(mats, polys, parts)]
    return mats


def fast_updates(k, v, rate_row, g, u, dt, step):
    kf = k.astype(F32)
    rk = lax.rsqrt(jnp.mean(kf * kf, axis=1, keepdims=True) + 1e-6)
    rate = jnp.broadcast_to(rate_row, (128, BLK)).T[:, 0:1]
    gh, gl = split(g.get()[...])
    pre_gate = rk * (nn(k, gh) + nn(k, gl))
    uh, ul = split(u.get()[...])
    pre_up = rk * (nn(k, uh) + nn(k, ul))
    dh, dl = split(dt.get()[...])
    back = -rate * (nn(v, dh) + nn(v, dl))
    sig = jax.nn.sigmoid(pre_gate)
    act = pre_gate * sig
    mid_h, mid_l = split(-rate * (act * pre_up))
    gate_h, gate_l = split(rk * (back * pre_up * (sig * (1.0 + pre_gate * (1.0 - sig)))))
    up_h, up_l = split(rk * (back * act))
    kt = k.T
    vt = v.T
    grads = [
        nn(kt, gate_h) + nn(kt, gate_l),
        nn(kt, up_h) + nn(kt, up_l),
        nn(vt, mid_h) + nn(vt, mid_l),
    ]
    row = step.get()[...]
    scale = -jnp.where(lax.axis_index("zh") == 0, row[:, 0:1], row[:, 1:2])
    return [scale * x for x in orthogonalize(grads)]


def first_body(k, v, r, d, g, u, dt, step, q, upd_ref, own_ref, query_ref):
    zh = lax.axis_index("zh")
    key = pick(k.get(), zh)
    value = pick(v.get(), zh)
    rate_row = one_of(r.get()[...], zh)
    fill(own_ref, key, value, rate_row, jnp.where(zh == 0, d.get()[:, 0:1], d.get()[:, 1:2]))
    for i, x in enumerate(fast_updates(key, value, rate_row, g, u, dt, step)):
        upd_ref[i] = x
    fold_queries(query_ref, pick(q.get(), zh))


def relay_body(pair_kv, shifted, out_ref):
    y = lax.axis_index("y")
    out_ref[...] = jnp.where(y < 1, pair_kv.get()[...], shifted.get()[...])


def join_body(own, recv, out_ref):
    out_ref[0:BLK] = own.get()[0:BLK]
    out_ref[BLK:] = recv.get()[0:BLK]


def second_body(pay, g, u, dt, step, own, upd, even_ref, send_ref, flat_ref):
    pay_ref = pay.get()
    others = fast_updates(
        pay_ref[0:BLK, 0:HD], pay_ref[0:BLK, HD:], tail(pay_ref)[:, :BLK], g, u, dt, step
    )
    zh = lax.axis_index("zh")
    upd_ref = upd.get()
    mine = tail(own.get())[:, BLK:]
    theirs = tail(pay_ref)[:, BLK:]
    keep_even = jnp.where(zh == 0, mine, theirs)
    keep_odd = jnp.where(zh == 0, theirs, mine)
    flat_ref[PAIRS * CHUNK :, :] = jnp.zeros((64, 128), F32)
    for i in range(3):
        other = others[i]
        own_upd = upd_ref[i]
        even = jnp.where(zh == 0, own_upd, other)
        odd = jnp.where(zh == 0, other, own_upd)
        even_ref[i] = even
        for j in range(3):
            cols = slice(j * 128, (j + 1) * 128)
            flat_ref[(3 * i + j) * HD : (3 * i + j + 1) * HD, :] = keep_odd * even[:, cols] + odd[:, cols]
    keep = three(jnp.broadcast_to(keep_even * keep_odd, (16, 128)))[0:4]
    for c in range(PAIRS):
        send_ref[c] = jnp.concatenate([flat_ref[c * CHUNK : (c + 1) * CHUNK, :], keep], axis=0).astype(BF16)


def scan_body(pieces, out_ref):
    in_ref = pieces.get()
    run = jnp.zeros((CROWS, 128), F32)
    for j in range(PAIRS):
        out_ref[j] = run.astype(BF16)
        if j < PAIRS - 1:
            here = in_ref[j].astype(F32)
            keep = here[CHUNK : CHUNK + 1] + here[CHUNK + 1 : CHUNK + 2] + here[CHUNK + 2 : CHUNK + 3]
            run = keep * run + here


def scores_of(q, keys, blocks, score_ref, rows_of, pair):
    row = lax.broadcasted_iota(jnp.int32, (BLK, BLK), 0)
    col = lax.broadcasted_iota(jnp.int32, (BLK, BLK), 1)
    top = None
    for n, (o, e, kind) in enumerate(blocks):
        s = nt(q, keys[o][rows_of(e), 0:HD]) * (1.0 / math.sqrt(HD))
        if kind == "oldest":
            s = jnp.where(col > row, s, -1e30)
        if kind == "newest":
            s = jnp.where(col <= row, s, -1e30)
        if o > 0:
            s = s + jnp.where(pair >= o, 0.0, -1e30)
        score_ref[n] = s
        top = s if top is None else jnp.maximum(top, s)
    return jnp.max(top, axis=1, keepdims=True)


def weighted(values, blocks, score_ref, rows_of, top):
    total = None
    acc = None
    for n, (o, e, _) in enumerate(blocks):
        w = jnp.exp(score_ref[n] - top)
        total = w if total is None else total + w
        part = nn(w.astype(BF16), values[o][rows_of(e), HD:])
        acc = part if acc is None else acc + part
    return jnp.sum(total, axis=1, keepdims=True), acc


def window_blocks(parity, offsets):
    blocks = [(o, e) for o in (4, 3, 2, 1, 0) for e in (0, 1)][parity : parity + 9]
    kinds = ["oldest"] + ["inner"] * 7 + ["newest"]
    return [(o, e, kind) for (o, e), kind in zip(blocks, kinds) if o in offsets]


def ordered_rows(zh):
    def rows_of(parity):
        slot = zh if parity == 0 else 1 - zh
        return pl.ds(pl.multiple_of(slot * BLK, BLK), BLK)

    return rows_of


def pair_index():
    return lax.axis_index("x") * 4 + lax.axis_index("y")


def attend_first_body(own, recv, pair_kv, shifted, w2, acc_ref, stat_ref, score_ref):
    zh = lax.axis_index("zh")
    q_own = queries(own.get())
    q_recv = queries(recv.get())
    wins = {0: pair_kv.get(), 4: shifted.get(), 2: w2.get()}
    rows_of = ordered_rows(zh)
    lane = lax.broadcasted_iota(jnp.int32, (BLK, 128), 1)
    for parity in range(2):
        q = jnp.where(zh == parity, q_own, q_recv)
        blocks = window_blocks(parity, wins)
        scores = score_ref.at[parity]
        top = scores_of(q, wins, blocks, scores, rows_of, pair_index())
        total, acc = weighted(wins, blocks, scores, rows_of, top)
        acc_ref[parity] = acc
        stat_ref[parity] = jnp.where(lane < 64, top, total)


def attend_second_body(own, recv, w1, w3, acc_in, stat, gain_in, out_ref, score_ref):
    zh = lax.axis_index("zh")
    q_own = queries(own.get())
    q_recv = queries(recv.get())
    gain_ref = gain_in.get()
    wins = {1: w1.get(), 3: w3.get()}
    gain = jnp.where(zh == 0, gain_ref[:, :HD], gain_ref[:, HD:])
    rows_of = ordered_rows(zh)
    stats = stat.get()
    before = acc_in.get()
    for parity in range(2):
        q = jnp.where(zh == parity, q_own, q_recv)
        blocks = window_blocks(parity, wins)
        scores = score_ref.at[parity]
        old_top = stats[parity, :, 0:1]
        top = jnp.maximum(old_top, scores_of(q, wins, blocks, scores, rows_of, pair_index()))
        total, acc = weighted(wins, blocks, scores, rows_of, top)
        rescale = jnp.exp(old_top - top)
        total = total + rescale * stats[parity, :, 64:65]
        att = (acc + rescale * before[parity]) / total
        norm = lax.rsqrt(jnp.mean(att * att, axis=1, keepdims=True) + 1e-6)
        out_ref[parity] = att * norm * gain


def apply_body(pre, even, own, recv, q_mine, q_theirs, g, u, dt, gain_in, att, out_ref, flat_ref):
    zh = lax.axis_index("zh")
    pre_ref, even_ref, own_ref, recv_ref, gain_ref, att_ref = [
        x.get() for x in (pre, even, own, recv, gain_in, att)
    ]
    for c in range(PAIRS):
        flat_ref[c * CHUNK : (c + 1) * CHUNK, :] = pre_ref[c].astype(F32)[0:CHUNK]
    keep = jnp.where(zh == 0, tail(own_ref)[:, BLK : BLK + 1], tail(recv_ref)[:, BLK : BLK + 1])
    gain = jnp.where(zh == 0, gain_ref[:, :HD], gain_ref[:, HD:])
    q_own = queries(q_mine.get())
    q_recv = queries(q_theirs.get())
    base = [x.get()[...] for x in (g, u, dt)]
    for parity in range(2):
        q = jnp.where(zh == parity, q_own, q_recv)
        qf = q.astype(F32)
        rq = lax.rsqrt(jnp.mean(qf * qf, axis=1, keepdims=True) + 1e-6)
        mats = []
        for i in range(3):
            state = jnp.concatenate(
                [flat_ref[(3 * i + j) * HD : (3 * i + j + 1) * HD, :] for j in range(3)], axis=1
            )
            if parity == 1:
                state = keep * state + even_ref[i]
            mats.append(split(base[i] + state))
        gate = rq * (nn(q, mats[0][0]) + nn(q, mats[0][1]))
        up = rq * (nn(q, mats[1][0]) + nn(q, mats[1][1]))
        applied = nt3(split(gate * jax.nn.sigmoid(gate) * up), mats[2])
        norm = lax.rsqrt(jnp.mean(applied * applied, axis=1, keepdims=True) + 1e-6)
        mixed = (applied * norm * gain + att_ref[parity]).astype(BF16)
        for c in range(2):
            for z in range(4):
                out_ref[c * 2 + parity, (z % 2) * 32 : (z % 2) * 32 + 32, (z // 2) * HD : (z // 2 + 1) * HD] = mixed[
                    z * 64 + c * 32 : z * 64 + c * 32 + 32
                ]


def project_body(mix, own, other, out_ref):
    core = lax.axis_index("c")
    mix_ref = mix.get()
    total = None
    for w, which in ((own, core), (other, 1 - core)):
        w_ref = w.get()
        for zh in range(2):
            part = mix_ref[which * 2 + zh]
            part = jnp.concatenate([part[:, :HD], part[:, HD:]], axis=0)
            part = nn(part, w_ref[zh * HD : (zh + 1) * HD, :])
            total = part if total is None else total + part
    out_ref[...] = total.astype(BF16)


def total_body(parts, out_ref):
    ref = parts.get()
    out_ref[...] = sum(ref[i].astype(F32) for i in range(4)).astype(BF16)


def local(q, k, v, rates, decay, step, gate, up, down, ttt_gain, attn_gain, proj):
    sds = jax.ShapeDtypeStruct
    pay = sds((PAY, FD), BF16)
    rates = rates.T
    down = jnp.swapaxes(down, 1, 2)
    step = step.reshape(1, 2)
    folded = sds((128, FD), BF16)
    send, send_q = call(pack_body, [pay, folded], (k, v, rates, decay, q), 0, 1_000_000)
    recv = lax.ppermute(send, "zh", [(0, 1), (1, 0)])
    proj_other = lax.ppermute(proj, "c", [(0, 1), (1, 0)])
    mats = sds((3, HD, FD), F32)
    flat = pltpu.VMEM((PAIRS * CHUNK + 64, 128), F32)
    upd, own, own_q = call(
        first_body,
        [mats, pay, folded],
        (k, v, rates, decay, gate, up, down, step, q),
        6_000_000_000,
        3_000_000,
        mine=(4, 5, 6),
    )
    (pair_kv,) = call(join_body, [sds((2 * BLK, FD), BF16)], (own, recv), 0, 800_000)
    pair_kv, proj_other = lax.optimization_barrier((pair_kv, proj_other))
    shifted = lax.ppermute(pair_kv, "x", [(i, i + 1) for i in range(3)])
    w1, w2 = [lax.ppermute(pair_kv, ("x", "y"), [(i, i + o) for i in range(PAIRS - o)]) for o in (1, 2)]
    even, outgoing = call(
        second_body,
        [mats, sds((PAIRS, CROWS, 128), BF16)],
        (recv, gate, up, down, step, own, upd),
        6_000_000_000,
        4_000_000,
        scratch=[flat],
        mine=(1, 2, 3),
    )
    (behind,) = call(relay_body, [sds((2 * BLK, FD), BF16)], (pair_kv, shifted), 0, 1_000_000)
    outgoing, behind, send_q = lax.optimization_barrier((outgoing, behind, send_q))
    w3 = lax.ppermute(behind, "y", [(i, (i + 3) % 4) for i in range(4)])
    recv_q = lax.ppermute(send_q, "zh", [(0, 1), (1, 0)])
    pieces = lax.all_to_all(outgoing, ("x", "y"), 0, 0, tiled=True)
    acc, stat = call(
        attend_first_body,
        [sds((2, BLK, HD), F32), sds((2, BLK, 128), F32)],
        (own_q, recv_q, pair_kv, shifted, w2),
        30_000_000_000,
        2_000_000,
        600_000,
        scratch=[pltpu.VMEM((2, 5, BLK, BLK), F32)],
    )
    pieces, acc = lax.optimization_barrier((pieces, acc))
    (sums,) = call(scan_body, [sds((PAIRS, CROWS, 128), BF16)], (pieces,), 500_000, 1_000_000, cap=SMALL)
    prefix = lax.all_to_all(sums, ("x", "y"), 0, 0, tiled=True)
    (att,) = call(
        attend_second_body,
        [sds((2, BLK, HD), F32)],
        (own_q, recv_q, w1, w3, acc, stat, attn_gain.reshape(1, FD)),
        500_000_000,
        2_000_000,
        600_000,
        scratch=[pltpu.VMEM((2, 4, BLK, BLK), F32)],
    )
    (mixed,) = call(
        apply_body,
        [sds((4, 64, FD), BF16)],
        (prefix, even, own, recv, own_q, recv_q, gate, up, down, ttt_gain.reshape(1, FD), att),
        600_000_000,
        5_000_000,
        scratch=[flat],
        mine=(6, 7, 8),
    )
    mixed = lax.all_to_all(mixed, ("c", "zh"), 0, 0, tiled=True)
    (partial,) = call(
        project_body,
        [sds((128, WIDTH), BF16)],
        (mixed, proj, proj_other),
        600_000_000,
        6_000_000,
        cap=VMEM_CAP,
    )
    parts = lax.all_to_all(partial.reshape(4, 32, WIDTH), "zl", 0, 0, tiled=True)
    (result,) = call(total_body, [sds((32, WIDTH), BF16)], (parts,), 400_000, 1_000_000, cap=SMALL)
    return result


def solution(mesh):
    fine = Mesh(mesh.devices.reshape(4, 4, 2, 4, 2), ("x", "y", "zh", "zl", "c"))
    seq = ("x", "y", "zh")
    head = ("zl", "c")
    in_specs = (
        P(seq, head),
        P(seq, head),
        P(seq, head),
        P(seq, head),
        P(seq, head),
        P(head),
        P(head, None, None),
        P(head, None, None),
        P(head, None, None),
        P(head),
        P(head),
        P(head, None),
    )
    out_specs = P(("x", "y", "zh", "zl", "c"), None)
    return jax.shard_map(local, mesh=fine, in_specs=in_specs, out_specs=out_specs, check_vma=False)
```

```python
import functools
import math

import jax
import jax.numpy as jnp
from jax import lax
from jax.experimental import pallas as pl
from jax.experimental.pallas import tpu as pltpu
from jax.sharding import Mesh, PartitionSpec as P

F32 = jnp.float32
BF16 = jnp.bfloat16
HD = 192
FD = 384
BLK = 256
WIDTH = 3072
NS_STEPS = 5
PAIRS = 16
CHUNK = 108
CROWS = 112
PAY = 272
COEF = (3.4445, -4.775, 2.0315)
VMEM_CAP = 60 * 1024 * 1024
SMALL = 12 * 1024 * 1024


class Lazy:
    def __init__(self, copy, ref):
        self.copy, self.ref = copy, ref

    def get(self):
        if self.copy is not None:
            self.copy.wait()
            self.copy = None
        return self.ref


def call(body, outs, ins, flops, nbytes, trans=0, scratch=(), mine=(), cap=VMEM_CAP):
    outs = list(outs)
    n_in, n_out = len(ins), len(outs)
    shapes = [a.shape[1:] if i in mine else a.shape for i, a in enumerate(ins)]

    def kernel(*refs):
        in_refs, out_refs = refs[:n_in], refs[n_in : n_in + n_out]
        rest = refs[n_in + n_out :]
        in_vm, out_vm = rest[:n_in], rest[n_in : n_in + n_out]
        in_sem, out_sem, extra = rest[n_in + n_out], rest[n_in + n_out + 1], rest[n_in + n_out + 2 :]
        zh = lax.axis_index("zh")
        lazy = []
        for i in range(n_in):
            src = in_refs[i].at[zh] if i in mine else in_refs[i]
            copy = pltpu.make_async_copy(src, in_vm[i], in_sem.at[i])
            copy.start()
            lazy.append(Lazy(copy, in_vm[i]))
        copies = [pltpu.make_async_copy(out_vm[i], out_refs[i], out_sem.at[i]) for i in range(n_out)]
        body(*lazy, *out_vm, *extra)
        for copy in copies:
            copy.start()
        for item in lazy:
            item.get()
        for copy in copies:
            copy.wait()

    any_spec = pl.BlockSpec(memory_space=pltpu.MemorySpace.HBM)
    return pl.pallas_call(
        kernel,
        out_shape=outs,
        in_specs=[any_spec] * n_in,
        out_specs=[any_spec] * n_out,
        scratch_shapes=[pltpu.VMEM(sh, a.dtype) for sh, a in zip(shapes, ins)]
        + [pltpu.VMEM(o.shape, o.dtype) for o in outs]
        + [pltpu.SemaphoreType.DMA((n_in,)), pltpu.SemaphoreType.DMA((n_out,))]
        + list(scratch),
        compiler_params=pltpu.CompilerParams(vmem_limit_bytes=cap),
        cost_estimate=pl.CostEstimate(flops=flops, bytes_accessed=nbytes, transcendentals=trans),
    )(*ins)


def nn(a, b):
    return lax.dot_general(a, b, (((1,), (0,)), ((), ())), preferred_element_type=F32)


def nt(a, b):
    return lax.dot_general(a, b, (((1,), (1,)), ((), ())), preferred_element_type=F32)


def split(x):
    hi = x.astype(BF16)
    return hi, (x - hi.astype(F32)).astype(BF16)


def nn3(a, b):
    return nn(a[0], b[0]) + (nn(a[0], b[1]) + nn(a[1], b[0]))


def nt3(a, b):
    return nt(a[0], b[0]) + (nt(a[0], b[1]) + nt(a[1], b[0]))


def three(x):
    hi = x.astype(BF16).astype(F32)
    mid = (x - hi).astype(BF16).astype(F32)
    low = x - hi - mid
    row = lax.broadcasted_iota(jnp.int32, x.shape, 0)
    return jnp.where(row == 0, hi, jnp.where(row == 1, mid, jnp.where(row == 2, low, 0.0)))


def pick(ref, who):
    return jnp.where(who == 0, ref[:, :HD], ref[:, HD:])


def one_of(row, who):
    return jnp.where(who == 0, row[0:1], row[1:2])


def fill(out_ref, k, v, rate_row, decay):
    out_ref[0:BLK, 0:HD] = k
    out_ref[0:BLK, HD:] = v
    row = jnp.concatenate([rate_row, jnp.broadcast_to(decay, (1, 128))], axis=1)
    out_ref[BLK:PAY, :] = three(jnp.broadcast_to(row, (16, FD))).astype(BF16)


def fold_queries(out_ref, q):
    out_ref[:, 0:HD] = q[0:128]
    out_ref[:, HD:] = q[128:256]


def pack_body(k, v, r, d, q, send_ref, query_ref):
    who = 1 - lax.axis_index("zh")
    fill(
        send_ref,
        pick(k.get(), who),
        pick(v.get(), who),
        one_of(r.get()[...], who),
        jnp.where(who == 0, d.get()[:, 0:1], d.get()[:, 1:2]),
    )
    fold_queries(query_ref, pick(q.get(), who))


def tail(pay_ref):
    rows = pay_ref[BLK:PAY, :].astype(F32)
    return rows[0:1] + rows[1:2] + rows[2:3]


def queries(ref):
    both = ref[...]
    return jnp.concatenate([both[:, :HD], both[:, HD:]], axis=0)


def orthogonalize(mats):
    norms = [jnp.sqrt(jnp.sum(m * m, keepdims=True)) + 1e-7 for m in mats]
    mats = [m / n for m, n in zip(mats, norms)]
    for _ in range(NS_STEPS):
        parts = [split(x) for x in mats]
        grams = []
        for hi, lo in parts:
            cross = nt(hi, lo)
            grams.append(nt(hi, hi) + (cross + cross.T))
        polys = []
        for gram in grams:
            hi, lo = split(gram)
            cross = nn(hi, lo)
            polys.append(split(COEF[1] * gram + COEF[2] * (nn(hi, hi) + (cross + cross.T))))
        mats = [COEF[0] * x + nn3(p, s) for x, p, s in zip(mats, polys, parts)]
    return mats


def fast_updates(k, v, rate_row, g, u, dt, step):
    kf = k.astype(F32)
    rk = lax.rsqrt(jnp.mean(kf * kf, axis=1, keepdims=True) + 1e-6)
    rate = jnp.broadcast_to(rate_row, (128, BLK)).T[:, 0:1]
    gh, gl = split(g.get()[...])
    pre_gate = rk * (nn(k, gh) + nn(k, gl))
    uh, ul = split(u.get()[...])
    pre_up = rk * (nn(k, uh) + nn(k, ul))
    dh, dl = split(dt.get()[...])
    back = -rate * (nn(v, dh) + nn(v, dl))
    sig = jax.nn.sigmoid(pre_gate)
    act = pre_gate * sig
    mid_h, mid_l = split(-rate * (act * pre_up))
    gate_h, gate_l = split(rk * (back * pre_up * (sig * (1.0 + pre_gate * (1.0 - sig)))))
    up_h, up_l = split(rk * (back * act))
    kt = k.T
    vt = v.T
    grads = [
        nn(kt, gate_h) + nn(kt, gate_l),
        nn(kt, up_h) + nn(kt, up_l),
        nn(vt, mid_h) + nn(vt, mid_l),
    ]
    row = step.get()[...]
    scale = -jnp.where(lax.axis_index("zh") == 0, row[:, 0:1], row[:, 1:2])
    return [scale * x for x in orthogonalize(grads)]


def first_body(k, v, r, d, g, u, dt, step, q, upd_ref, own_ref, query_ref):
    zh = lax.axis_index("zh")
    key = pick(k.get(), zh)
    value = pick(v.get(), zh)
    rate_row = one_of(r.get()[...], zh)
    fill(own_ref, key, value, rate_row, jnp.where(zh == 0, d.get()[:, 0:1], d.get()[:, 1:2]))
    for i, x in enumerate(fast_updates(key, value, rate_row, g, u, dt, step)):
        upd_ref[i] = x
    fold_queries(query_ref, pick(q.get(), zh))


def join_body(own, recv, out_ref):
    out_ref[0:BLK] = own.get()[0:BLK]
    out_ref[BLK:] = recv.get()[0:BLK]


def second_body(pay, g, u, dt, step, own, upd, even_ref, send_ref, flat_ref):
    pay_ref = pay.get()
    others = fast_updates(
        pay_ref[0:BLK, 0:HD], pay_ref[0:BLK, HD:], tail(pay_ref)[:, :BLK], g, u, dt, step
    )
    zh = lax.axis_index("zh")
    upd_ref = upd.get()
    mine = tail(own.get())[:, BLK:]
    theirs = tail(pay_ref)[:, BLK:]
    keep_even = jnp.where(zh == 0, mine, theirs)
    keep_odd = jnp.where(zh == 0, theirs, mine)
    flat_ref[PAIRS * CHUNK :, :] = jnp.zeros((64, 128), F32)
    for i in range(3):
        other = others[i]
        own_upd = upd_ref[i]
        even = jnp.where(zh == 0, own_upd, other)
        odd = jnp.where(zh == 0, other, own_upd)
        even_ref[i] = even
        for j in range(3):
            cols = slice(j * 128, (j + 1) * 128)
            flat_ref[(3 * i + j) * HD : (3 * i + j + 1) * HD, :] = keep_odd * even[:, cols] + odd[:, cols]
    keep = three(jnp.broadcast_to(keep_even * keep_odd, (16, 128)))[0:4]
    for c in range(PAIRS):
        send_ref[c] = jnp.concatenate([flat_ref[c * CHUNK : (c + 1) * CHUNK, :], keep], axis=0).astype(BF16)


def scan_body(pieces, out_ref):
    in_ref = pieces.get()
    run = jnp.zeros((CROWS, 128), F32)
    for j in range(PAIRS):
        out_ref[j] = run.astype(BF16)
        if j < PAIRS - 1:
            here = in_ref[j].astype(F32)
            keep = here[CHUNK : CHUNK + 1] + here[CHUNK + 1 : CHUNK + 2] + here[CHUNK + 2 : CHUNK + 3]
            run = keep * run + here


def scores_of(q, keys, blocks, score_ref, rows_of, pair):
    row = lax.broadcasted_iota(jnp.int32, (BLK, BLK), 0)
    col = lax.broadcasted_iota(jnp.int32, (BLK, BLK), 1)
    top = None
    for n, (o, e, kind) in enumerate(blocks):
        s = nt(q, keys[o][rows_of(e), 0:HD]) * (1.0 / math.sqrt(HD))
        if kind == "oldest":
            s = jnp.where(col > row, s, -1e30)
        if kind == "newest":
            s = jnp.where(col <= row, s, -1e30)
        if o > 0:
            s = s + jnp.where(pair >= o, 0.0, -1e30)
        score_ref[n] = s
        top = s if top is None else jnp.maximum(top, s)
    return jnp.max(top, axis=1, keepdims=True)


def weighted(values, blocks, score_ref, rows_of, top):
    total = None
    acc = None
    for n, (o, e, _) in enumerate(blocks):
        w = jnp.exp(score_ref[n] - top)
        total = w if total is None else total + w
        part = nn(w.astype(BF16), values[o][rows_of(e), HD:])
        acc = part if acc is None else acc + part
    return jnp.sum(total, axis=1, keepdims=True), acc


def window_blocks(parity, offsets):
    blocks = [(o, e) for o in (4, 3, 2, 1, 0) for e in (0, 1)][parity : parity + 9]
    kinds = ["oldest"] + ["inner"] * 7 + ["newest"]
    return [(o, e, kind) for (o, e), kind in zip(blocks, kinds) if o in offsets]


def ordered_rows(zh):
    def rows_of(parity):
        slot = zh if parity == 0 else 1 - zh
        return pl.ds(pl.multiple_of(slot * BLK, BLK), BLK)

    return rows_of


def pair_index():
    return lax.axis_index("x") * 4 + lax.axis_index("y")


def attend_first_body(own, recv, pair_kv, shifted, w2, acc_ref, stat_ref, score_ref):
    zh = lax.axis_index("zh")
    q_own = queries(own.get())
    q_recv = queries(recv.get())
    wins = {0: pair_kv.get(), 4: shifted.get(), 2: w2.get()}
    rows_of = ordered_rows(zh)
    lane = lax.broadcasted_iota(jnp.int32, (BLK, 128), 1)
    for parity in range(2):
        q = jnp.where(zh == parity, q_own, q_recv)
        blocks = window_blocks(parity, wins)
        scores = score_ref.at[parity]
        top = scores_of(q, wins, blocks, scores, rows_of, pair_index())
        total, acc = weighted(wins, blocks, scores, rows_of, top)
        acc_ref[parity] = acc
        stat_ref[parity] = jnp.where(lane < 64, top, total)


def attend_second_body(own, recv, w1, w3, acc_in, stat, gain_in, out_ref, score_ref):
    zh = lax.axis_index("zh")
    q_own = queries(own.get())
    q_recv = queries(recv.get())
    wins = {1: w1.get(), 3: w3.get()}
    gain = head_gain(gain_in, zh)
    rows_of = ordered_rows(zh)
    stats = stat.get()
    before = acc_in.get()
    for parity in range(2):
        q = jnp.where(zh == parity, q_own, q_recv)
        blocks = window_blocks(parity, wins)
        scores = score_ref.at[parity]
        old_top = stats[parity, :, 0:1]
        top = jnp.maximum(old_top, scores_of(q, wins, blocks, scores, rows_of, pair_index()))
        total, acc = weighted(wins, blocks, scores, rows_of, top)
        rescale = jnp.exp(old_top - top)
        total = total + rescale * stats[parity, :, 64:65]
        att = (acc + rescale * before[parity]) / total
        norm = lax.rsqrt(jnp.mean(att * att, axis=1, keepdims=True) + 1e-6)
        out_ref[parity] = att * norm * gain


def apply_body(pre, even, own, recv, q_mine, q_theirs, g, u, dt, gain_in, att, out_ref, flat_ref):
    zh = lax.axis_index("zh")
    pre_ref, even_ref, own_ref, recv_ref, att_ref = [x.get() for x in (pre, even, own, recv, att)]
    for c in range(PAIRS):
        flat_ref[c * CHUNK : (c + 1) * CHUNK, :] = pre_ref[c].astype(F32)[0:CHUNK]
    keep = jnp.where(zh == 0, tail(own_ref)[:, BLK : BLK + 1], tail(recv_ref)[:, BLK : BLK + 1])
    gain = head_gain(gain_in, zh)
    q_own = queries(q_mine.get())
    q_recv = queries(q_theirs.get())
    base = [x.get()[...] for x in (g, u, dt)]
    for parity in range(2):
        q = jnp.where(zh == parity, q_own, q_recv)
        qf = q.astype(F32)
        rq = lax.rsqrt(jnp.mean(qf * qf, axis=1, keepdims=True) + 1e-6)
        mats = []
        for i in range(3):
            state = jnp.concatenate(
                [flat_ref[(3 * i + j) * HD : (3 * i + j + 1) * HD, :] for j in range(3)], axis=1
            )
            if parity == 1:
                state = keep * state + even_ref[i]
            mats.append(split(base[i] + state))
        gate = rq * (nn(q, mats[0][0]) + nn(q, mats[0][1]))
        up = rq * (nn(q, mats[1][0]) + nn(q, mats[1][1]))
        applied = nt3(split(gate * jax.nn.sigmoid(gate) * up), mats[2])
        norm = lax.rsqrt(jnp.mean(applied * applied, axis=1, keepdims=True) + 1e-6)
        mixed = (applied * norm * gain + att_ref[parity]).astype(BF16)
        for c in range(2):
            for z in range(4):
                out_ref[c * 2 + parity, (z % 2) * 32 : (z % 2) * 32 + 32, (z // 2) * HD : (z // 2 + 1) * HD] = mixed[
                    z * 64 + c * 32 : z * 64 + c * 32 + 32
                ]


def project_body(mix, own, other, out_ref):
    core = lax.axis_index("c")
    mix_ref = mix.get()
    total = None
    for w, which in ((own, core), (other, 1 - core)):
        w_ref = w.get()
        for zh in range(2):
            part = mix_ref[which * 2 + zh]
            part = jnp.concatenate([part[:, :HD], part[:, HD:]], axis=0)
            part = nn(part, w_ref[zh * HD : (zh + 1) * HD, :])
            total = part if total is None else total + part
    out_ref[...] = total.astype(BF16)


def total_body(parts, out_ref):
    ref = parts.get()
    out_ref[...] = sum(ref[i].astype(F32) for i in range(4)).astype(BF16)


def behind(pair_kv, distance):
    return lax.ppermute(pair_kv, ("x", "y"), [(i, i + distance) for i in range(PAIRS - distance)])


def head_gain(gain, zh):
    rows = gain.get()[...]
    first = jnp.concatenate([rows[0:1], rows[1:2, :64]], axis=1)
    second = jnp.concatenate([rows[1:2, 64:], rows[2:3]], axis=1)
    return jnp.where(zh == 0, first, second)


def local(q, k, v, rates, decay, step, gate, up, down, ttt_gain, attn_gain, proj):
    sds = jax.ShapeDtypeStruct
    pay = sds((PAY, FD), BF16)
    rates = rates.T
    down = jnp.swapaxes(down, 1, 2)
    step = step.reshape(1, 2)
    folded = sds((128, FD), BF16)
    send, send_q = call(pack_body, [pay, folded], (k, v, rates, decay, q), 0, 1_000_000)
    recv = lax.ppermute(send, "zh", [(0, 1), (1, 0)])
    proj_other = lax.ppermute(proj, "c", [(0, 1), (1, 0)])
    mats = sds((3, HD, FD), F32)
    flat = pltpu.VMEM((PAIRS * CHUNK + 64, 128), F32)
    upd, own, own_q = call(
        first_body,
        [mats, pay, folded],
        (k, v, rates, decay, gate, up, down, step, q),
        6_000_000_000,
        3_000_000,
        mine=(4, 5, 6),
    )
    (pair_kv,) = call(join_body, [sds((2 * BLK, FD), BF16)], (own, recv), 0, 800_000)
    pair_kv, proj_other = lax.optimization_barrier((pair_kv, proj_other))
    shifted = lax.ppermute(pair_kv, "x", [(i, i + 1) for i in range(3)])
    w2 = behind(pair_kv, 2)
    even, outgoing = call(
        second_body,
        [mats, sds((PAIRS, CROWS, 128), BF16)],
        (recv, gate, up, down, step, own, upd),
        6_000_000_000,
        4_000_000,
        scratch=[flat],
        mine=(1, 2, 3),
    )
    even, later_kv, send_q = lax.optimization_barrier((even, pair_kv, send_q))
    w1 = behind(later_kv, 1)
    w3 = behind(later_kv, 3)
    recv_q = lax.ppermute(send_q, "zh", [(0, 1), (1, 0)])
    pieces = lax.all_to_all(outgoing, ("x", "y"), 0, 0, tiled=True)
    acc, stat = call(
        attend_first_body,
        [sds((2, BLK, HD), F32), sds((2, BLK, 128), F32)],
        (own_q, recv_q, pair_kv, shifted, w2),
        500_000_000,
        2_000_000,
        600_000,
        scratch=[pltpu.VMEM((2, 5, BLK, BLK), F32)],
    )
    pieces, acc = lax.optimization_barrier((pieces, acc))
    (sums,) = call(scan_body, [sds((PAIRS, CROWS, 128), BF16)], (pieces,), 500_000, 1_000_000, cap=SMALL)
    prefix = lax.all_to_all(sums, ("x", "y"), 0, 0, tiled=True)
    (att,) = call(
        attend_second_body,
        [sds((2, BLK, HD), F32)],
        (own_q, recv_q, w1, w3, acc, stat, attn_gain.reshape(3, 128)),
        500_000_000,
        2_000_000,
        600_000,
        scratch=[pltpu.VMEM((2, 4, BLK, BLK), F32)],
    )
    (mixed,) = call(
        apply_body,
        [sds((4, 64, FD), BF16)],
        (prefix, even, own, recv, own_q, recv_q, gate, up, down, ttt_gain.reshape(3, 128), att),
        600_000_000,
        5_000_000,
        scratch=[flat],
        mine=(6, 7, 8),
    )
    mixed = lax.all_to_all(mixed, ("c", "zh"), 0, 0, tiled=True)
    (partial,) = call(
        project_body,
        [sds((128, WIDTH), BF16)],
        (mixed, proj, proj_other),
        600_000_000,
        6_000_000,
        cap=VMEM_CAP,
    )
    parts = lax.all_to_all(partial.reshape(4, 32, WIDTH), "zl", 0, 0, tiled=True)
    (result,) = call(total_body, [sds((32, WIDTH), BF16)], (parts,), 400_000, 1_000_000, cap=SMALL)
    return result


def solution(mesh):
    fine = Mesh(mesh.devices.reshape(4, 4, 2, 4, 2), ("x", "y", "zh", "zl", "c"))
    seq = ("x", "y", "zh")
    head = ("zl", "c")
    in_specs = (
        P(seq, head),
        P(seq, head),
        P(seq, head),
        P(seq, head),
        P(seq, head),
        P(head),
        P(head, None, None),
        P(head, None, None),
        P(head, None, None),
        P(head),
        P(head),
        P(head, None),
    )
    out_specs = P(("x", "y", "zh", "zl", "c"), None)
    return jax.shard_map(local, mesh=fine, in_specs=in_specs, out_specs=out_specs, check_vma=False)
```

```python
import functools
import math

import jax
import jax.numpy as jnp
from jax import lax
from jax.experimental import pallas as pl
from jax.experimental.pallas import tpu as pltpu
from jax.sharding import Mesh, PartitionSpec as P

F32 = jnp.float32
BF16 = jnp.bfloat16
HD = 192
FD = 384
BLK = 256
WIDTH = 3072
NS_STEPS = 5
PAIRS = 16
CHUNK = 108
CROWS = 112
PAY = 272
COEF = (3.4445, -4.775, 2.0315)
VMEM_CAP = 60 * 1024 * 1024
SMALL = 12 * 1024 * 1024


class Lazy:
    def __init__(self, copy, ref):
        self.copy, self.ref = copy, ref

    def get(self):
        if self.copy is not None:
            self.copy.wait()
            self.copy = None
        return self.ref


def call(body, outs, ins, flops, nbytes, trans=0, scratch=(), mine=(), cap=VMEM_CAP, part=None):
    part = part or {}
    outs = list(outs)
    n_in, n_out = len(ins), len(outs)
    shapes = [a.shape[1:] if i in mine or i in part else a.shape for i, a in enumerate(ins)]

    def kernel(*refs):
        in_refs, out_refs = refs[:n_in], refs[n_in : n_in + n_out]
        rest = refs[n_in + n_out :]
        in_vm, out_vm = rest[:n_in], rest[n_in : n_in + n_out]
        in_sem, out_sem, extra = rest[n_in + n_out], rest[n_in + n_out + 1], rest[n_in + n_out + 2 :]
        zh = lax.axis_index("zh")
        lazy = []
        for i in range(n_in):
            src = in_refs[i]
            if i in mine or i in part:
                src = src.at[part.get(i, zh)]
            copy = pltpu.make_async_copy(src, in_vm[i], in_sem.at[i])
            copy.start()
            lazy.append(Lazy(copy, in_vm[i]))
        copies = [pltpu.make_async_copy(out_vm[i], out_refs[i], out_sem.at[i]) for i in range(n_out)]
        body(*lazy, *out_vm, *extra)
        for copy in copies:
            copy.start()
        for item in lazy:
            item.get()
        for copy in copies:
            copy.wait()

    any_spec = pl.BlockSpec(memory_space=pltpu.MemorySpace.HBM)
    return pl.pallas_call(
        kernel,
        out_shape=outs,
        in_specs=[any_spec] * n_in,
        out_specs=[any_spec] * n_out,
        scratch_shapes=[pltpu.VMEM(sh, a.dtype) for sh, a in zip(shapes, ins)]
        + [pltpu.VMEM(o.shape, o.dtype) for o in outs]
        + [pltpu.SemaphoreType.DMA((n_in,)), pltpu.SemaphoreType.DMA((n_out,))]
        + list(scratch),
        compiler_params=pltpu.CompilerParams(vmem_limit_bytes=cap),
        cost_estimate=pl.CostEstimate(flops=flops, bytes_accessed=nbytes, transcendentals=trans),
    )(*ins)


def nn(a, b):
    return lax.dot_general(a, b, (((1,), (0,)), ((), ())), preferred_element_type=F32)


def nt(a, b):
    return lax.dot_general(a, b, (((1,), (1,)), ((), ())), preferred_element_type=F32)


def split(x):
    hi = x.astype(BF16)
    return hi, (x - hi.astype(F32)).astype(BF16)


def nn3(a, b):
    return nn(a[0], b[0]) + (nn(a[0], b[1]) + nn(a[1], b[0]))


def nt3(a, b):
    return nt(a[0], b[0]) + (nt(a[0], b[1]) + nt(a[1], b[0]))


def three(x):
    hi = x.astype(BF16).astype(F32)
    mid = (x - hi).astype(BF16).astype(F32)
    low = x - hi - mid
    row = lax.broadcasted_iota(jnp.int32, x.shape, 0)
    return jnp.where(row == 0, hi, jnp.where(row == 1, mid, jnp.where(row == 2, low, 0.0)))


def pick(ref, who):
    return jnp.where(who == 0, ref[:, :HD], ref[:, HD:])


def one_of(row, who):
    return jnp.where(who == 0, row[0:1], row[1:2])


def fill(out_ref, k, v, rate_row, decay):
    out_ref[0:BLK, 0:HD] = k
    out_ref[0:BLK, HD:] = v
    row = jnp.concatenate([rate_row, jnp.broadcast_to(decay, (1, 128))], axis=1)
    out_ref[BLK:PAY, :] = three(jnp.broadcast_to(row, (16, FD))).astype(BF16)


def fold_queries(out_ref, q):
    out_ref[:, 0:HD] = q[0:128]
    out_ref[:, HD:] = q[128:256]


def pack_body(k, v, r, d, send_ref):
    who = 1 - lax.axis_index("zh")
    fill(
        send_ref,
        pick(k.get(), who),
        pick(v.get(), who),
        one_of(r.get()[...], who),
        jnp.where(who == 0, d.get()[:, 0:1], d.get()[:, 1:2]),
    )


def tail(pay_ref):
    rows = pay_ref[BLK:PAY, :].astype(F32)
    return rows[0:1] + rows[1:2] + rows[2:3]


def queries(ref):
    both = ref[...]
    return jnp.concatenate([both[:, :HD], both[:, HD:]], axis=0)


def orthogonalize(mats):
    norms = [jnp.sqrt(jnp.sum(m * m, keepdims=True)) + 1e-7 for m in mats]
    mats = [m / n for m, n in zip(mats, norms)]
    for _ in range(NS_STEPS):
        parts = [split(x) for x in mats]
        grams = []
        for hi, lo in parts:
            cross = nt(hi, lo)
            grams.append(nt(hi, hi) + (cross + cross.T))
        polys = []
        for gram in grams:
            hi, lo = split(gram)
            cross = nn(hi, lo)
            polys.append(split(COEF[1] * gram + COEF[2] * (nn(hi, hi) + (cross + cross.T))))
        mats = [COEF[0] * x + nn3(p, s) for x, p, s in zip(mats, polys, parts)]
    return mats


def fast_updates(k, v, rate_row, g, u, dt, step):
    kf = k.astype(F32)
    rk = lax.rsqrt(jnp.mean(kf * kf, axis=1, keepdims=True) + 1e-6)
    rate = jnp.broadcast_to(rate_row, (128, BLK)).T[:, 0:1]
    gh, gl = split(g.get()[...])
    pre_gate = rk * (nn(k, gh) + nn(k, gl))
    uh, ul = split(u.get()[...])
    pre_up = rk * (nn(k, uh) + nn(k, ul))
    dh, dl = split(dt.get()[...])
    back = -rate * (nn(v, dh) + nn(v, dl))
    sig = jax.nn.sigmoid(pre_gate)
    act = pre_gate * sig
    mid_h, mid_l = split(-rate * (act * pre_up))
    gate_h, gate_l = split(rk * (back * pre_up * (sig * (1.0 + pre_gate * (1.0 - sig)))))
    up_h, up_l = split(rk * (back * act))
    kt = k.T
    vt = v.T
    grads = [
        nn(kt, gate_h) + nn(kt, gate_l),
        nn(kt, up_h) + nn(kt, up_l),
        nn(vt, mid_h) + nn(vt, mid_l),
    ]
    row = step.get()[...]
    scale = -jnp.where(lax.axis_index("zh") == 0, row[:, 0:1], row[:, 1:2])
    return [scale * x for x in orthogonalize(grads)]


def first_body(k, v, r, d, g, u, dt, step, q, upd_ref, own_ref, query_ref, send_ref):
    zh = lax.axis_index("zh")
    key = pick(k.get(), zh)
    value = pick(v.get(), zh)
    rate_row = one_of(r.get()[...], zh)
    fill(own_ref, key, value, rate_row, jnp.where(zh == 0, d.get()[:, 0:1], d.get()[:, 1:2]))
    for i, x in enumerate(fast_updates(key, value, rate_row, g, u, dt, step)):
        upd_ref[i] = x
    fold_queries(query_ref, pick(q.get(), zh))
    fold_queries(send_ref, pick(q.get(), 1 - zh))


def join_body(own, recv, out_ref):
    out_ref[0:BLK] = own.get()[0:BLK]
    out_ref[BLK:] = recv.get()[0:BLK]


def second_body(pay, g, u, dt, step, own, upd, even_ref, send_ref, flat_ref):
    pay_ref = pay.get()
    others = fast_updates(
        pay_ref[0:BLK, 0:HD], pay_ref[0:BLK, HD:], tail(pay_ref)[:, :BLK], g, u, dt, step
    )
    zh = lax.axis_index("zh")
    upd_ref = upd.get()
    mine = tail(own.get())[:, BLK:]
    theirs = tail(pay_ref)[:, BLK:]
    keep_even = jnp.where(zh == 0, mine, theirs)
    keep_odd = jnp.where(zh == 0, theirs, mine)
    flat_ref[PAIRS * CHUNK :, :] = jnp.zeros((64, 128), F32)
    for i in range(3):
        other = others[i]
        own_upd = upd_ref[i]
        even = jnp.where(zh == 0, own_upd, other)
        odd = jnp.where(zh == 0, other, own_upd)
        even_ref[i] = even
        for j in range(3):
            cols = slice(j * 128, (j + 1) * 128)
            flat_ref[(3 * i + j) * HD : (3 * i + j + 1) * HD, :] = keep_odd * even[:, cols] + odd[:, cols]
    keep = three(jnp.broadcast_to(keep_even * keep_odd, (16, 128)))[0:4]
    for c in range(PAIRS):
        send_ref[c] = jnp.concatenate([flat_ref[c * CHUNK : (c + 1) * CHUNK, :], keep], axis=0).astype(BF16)


def scan_body(pieces, out_ref):
    in_ref = pieces.get()
    run = jnp.zeros((CROWS, 128), F32)
    for j in range(PAIRS):
        out_ref[j] = run.astype(BF16)
        if j < PAIRS - 1:
            here = in_ref[j].astype(F32)
            keep = here[CHUNK : CHUNK + 1] + here[CHUNK + 1 : CHUNK + 2] + here[CHUNK + 2 : CHUNK + 3]
            run = keep * run + here


def scores_of(q, keys, blocks, score_ref, rows_of, pair):
    row = lax.broadcasted_iota(jnp.int32, (BLK, BLK), 0)
    col = lax.broadcasted_iota(jnp.int32, (BLK, BLK), 1)
    top = None
    for n, (o, e, kind) in enumerate(blocks):
        s = nt(q, keys[o][rows_of(e), 0:HD]) * (1.0 / math.sqrt(HD))
        if kind == "oldest":
            s = jnp.where(col > row, s, -1e30)
        if kind == "newest":
            s = jnp.where(col <= row, s, -1e30)
        if o > 0:
            s = s + jnp.where(pair >= o, 0.0, -1e30)
        score_ref[n] = s
        top = s if top is None else jnp.maximum(top, s)
    return jnp.max(top, axis=1, keepdims=True)


def weighted(values, blocks, score_ref, rows_of, top):
    total = None
    acc = None
    for n, (o, e, _) in enumerate(blocks):
        w = jnp.exp(score_ref[n] - top)
        total = w if total is None else total + w
        part = nn(w.astype(BF16), values[o][rows_of(e), HD:])
        acc = part if acc is None else acc + part
    return jnp.sum(total, axis=1, keepdims=True), acc


def window_blocks(parity, offsets):
    blocks = [(o, e) for o in (4, 3, 2, 1, 0) for e in (0, 1)][parity : parity + 9]
    kinds = ["oldest"] + ["inner"] * 7 + ["newest"]
    return [(o, e, kind) for (o, e), kind in zip(blocks, kinds) if o in offsets]


def ordered_rows(zh):
    def rows_of(parity):
        slot = zh if parity == 0 else 1 - zh
        return pl.ds(pl.multiple_of(slot * BLK, BLK), BLK)

    return rows_of


def pair_index():
    return lax.axis_index("x") * 4 + lax.axis_index("y")


def attend_first_body(own, recv, pair_kv, shifted, w1, acc_ref, stat_ref, score_ref):
    zh = lax.axis_index("zh")
    q_own = queries(own.get())
    q_recv = queries(recv.get())
    wins = {0: pair_kv.get(), 4: shifted.get(), 1: w1.get()}
    rows_of = ordered_rows(zh)
    lane = lax.broadcasted_iota(jnp.int32, (BLK, 128), 1)
    for parity in range(2):
        q = jnp.where(zh == parity, q_own, q_recv)
        blocks = window_blocks(parity, wins)
        scores = score_ref.at[parity]
        top = scores_of(q, wins, blocks, scores, rows_of, pair_index())
        total, acc = weighted(wins, blocks, scores, rows_of, top)
        acc_ref[parity] = acc
        stat_ref[parity] = jnp.where(lane < 64, top, total)


def attend_second_body(own, recv, w2, w3, acc_in, stat, gain_in, out_ref, score_ref):
    zh = lax.axis_index("zh")
    q_own = queries(own.get())
    q_recv = queries(recv.get())
    wins = {2: w2.get(), 3: w3.get()}
    gain = head_gain(gain_in, zh)
    rows_of = ordered_rows(zh)
    stats = stat.get()
    before = acc_in.get()
    for parity in range(2):
        q = jnp.where(zh == parity, q_own, q_recv)
        blocks = window_blocks(parity, wins)
        scores = score_ref.at[parity]
        old_top = stats[parity, :, 0:1]
        top = jnp.maximum(old_top, scores_of(q, wins, blocks, scores, rows_of, pair_index()))
        total, acc = weighted(wins, blocks, scores, rows_of, top)
        rescale = jnp.exp(old_top - top)
        total = total + rescale * stats[parity, :, 64:65]
        att = (acc + rescale * before[parity]) / total
        norm = lax.rsqrt(jnp.mean(att * att, axis=1, keepdims=True) + 1e-6)
        out_ref[parity] = att * norm * gain


def apply_body(pre, even, own, recv, q_mine, q_theirs, g, u, dt, gain_in, att, out_ref, flat_ref):
    zh = lax.axis_index("zh")
    pre_ref, even_ref, own_ref, recv_ref, att_ref = [x.get() for x in (pre, even, own, recv, att)]
    for c in range(PAIRS):
        flat_ref[c * CHUNK : (c + 1) * CHUNK, :] = pre_ref[c].astype(F32)[0:CHUNK]
    keep = jnp.where(zh == 0, tail(own_ref)[:, BLK : BLK + 1], tail(recv_ref)[:, BLK : BLK + 1])
    gain = head_gain(gain_in, zh)
    q_own = queries(q_mine.get())
    q_recv = queries(q_theirs.get())
    base = [x.get()[...] for x in (g, u, dt)]
    for parity in range(2):
        q = jnp.where(zh == parity, q_own, q_recv)
        qf = q.astype(F32)
        rq = lax.rsqrt(jnp.mean(qf * qf, axis=1, keepdims=True) + 1e-6)
        mats = []
        for i in range(3):
            state = jnp.concatenate(
                [flat_ref[(3 * i + j) * HD : (3 * i + j + 1) * HD, :] for j in range(3)], axis=1
            )
            if parity == 1:
                state = keep * state + even_ref[i]
            mats.append(split(base[i] + state))
        gate = rq * (nn(q, mats[0][0]) + nn(q, mats[0][1]))
        up = rq * (nn(q, mats[1][0]) + nn(q, mats[1][1]))
        applied = nt3(split(gate * jax.nn.sigmoid(gate) * up), mats[2])
        norm = lax.rsqrt(jnp.mean(applied * applied, axis=1, keepdims=True) + 1e-6)
        mixed = (applied * norm * gain + att_ref[parity]).astype(BF16)
        for c in range(2):
            for z in range(4):
                out_ref[c * 2 + parity, (z % 2) * 32 : (z % 2) * 32 + 32, (z // 2) * HD : (z // 2 + 1) * HD] = mixed[
                    z * 64 + c * 32 : z * 64 + c * 32 + 32
                ]


def project_body(mix, own_a, own_b, other_a, other_b, out_ref):
    core = lax.axis_index("c")
    mix_ref = mix.get()
    total = None
    for zh, w, which in ((0, own_a, core), (1, own_b, core), (0, other_a, 1 - core), (1, other_b, 1 - core)):
        rows = mix_ref[which * 2 + zh]
        rows = jnp.concatenate([rows[:, :HD], rows[:, HD:]], axis=0)
        rows = nn(rows, w.get()[...])
        total = rows if total is None else total + rows
    out_ref[...] = total.astype(BF16)


def total_body(parts, out_ref):
    ref = parts.get()
    out_ref[...] = sum(ref[i].astype(F32) for i in range(4)).astype(BF16)


def behind(pair_kv, distance):
    return lax.ppermute(pair_kv, ("x", "y"), [(i, i + distance) for i in range(PAIRS - distance)])


def head_gain(gain, zh):
    rows = gain.get()[...]
    first = jnp.concatenate([rows[0:1], rows[1:2, :64]], axis=1)
    second = jnp.concatenate([rows[1:2, 64:], rows[2:3]], axis=1)
    return jnp.where(zh == 0, first, second)


def local(q, k, v, rates, decay, step, gate, up, down, ttt_gain, attn_gain, proj):
    sds = jax.ShapeDtypeStruct
    pay = sds((PAY, FD), BF16)
    rates = rates.T
    down = jnp.swapaxes(down, 1, 2)
    step = step.reshape(1, 2)
    folded = sds((128, FD), BF16)
    (send,) = call(pack_body, [pay], (k, v, rates, decay), 0, 1_000_000)
    recv = lax.ppermute(send, "zh", [(0, 1), (1, 0)])
    proj_other = lax.ppermute(proj, "c", [(0, 1), (1, 0)])
    mats = sds((3, HD, FD), F32)
    flat = pltpu.VMEM((PAIRS * CHUNK + 64, 128), F32)
    upd, own, own_q, send_q = call(
        first_body,
        [mats, pay, folded, folded],
        (k, v, rates, decay, gate, up, down, step, q),
        6_000_000_000,
        3_000_000,
        mine=(4, 5, 6),
    )
    (pair_kv,) = call(join_body, [sds((2 * BLK, FD), BF16)], (own, recv), 0, 800_000)
    pair_kv, proj_other = lax.optimization_barrier((pair_kv, proj_other))
    shifted = lax.ppermute(pair_kv, "x", [(i, i + 1) for i in range(3)])
    w1 = behind(pair_kv, 1)
    even, outgoing = call(
        second_body,
        [mats, sds((PAIRS, CROWS, 128), BF16)],
        (recv, gate, up, down, step, own, upd),
        6_000_000_000,
        4_000_000,
        scratch=[flat],
        mine=(1, 2, 3),
    )
    even, later_kv, later_w1, send_q = lax.optimization_barrier((even, pair_kv, w1, send_q))
    w2 = behind(later_w1, 1)
    w3 = behind(later_kv, 3)
    recv_q = lax.ppermute(send_q, "zh", [(0, 1), (1, 0)])
    pieces = lax.all_to_all(outgoing, ("x", "y"), 0, 0, tiled=True)
    acc, stat = call(
        attend_first_body,
        [sds((2, BLK, HD), F32), sds((2, BLK, 128), F32)],
        (own_q, recv_q, pair_kv, shifted, w1),
        500_000_000,
        2_000_000,
        600_000,
        scratch=[pltpu.VMEM((2, 5, BLK, BLK), F32)],
    )
    pieces, acc = lax.optimization_barrier((pieces, acc))
    (sums,) = call(scan_body, [sds((PAIRS, CROWS, 128), BF16)], (pieces,), 500_000, 1_000_000, cap=SMALL)
    prefix = lax.all_to_all(sums, ("x", "y"), 0, 0, tiled=True)
    (att,) = call(
        attend_second_body,
        [sds((2, BLK, HD), F32)],
        (own_q, recv_q, w2, w3, acc, stat, attn_gain.reshape(3, 128)),
        500_000_000,
        2_000_000,
        600_000,
        scratch=[pltpu.VMEM((2, 4, BLK, BLK), F32)],
    )
    (mixed,) = call(
        apply_body,
        [sds((4, 64, FD), BF16)],
        (prefix, even, own, recv, own_q, recv_q, gate, up, down, ttt_gain.reshape(3, 128), att),
        600_000_000,
        5_000_000,
        scratch=[flat],
        mine=(6, 7, 8),
    )
    mixed = lax.all_to_all(mixed, ("c", "zh"), 0, 0, tiled=True)
    own_w = proj.reshape(2, HD, WIDTH)
    other_w = proj_other.reshape(2, HD, WIDTH)
    (partial,) = call(
        project_body,
        [sds((128, WIDTH), BF16)],
        (mixed, own_w, own_w, other_w, other_w),
        600_000_000,
        6_000_000,
        part={1: 0, 2: 1, 3: 0, 4: 1},
    )
    parts = lax.all_to_all(partial.reshape(4, 32, WIDTH), "zl", 0, 0, tiled=True)
    (result,) = call(total_body, [sds((32, WIDTH), BF16)], (parts,), 400_000, 1_000_000, cap=SMALL)
    return result


def solution(mesh):
    fine = Mesh(mesh.devices.reshape(4, 4, 2, 4, 2), ("x", "y", "zh", "zl", "c"))
    seq = ("x", "y", "zh")
    head = ("zl", "c")
    in_specs = (
        P(seq, head),
        P(seq, head),
        P(seq, head),
        P(seq, head),
        P(seq, head),
        P(head),
        P(head, None, None),
        P(head, None, None),
        P(head, None, None),
        P(head),
        P(head),
        P(head, None),
    )
    out_specs = P(("x", "y", "zh", "zl", "c"), None)
    return jax.shard_map(local, mesh=fine, in_specs=in_specs, out_specs=out_specs, check_vma=False)
```

```python
import functools
import math

import jax
import jax.numpy as jnp
from jax import lax
from jax.experimental import pallas as pl
from jax.experimental.pallas import tpu as pltpu
from jax.sharding import Mesh, PartitionSpec as P

F32 = jnp.float32
BF16 = jnp.bfloat16
HD = 192
FD = 384
BLK = 256
WIDTH = 3072
NS_STEPS = 5
PAIRS = 16
CHUNK = 108
CROWS = 112
PAY = 272
COEF = (3.4445, -4.775, 2.0315)
VMEM_CAP = 60 * 1024 * 1024
SMALL = 12 * 1024 * 1024


class Lazy:
    def __init__(self, copy, ref):
        self.copy, self.ref = copy, ref

    def get(self):
        if self.copy is not None:
            self.copy.wait()
            self.copy = None
        return self.ref


def call(body, outs, ins, flops, nbytes, trans=0, scratch=(), mine=(), cap=VMEM_CAP, part=None, head_rows=None):
    part = part or {}
    head_rows = head_rows or {}
    outs = list(outs)
    n_in, n_out = len(ins), len(outs)
    shapes = [a.shape[1:] if i in mine or i in part else a.shape for i, a in enumerate(ins)]

    def kernel(*refs):
        in_refs, out_refs = refs[:n_in], refs[n_in : n_in + n_out]
        rest = refs[n_in + n_out :]
        in_vm, out_vm = rest[:n_in], rest[n_in : n_in + n_out]
        in_sem, out_sem, extra = rest[n_in + n_out], rest[n_in + n_out + 1], rest[n_in + n_out + 2 :]
        zh = lax.axis_index("zh")
        lazy = []
        for i in range(n_in):
            src = in_refs[i]
            if i in mine or i in part:
                src = src.at[part.get(i, zh)]
            copy = pltpu.make_async_copy(src, in_vm[i], in_sem.at[i])
            copy.start()
            lazy.append(Lazy(copy, in_vm[i]))
        copies = []
        for i in range(n_out):
            dst = out_refs[i].at[0 : head_rows[i]] if i in head_rows else out_refs[i]
            copies.append(pltpu.make_async_copy(out_vm[i], dst, out_sem.at[i]))
        body(*lazy, *out_vm, *extra)
        for copy in copies:
            copy.start()
        for item in lazy:
            item.get()
        for copy in copies:
            copy.wait()

    any_spec = pl.BlockSpec(memory_space=pltpu.MemorySpace.HBM)
    return pl.pallas_call(
        kernel,
        out_shape=outs,
        in_specs=[any_spec] * n_in,
        out_specs=[any_spec] * n_out,
        scratch_shapes=[pltpu.VMEM(sh, a.dtype) for sh, a in zip(shapes, ins)]
        + [pltpu.VMEM((head_rows.get(i, o.shape[0]),) + o.shape[1:], o.dtype) for i, o in enumerate(outs)]
        + [pltpu.SemaphoreType.DMA((n_in,)), pltpu.SemaphoreType.DMA((n_out,))]
        + list(scratch),
        compiler_params=pltpu.CompilerParams(vmem_limit_bytes=cap),
        cost_estimate=pl.CostEstimate(flops=flops, bytes_accessed=nbytes, transcendentals=trans),
    )(*ins)


def nn(a, b):
    return lax.dot_general(a, b, (((1,), (0,)), ((), ())), preferred_element_type=F32)


def nt(a, b):
    return lax.dot_general(a, b, (((1,), (1,)), ((), ())), preferred_element_type=F32)


def split(x):
    hi = x.astype(BF16)
    return hi, (x - hi.astype(F32)).astype(BF16)


def nn3(a, b):
    return nn(a[0], b[0]) + (nn(a[0], b[1]) + nn(a[1], b[0]))


def nt3(a, b):
    return nt(a[0], b[0]) + (nt(a[0], b[1]) + nt(a[1], b[0]))


def three(x):
    hi = x.astype(BF16).astype(F32)
    mid = (x - hi).astype(BF16).astype(F32)
    low = x - hi - mid
    row = lax.broadcasted_iota(jnp.int32, x.shape, 0)
    return jnp.where(row == 0, hi, jnp.where(row == 1, mid, jnp.where(row == 2, low, 0.0)))


def pick(ref, who):
    return jnp.where(who == 0, ref[:, :HD], ref[:, HD:])


def one_of(row, who):
    return jnp.where(who == 0, row[0:1], row[1:2])


def fill(out_ref, k, v, rate_row, decay):
    out_ref[0:BLK, 0:HD] = k
    out_ref[0:BLK, HD:] = v
    row = jnp.concatenate([rate_row, jnp.broadcast_to(decay, (1, 128))], axis=1)
    out_ref[BLK:PAY, :] = three(jnp.broadcast_to(row, (16, FD))).astype(BF16)


def fold_queries(out_ref, q):
    out_ref[:, 0:HD] = q[0:128]
    out_ref[:, HD:] = q[128:256]


def pack_body(k, v, r, d, send_ref):
    who = 1 - lax.axis_index("zh")
    fill(
        send_ref,
        pick(k.get(), who),
        pick(v.get(), who),
        one_of(r.get()[...], who),
        jnp.where(who == 0, d.get()[:, 0:1], d.get()[:, 1:2]),
    )


def tail(pay_ref):
    rows = pay_ref[BLK:PAY, :].astype(F32)
    return rows[0:1] + rows[1:2] + rows[2:3]


def queries(ref):
    both = ref[...]
    return jnp.concatenate([both[:, :HD], both[:, HD:]], axis=0)


def orthogonalize(mats):
    norms = [jnp.sqrt(jnp.sum(m * m, keepdims=True)) + 1e-7 for m in mats]
    mats = [m / n for m, n in zip(mats, norms)]
    for _ in range(NS_STEPS):
        parts = [split(x) for x in mats]
        grams = []
        for hi, lo in parts:
            cross = nt(hi, lo)
            grams.append(nt(hi, hi) + (cross + cross.T))
        polys = []
        for gram in grams:
            hi, lo = split(gram)
            cross = nn(hi, lo)
            polys.append(split(COEF[1] * gram + COEF[2] * (nn(hi, hi) + (cross + cross.T))))
        mats = [COEF[0] * x + nn3(p, s) for x, p, s in zip(mats, polys, parts)]
    return mats


def fast_updates(k, v, rate_row, g, u, dt, step):
    kf = k.astype(F32)
    rk = lax.rsqrt(jnp.mean(kf * kf, axis=1, keepdims=True) + 1e-6)
    rate = jnp.broadcast_to(rate_row, (128, BLK)).T[:, 0:1]
    gh, gl = split(g.get()[...])
    pre_gate = rk * (nn(k, gh) + nn(k, gl))
    uh, ul = split(u.get()[...])
    pre_up = rk * (nn(k, uh) + nn(k, ul))
    dh, dl = split(dt.get()[...])
    back = -rate * (nn(v, dh) + nn(v, dl))
    sig = jax.nn.sigmoid(pre_gate)
    act = pre_gate * sig
    mid_h, mid_l = split(-rate * (act * pre_up))
    gate_h, gate_l = split(rk * (back * pre_up * (sig * (1.0 + pre_gate * (1.0 - sig)))))
    up_h, up_l = split(rk * (back * act))
    kt = k.T
    vt = v.T
    grads = [
        nn(kt, gate_h) + nn(kt, gate_l),
        nn(kt, up_h) + nn(kt, up_l),
        nn(vt, mid_h) + nn(vt, mid_l),
    ]
    row = step.get()[...]
    scale = -jnp.where(lax.axis_index("zh") == 0, row[:, 0:1], row[:, 1:2])
    return [scale * x for x in orthogonalize(grads)]


def first_body(k, v, r, d, g, u, dt, step, q, upd_ref, own_ref, query_ref, send_ref):
    zh = lax.axis_index("zh")
    key = pick(k.get(), zh)
    value = pick(v.get(), zh)
    rate_row = one_of(r.get()[...], zh)
    fill(own_ref, key, value, rate_row, jnp.where(zh == 0, d.get()[:, 0:1], d.get()[:, 1:2]))
    for i, x in enumerate(fast_updates(key, value, rate_row, g, u, dt, step)):
        upd_ref[i] = x
    fold_queries(query_ref, pick(q.get(), zh))
    fold_queries(send_ref, pick(q.get(), 1 - zh))


def second_body(pair_kv, g, u, dt, step, upd, even_ref, send_ref, flat_ref):
    pay_ref = pair_kv.get().at[PAY:]
    others = fast_updates(
        pay_ref[0:BLK, 0:HD], pay_ref[0:BLK, HD:], tail(pay_ref)[:, :BLK], g, u, dt, step
    )
    zh = lax.axis_index("zh")
    upd_ref = upd.get()
    mine = tail(pair_kv.get())[:, BLK:]
    theirs = tail(pay_ref)[:, BLK:]
    keep_even = jnp.where(zh == 0, mine, theirs)
    keep_odd = jnp.where(zh == 0, theirs, mine)
    flat_ref[PAIRS * CHUNK :, :] = jnp.zeros((64, 128), F32)
    for i in range(3):
        other = others[i]
        own_upd = upd_ref[i]
        even = jnp.where(zh == 0, own_upd, other)
        odd = jnp.where(zh == 0, other, own_upd)
        even_ref[i] = even
        for j in range(3):
            cols = slice(j * 128, (j + 1) * 128)
            flat_ref[(3 * i + j) * HD : (3 * i + j + 1) * HD, :] = keep_odd * even[:, cols] + odd[:, cols]
    keep = three(jnp.broadcast_to(keep_even * keep_odd, (16, 128)))[0:4]
    for c in range(PAIRS):
        send_ref[c] = jnp.concatenate([flat_ref[c * CHUNK : (c + 1) * CHUNK, :], keep], axis=0).astype(BF16)


def scan_body(pieces, out_ref):
    in_ref = pieces.get()
    run = jnp.zeros((CROWS, 128), F32)
    for j in range(PAIRS):
        out_ref[j] = run.astype(BF16)
        if j < PAIRS - 1:
            here = in_ref[j].astype(F32)
            keep = here[CHUNK : CHUNK + 1] + here[CHUNK + 1 : CHUNK + 2] + here[CHUNK + 2 : CHUNK + 3]
            run = keep * run + here


def scores_of(q, keys, blocks, score_ref, rows_of, pair):
    row = lax.broadcasted_iota(jnp.int32, (BLK, BLK), 0)
    col = lax.broadcasted_iota(jnp.int32, (BLK, BLK), 1)
    top = None
    for n, (o, e, kind) in enumerate(blocks):
        s = nt(q, keys[o][rows_of(e), 0:HD]) * (1.0 / math.sqrt(HD))
        if kind == "oldest":
            s = jnp.where(col > row, s, -1e30)
        if kind == "newest":
            s = jnp.where(col <= row, s, -1e30)
        if o > 0:
            s = s + jnp.where(pair >= o, 0.0, -1e30)
        score_ref[n] = s
        top = s if top is None else jnp.maximum(top, s)
    return jnp.max(top, axis=1, keepdims=True)


def weighted(values, blocks, score_ref, rows_of, top):
    total = None
    acc = None
    for n, (o, e, _) in enumerate(blocks):
        w = jnp.exp(score_ref[n] - top)
        total = w if total is None else total + w
        part = nn(w.astype(BF16), values[o][rows_of(e), HD:])
        acc = part if acc is None else acc + part
    return jnp.sum(total, axis=1, keepdims=True), acc


def window_blocks(parity, offsets):
    blocks = [(o, e) for o in (4, 3, 2, 1, 0) for e in (0, 1)][parity : parity + 9]
    kinds = ["oldest"] + ["inner"] * 7 + ["newest"]
    return [(o, e, kind) for (o, e), kind in zip(blocks, kinds) if o in offsets]


def ordered_rows(zh):
    def rows_of(parity):
        slot = zh if parity == 0 else 1 - zh
        return pl.ds(pl.multiple_of(slot * PAY, 16), BLK)

    return rows_of


def pair_index():
    return lax.axis_index("x") * 4 + lax.axis_index("y")


def attend_first_body(own, recv, pair_kv, shifted, w1, acc_ref, stat_ref, score_ref):
    zh = lax.axis_index("zh")
    q_own = queries(own.get())
    q_recv = queries(recv.get())
    wins = {0: pair_kv.get(), 4: shifted.get(), 1: w1.get()}
    rows_of = ordered_rows(zh)
    lane = lax.broadcasted_iota(jnp.int32, (BLK, 128), 1)
    for parity in range(2):
        q = jnp.where(zh == parity, q_own, q_recv)
        blocks = window_blocks(parity, wins)
        scores = score_ref.at[parity]
        top = scores_of(q, wins, blocks, scores, rows_of, pair_index())
        total, acc = weighted(wins, blocks, scores, rows_of, top)
        acc_ref[parity] = acc
        stat_ref[parity] = jnp.where(lane < 64, top, total)


def attend_second_body(own, recv, w2, w3, acc_in, stat, gain_in, out_ref, score_ref):
    zh = lax.axis_index("zh")
    q_own = queries(own.get())
    q_recv = queries(recv.get())
    wins = {2: w2.get(), 3: w3.get()}
    gain = head_gain(gain_in, zh)
    rows_of = ordered_rows(zh)
    stats = stat.get()
    before = acc_in.get()
    for parity in range(2):
        q = jnp.where(zh == parity, q_own, q_recv)
        blocks = window_blocks(parity, wins)
        scores = score_ref.at[parity]
        old_top = stats[parity, :, 0:1]
        top = jnp.maximum(old_top, scores_of(q, wins, blocks, scores, rows_of, pair_index()))
        total, acc = weighted(wins, blocks, scores, rows_of, top)
        rescale = jnp.exp(old_top - top)
        total = total + rescale * stats[parity, :, 64:65]
        att = (acc + rescale * before[parity]) / total
        norm = lax.rsqrt(jnp.mean(att * att, axis=1, keepdims=True) + 1e-6)
        out_ref[parity] = att * norm * gain


def apply_body(pre, even, pair_kv, q_mine, q_theirs, g, u, dt, gain_in, att, out_ref, flat_ref):
    zh = lax.axis_index("zh")
    pre_ref, even_ref, own_ref, att_ref = [x.get() for x in (pre, even, pair_kv, att)]
    recv_ref = own_ref.at[PAY:]
    for c in range(PAIRS):
        flat_ref[c * CHUNK : (c + 1) * CHUNK, :] = pre_ref[c].astype(F32)[0:CHUNK]
    keep = jnp.where(zh == 0, tail(own_ref)[:, BLK : BLK + 1], tail(recv_ref)[:, BLK : BLK + 1])
    gain = head_gain(gain_in, zh)
    q_own = queries(q_mine.get())
    q_recv = queries(q_theirs.get())
    base = [x.get()[...] for x in (g, u, dt)]
    for parity in range(2):
        q = jnp.where(zh == parity, q_own, q_recv)
        qf = q.astype(F32)
        rq = lax.rsqrt(jnp.mean(qf * qf, axis=1, keepdims=True) + 1e-6)
        mats = []
        for i in range(3):
            state = jnp.concatenate(
                [flat_ref[(3 * i + j) * HD : (3 * i + j + 1) * HD, :] for j in range(3)], axis=1
            )
            if parity == 1:
                state = keep * state + even_ref[i]
            mats.append(split(base[i] + state))
        gate = rq * (nn(q, mats[0][0]) + nn(q, mats[0][1]))
        up = rq * (nn(q, mats[1][0]) + nn(q, mats[1][1]))
        applied = nt3(split(gate * jax.nn.sigmoid(gate) * up), mats[2])
        norm = lax.rsqrt(jnp.mean(applied * applied, axis=1, keepdims=True) + 1e-6)
        mixed = (applied * norm * gain + att_ref[parity]).astype(BF16)
        for c in range(2):
            for z in range(4):
                out_ref[c * 2 + parity, (z % 2) * 32 : (z % 2) * 32 + 32, (z // 2) * HD : (z // 2 + 1) * HD] = mixed[
                    z * 64 + c * 32 : z * 64 + c * 32 + 32
                ]


def project_body(mix, own_a, own_b, other_a, other_b, out_ref):
    core = lax.axis_index("c")
    mix_ref = mix.get()
    total = None
    for zh, w, which in ((0, own_a, core), (1, own_b, core), (0, other_a, 1 - core), (1, other_b, 1 - core)):
        rows = mix_ref[which * 2 + zh]
        rows = jnp.concatenate([rows[:, :HD], rows[:, HD:]], axis=0)
        rows = nn(rows, w.get()[...])
        total = rows if total is None else total + rows
    out_ref[...] = total.astype(BF16)


def total_body(parts, out_ref):
    ref = parts.get()
    out_ref[...] = sum(ref[i].astype(F32) for i in range(4)).astype(BF16)


def behind(pair_kv, distance):
    return lax.ppermute(pair_kv, ("x", "y"), [(i, i + distance) for i in range(PAIRS - distance)])


def head_gain(gain, zh):
    rows = gain.get()[...]
    first = jnp.concatenate([rows[0:1], rows[1:2, :64]], axis=1)
    second = jnp.concatenate([rows[1:2, 64:], rows[2:3]], axis=1)
    return jnp.where(zh == 0, first, second)


def local(q, k, v, rates, decay, step, gate, up, down, ttt_gain, attn_gain, proj):
    sds = jax.ShapeDtypeStruct
    pay = sds((PAY, FD), BF16)
    rates = rates.T
    down = jnp.swapaxes(down, 1, 2)
    step = step.reshape(1, 2)
    folded = sds((128, FD), BF16)
    (send,) = call(pack_body, [pay], (k, v, rates, decay), 0, 1_000_000)
    recv = lax.ppermute(send, "zh", [(0, 1), (1, 0)])
    proj_other = lax.ppermute(proj, "c", [(0, 1), (1, 0)])
    mats = sds((3, HD, FD), F32)
    flat = pltpu.VMEM((PAIRS * CHUNK + 64, 128), F32)
    upd, own, own_q, send_q = call(
        first_body,
        [mats, sds((2 * PAY, FD), BF16), folded, folded],
        (k, v, rates, decay, gate, up, down, step, q),
        6_000_000_000,
        3_000_000,
        mine=(4, 5, 6),
        head_rows={1: PAY},
    )
    pair_kv = lax.dynamic_update_slice(own, recv, (PAY, 0))
    pair_kv, proj_other = lax.optimization_barrier((pair_kv, proj_other))
    shifted = lax.ppermute(pair_kv, "x", [(i, i + 1) for i in range(3)])
    w1 = behind(pair_kv, 1)
    even, outgoing = call(
        second_body,
        [mats, sds((PAIRS, CROWS, 128), BF16)],
        (pair_kv, gate, up, down, step, upd),
        6_000_000_000,
        4_000_000,
        scratch=[flat],
        mine=(1, 2, 3),
    )
    even, later_kv, later_w1, send_q = lax.optimization_barrier((even, pair_kv, w1, send_q))
    w2 = behind(later_w1, 1)
    w3 = behind(later_kv, 3)
    recv_q = lax.ppermute(send_q, "zh", [(0, 1), (1, 0)])
    outgoing, shifted, w1 = lax.optimization_barrier((outgoing, shifted, w1))
    pieces = lax.all_to_all(outgoing, ("x", "y"), 0, 0, tiled=True)
    pieces, recv_q = lax.optimization_barrier((pieces, recv_q))
    acc, stat = call(
        attend_first_body,
        [sds((2, BLK, HD), F32), sds((2, BLK, 128), F32)],
        (own_q, recv_q, pair_kv, shifted, w1),
        500_000_000,
        2_000_000,
        600_000,
        scratch=[pltpu.VMEM((2, 5, BLK, BLK), F32)],
    )
    (sums,) = call(scan_body, [sds((PAIRS, CROWS, 128), BF16)], (pieces,), 500_000, 1_000_000, cap=SMALL)
    prefix = lax.all_to_all(sums, ("x", "y"), 0, 0, tiled=True)
    (att,) = call(
        attend_second_body,
        [sds((2, BLK, HD), F32)],
        (own_q, recv_q, w2, w3, acc, stat, attn_gain.reshape(3, 128)),
        500_000_000,
        2_000_000,
        600_000,
        scratch=[pltpu.VMEM((2, 4, BLK, BLK), F32)],
    )
    (mixed,) = call(
        apply_body,
        [sds((4, 64, FD), BF16)],
        (prefix, even, pair_kv, own_q, recv_q, gate, up, down, ttt_gain.reshape(3, 128), att),
        600_000_000,
        5_000_000,
        scratch=[flat],
        mine=(5, 6, 7),
    )
    mixed = lax.all_to_all(mixed, ("c", "zh"), 0, 0, tiled=True)
    own_w = proj.reshape(2, HD, WIDTH)
    other_w = proj_other.reshape(2, HD, WIDTH)
    (partial,) = call(
        project_body,
        [sds((128, WIDTH), BF16)],
        (mixed, own_w, own_w, other_w, other_w),
        600_000_000,
        6_000_000,
        part={1: 0, 2: 1, 3: 0, 4: 1},
    )
    parts = lax.all_to_all(partial.reshape(4, 32, WIDTH), "zl", 0, 0, tiled=True)
    (result,) = call(total_body, [sds((32, WIDTH), BF16)], (parts,), 400_000, 1_000_000, cap=SMALL)
    return result


def solution(mesh):
    fine = Mesh(mesh.devices.reshape(4, 4, 2, 4, 2), ("x", "y", "zh", "zl", "c"))
    seq = ("x", "y", "zh")
    head = ("zl", "c")
    in_specs = (
        P(seq, head),
        P(seq, head),
        P(seq, head),
        P(seq, head),
        P(seq, head),
        P(head),
        P(head, None, None),
        P(head, None, None),
        P(head, None, None),
        P(head),
        P(head),
        P(head, None),
    )
    out_specs = P(("x", "y", "zh", "zl", "c"), None)
    return jax.shard_map(local, mesh=fine, in_specs=in_specs, out_specs=out_specs, check_vma=False)
```

```python
import functools
import math

import jax
import jax.numpy as jnp
from jax import lax
from jax.experimental import pallas as pl
from jax.experimental.pallas import tpu as pltpu
from jax.sharding import Mesh, PartitionSpec as P

F32 = jnp.float32
BF16 = jnp.bfloat16
HD = 192
FD = 384
BLK = 256
WIDTH = 3072
NS_STEPS = 5
PAIRS = 16
CHUNK = 108
CROWS = 112
PAY = 272
COEF = (3.4445, -4.775, 2.0315)
VMEM_CAP = 60 * 1024 * 1024
SMALL = 12 * 1024 * 1024


class Lazy:
    def __init__(self, copy, ref):
        self.copy, self.ref = copy, ref

    def get(self):
        if self.copy is not None:
            self.copy.wait()
            self.copy = None
        return self.ref


def call(body, outs, ins, flops, nbytes, trans=0, scratch=(), mine=(), cap=VMEM_CAP, part=None, head_rows=None):
    part = part or {}
    head_rows = head_rows or {}
    outs = list(outs)
    n_in, n_out = len(ins), len(outs)
    shapes = [a.shape[1:] if i in mine or i in part else a.shape for i, a in enumerate(ins)]

    def kernel(*refs):
        in_refs, out_refs = refs[:n_in], refs[n_in : n_in + n_out]
        rest = refs[n_in + n_out :]
        in_vm, out_vm = rest[:n_in], rest[n_in : n_in + n_out]
        in_sem, out_sem, extra = rest[n_in + n_out], rest[n_in + n_out + 1], rest[n_in + n_out + 2 :]
        zh = lax.axis_index("zh")
        lazy = []
        for i in range(n_in):
            src = in_refs[i]
            if i in mine or i in part:
                src = src.at[part.get(i, zh)]
            copy = pltpu.make_async_copy(src, in_vm[i], in_sem.at[i])
            copy.start()
            lazy.append(Lazy(copy, in_vm[i]))
        copies = []
        for i in range(n_out):
            dst = out_refs[i].at[0 : head_rows[i]] if i in head_rows else out_refs[i]
            copies.append(pltpu.make_async_copy(out_vm[i], dst, out_sem.at[i]))
        body(*lazy, *out_vm, *extra)
        for copy in copies:
            copy.start()
        for item in lazy:
            item.get()
        for copy in copies:
            copy.wait()

    any_spec = pl.BlockSpec(memory_space=pltpu.MemorySpace.HBM)
    return pl.pallas_call(
        kernel,
        out_shape=outs,
        in_specs=[any_spec] * n_in,
        out_specs=[any_spec] * n_out,
        scratch_shapes=[pltpu.VMEM(sh, a.dtype) for sh, a in zip(shapes, ins)]
        + [pltpu.VMEM((head_rows.get(i, o.shape[0]),) + o.shape[1:], o.dtype) for i, o in enumerate(outs)]
        + [pltpu.SemaphoreType.DMA((n_in,)), pltpu.SemaphoreType.DMA((n_out,))]
        + list(scratch),
        compiler_params=pltpu.CompilerParams(vmem_limit_bytes=cap),
        cost_estimate=pl.CostEstimate(flops=flops, bytes_accessed=nbytes, transcendentals=trans),
    )(*ins)


def nn(a, b):
    return lax.dot_general(a, b, (((1,), (0,)), ((), ())), preferred_element_type=F32)


def nt(a, b):
    return lax.dot_general(a, b, (((1,), (1,)), ((), ())), preferred_element_type=F32)


def split(x):
    hi = x.astype(BF16)
    return hi, (x - hi.astype(F32)).astype(BF16)


def nn3(a, b):
    return nn(a[0], b[0]) + (nn(a[0], b[1]) + nn(a[1], b[0]))


def nt3(a, b):
    return nt(a[0], b[0]) + (nt(a[0], b[1]) + nt(a[1], b[0]))


def three(x):
    hi = x.astype(BF16).astype(F32)
    mid = (x - hi).astype(BF16).astype(F32)
    low = x - hi - mid
    row = lax.broadcasted_iota(jnp.int32, x.shape, 0)
    return jnp.where(row == 0, hi, jnp.where(row == 1, mid, jnp.where(row == 2, low, 0.0)))


def pick(ref, who):
    return jnp.where(who == 0, ref[:, :HD], ref[:, HD:])


def one_of(row, who):
    return jnp.where(who == 0, row[0:1], row[1:2])


def fill(out_ref, k, v, rate_row, decay):
    out_ref[0:BLK, 0:HD] = k
    out_ref[0:BLK, HD:] = v
    row = jnp.concatenate([rate_row, jnp.broadcast_to(decay, (1, 128))], axis=1)
    out_ref[BLK:PAY, :] = three(jnp.broadcast_to(row, (16, FD))).astype(BF16)


def fold_queries(out_ref, q):
    out_ref[:, 0:HD] = q[0:128]
    out_ref[:, HD:] = q[128:256]


def pack_body(k, v, r, d, send_ref):
    who = 1 - lax.axis_index("zh")
    fill(
        send_ref,
        pick(k.get(), who),
        pick(v.get(), who),
        one_of(r.get()[...], who),
        jnp.where(who == 0, d.get()[:, 0:1], d.get()[:, 1:2]),
    )


def tail(pay_ref):
    rows = pay_ref[BLK:PAY, :].astype(F32)
    return rows[0:1] + rows[1:2] + rows[2:3]


def queries(ref):
    both = ref[...]
    return jnp.concatenate([both[:, :HD], both[:, HD:]], axis=0)


def orthogonalize(mats):
    norms = [jnp.sqrt(jnp.sum(m * m, keepdims=True)) + 1e-7 for m in mats]
    mats = [m / n for m, n in zip(mats, norms)]
    for _ in range(NS_STEPS):
        parts = [split(x) for x in mats]
        grams = []
        for hi, lo in parts:
            cross = nt(hi, lo)
            grams.append(nt(hi, hi) + (cross + cross.T))
        polys = []
        for gram in grams:
            hi, lo = split(gram)
            cross = nn(hi, lo)
            polys.append(split(COEF[1] * gram + COEF[2] * (nn(hi, hi) + (cross + cross.T))))
        mats = [COEF[0] * x + nn3(p, s) for x, p, s in zip(mats, polys, parts)]
    return mats


def fast_updates(k, v, rate_row, g, u, dt, step):
    kf = k.astype(F32)
    rk = lax.rsqrt(jnp.mean(kf * kf, axis=1, keepdims=True) + 1e-6)
    rate = jnp.broadcast_to(rate_row, (128, BLK)).T[:, 0:1]
    gh, gl = split(g.get()[...])
    pre_gate = rk * (nn(k, gh) + nn(k, gl))
    uh, ul = split(u.get()[...])
    pre_up = rk * (nn(k, uh) + nn(k, ul))
    dh, dl = split(dt.get()[...])
    back = -rate * (nn(v, dh) + nn(v, dl))
    sig = jax.nn.sigmoid(pre_gate)
    act = pre_gate * sig
    mid_h, mid_l = split(-rate * (act * pre_up))
    gate_h, gate_l = split(rk * (back * pre_up * (sig * (1.0 + pre_gate * (1.0 - sig)))))
    up_h, up_l = split(rk * (back * act))
    kt = k.T
    vt = v.T
    grads = [
        nn(kt, gate_h) + nn(kt, gate_l),
        nn(kt, up_h) + nn(kt, up_l),
        nn(vt, mid_h) + nn(vt, mid_l),
    ]
    row = step.get()[...]
    scale = -jnp.where(lax.axis_index("zh") == 0, row[:, 0:1], row[:, 1:2])
    return [scale * x for x in orthogonalize(grads)]


def first_body(k, v, r, d, g, u, dt, step, q, upd_ref, own_ref, query_ref, send_ref):
    zh = lax.axis_index("zh")
    key = pick(k.get(), zh)
    value = pick(v.get(), zh)
    rate_row = one_of(r.get()[...], zh)
    fill(own_ref, key, value, rate_row, jnp.where(zh == 0, d.get()[:, 0:1], d.get()[:, 1:2]))
    for i, x in enumerate(fast_updates(key, value, rate_row, g, u, dt, step)):
        upd_ref[i] = x
    fold_queries(query_ref, pick(q.get(), zh))
    fold_queries(send_ref, pick(q.get(), 1 - zh))


def second_body(pair_kv, g, u, dt, step, upd, even_ref, send_ref, flat_ref):
    pay_ref = pair_kv.get().at[PAY:]
    others = fast_updates(
        pay_ref[0:BLK, 0:HD], pay_ref[0:BLK, HD:], tail(pay_ref)[:, :BLK], g, u, dt, step
    )
    zh = lax.axis_index("zh")
    upd_ref = upd.get()
    mine = tail(pair_kv.get())[:, BLK:]
    theirs = tail(pay_ref)[:, BLK:]
    keep_even = jnp.where(zh == 0, mine, theirs)
    keep_odd = jnp.where(zh == 0, theirs, mine)
    flat_ref[PAIRS * CHUNK :, :] = jnp.zeros((64, 128), F32)
    for i in range(3):
        other = others[i]
        own_upd = upd_ref[i]
        even = jnp.where(zh == 0, own_upd, other)
        odd = jnp.where(zh == 0, other, own_upd)
        even_ref[i] = even
        for j in range(3):
            cols = slice(j * 128, (j + 1) * 128)
            flat_ref[(3 * i + j) * HD : (3 * i + j + 1) * HD, :] = keep_odd * even[:, cols] + odd[:, cols]
    keep = three(jnp.broadcast_to(keep_even * keep_odd, (16, 128)))[0:4]
    for c in range(PAIRS):
        send_ref[c] = jnp.concatenate([flat_ref[c * CHUNK : (c + 1) * CHUNK, :], keep], axis=0).astype(BF16)


def scan_body(pieces, out_ref):
    in_ref = pieces.get()
    run = jnp.zeros((CROWS, 128), F32)
    for j in range(PAIRS):
        out_ref[j] = run.astype(BF16)
        if j < PAIRS - 1:
            here = in_ref[j].astype(F32)
            keep = here[CHUNK : CHUNK + 1] + here[CHUNK + 1 : CHUNK + 2] + here[CHUNK + 2 : CHUNK + 3]
            run = keep * run + here


def scores_of(q, keys, blocks, score_ref, rows_of, pair):
    row = lax.broadcasted_iota(jnp.int32, (BLK, BLK), 0)
    col = lax.broadcasted_iota(jnp.int32, (BLK, BLK), 1)
    top = None
    for n, (o, e, kind) in enumerate(blocks):
        s = nt(q, keys[o][rows_of(e), 0:HD]) * (1.0 / math.sqrt(HD))
        if kind == "oldest":
            s = jnp.where(col > row, s, -1e30)
        if kind == "newest":
            s = jnp.where(col <= row, s, -1e30)
        if o > 0:
            s = s + jnp.where(pair >= o, 0.0, -1e30)
        score_ref[n] = s
        top = s if top is None else jnp.maximum(top, s)
    return jnp.max(top, axis=1, keepdims=True)


def weighted(values, blocks, score_ref, rows_of, top):
    total = None
    acc = None
    for n, (o, e, _) in enumerate(blocks):
        w = jnp.exp(score_ref[n] - top)
        total = w if total is None else total + w
        part = nn(w.astype(BF16), values[o][rows_of(e), HD:])
        acc = part if acc is None else acc + part
    return jnp.sum(total, axis=1, keepdims=True), acc


def window_blocks(parity, offsets):
    blocks = [(o, e) for o in (4, 3, 2, 1, 0) for e in (0, 1)][parity : parity + 9]
    kinds = ["oldest"] + ["inner"] * 7 + ["newest"]
    return [(o, e, kind) for (o, e), kind in zip(blocks, kinds) if o in offsets]


def ordered_rows(zh):
    def rows_of(parity):
        slot = zh if parity == 0 else 1 - zh
        return pl.ds(pl.multiple_of(slot * PAY, 16), BLK)

    return rows_of


def pair_index():
    return lax.axis_index("x") * 4 + lax.axis_index("y")


def attend_first_body(own, recv, pair_kv, shifted, w1, acc_ref, stat_ref, score_ref):
    zh = lax.axis_index("zh")
    q_own = queries(own.get())
    q_recv = queries(recv.get())
    wins = {0: pair_kv.get(), 4: shifted.get(), 1: w1.get()}
    rows_of = ordered_rows(zh)
    lane = lax.broadcasted_iota(jnp.int32, (BLK, 128), 1)
    for parity in range(2):
        q = jnp.where(zh == parity, q_own, q_recv)
        blocks = window_blocks(parity, wins)
        scores = score_ref.at[parity]
        top = scores_of(q, wins, blocks, scores, rows_of, pair_index())
        total, acc = weighted(wins, blocks, scores, rows_of, top)
        acc_ref[parity] = acc
        stat_ref[parity] = jnp.where(lane < 64, top, total)


def attend_second_body(own, recv, w2, w3, acc_in, stat, gain_in, out_ref, score_ref):
    zh = lax.axis_index("zh")
    q_own = queries(own.get())
    q_recv = queries(recv.get())
    wins = {2: w2.get(), 3: w3.get()}
    gain = head_gain(gain_in, zh)
    rows_of = ordered_rows(zh)
    stats = stat.get()
    before = acc_in.get()
    for parity in range(2):
        q = jnp.where(zh == parity, q_own, q_recv)
        blocks = window_blocks(parity, wins)
        scores = score_ref.at[parity]
        old_top = stats[parity, :, 0:1]
        top = jnp.maximum(old_top, scores_of(q, wins, blocks, scores, rows_of, pair_index()))
        total, acc = weighted(wins, blocks, scores, rows_of, top)
        rescale = jnp.exp(old_top - top)
        total = total + rescale * stats[parity, :, 64:65]
        att = (acc + rescale * before[parity]) / total
        norm = lax.rsqrt(jnp.mean(att * att, axis=1, keepdims=True) + 1e-6)
        out_ref[parity] = att * norm * gain


def apply_body(pre, even, pair_kv, q_mine, q_theirs, g, u, dt, gain_in, att, out_ref, flat_ref):
    zh = lax.axis_index("zh")
    pre_ref, even_ref, own_ref, att_ref = [x.get() for x in (pre, even, pair_kv, att)]
    recv_ref = own_ref.at[PAY:]
    for c in range(PAIRS):
        flat_ref[c * CHUNK : (c + 1) * CHUNK, :] = pre_ref[c].astype(F32)[0:CHUNK]
    keep = jnp.where(zh == 0, tail(own_ref)[:, BLK : BLK + 1], tail(recv_ref)[:, BLK : BLK + 1])
    gain = head_gain(gain_in, zh)
    q_own = queries(q_mine.get())
    q_recv = queries(q_theirs.get())
    base = [x.get()[...] for x in (g, u, dt)]
    for parity in range(2):
        q = jnp.where(zh == parity, q_own, q_recv)
        qf = q.astype(F32)
        rq = lax.rsqrt(jnp.mean(qf * qf, axis=1, keepdims=True) + 1e-6)
        mats = []
        for i in range(3):
            state = jnp.concatenate(
                [flat_ref[(3 * i + j) * HD : (3 * i + j + 1) * HD, :] for j in range(3)], axis=1
            )
            if parity == 1:
                state = keep * state + even_ref[i]
            mats.append(split(base[i] + state))
        gate = rq * (nn(q, mats[0][0]) + nn(q, mats[0][1]))
        up = rq * (nn(q, mats[1][0]) + nn(q, mats[1][1]))
        applied = nt3(split(gate * jax.nn.sigmoid(gate) * up), mats[2])
        norm = lax.rsqrt(jnp.mean(applied * applied, axis=1, keepdims=True) + 1e-6)
        mixed = (applied * norm * gain + att_ref[parity]).astype(BF16)
        for c in range(2):
            for z in range(4):
                out_ref[c * 2 + parity, (z % 2) * 32 : (z % 2) * 32 + 32, (z // 2) * HD : (z // 2 + 1) * HD] = mixed[
                    z * 64 + c * 32 : z * 64 + c * 32 + 32
                ]


def project_body(mix, own_a, own_b, other_a, other_b, out_ref):
    core = lax.axis_index("c")
    mix_ref = mix.get()
    total = None
    for zh, w, which in ((0, own_a, core), (1, own_b, core), (0, other_a, 1 - core), (1, other_b, 1 - core)):
        rows = mix_ref[which * 2 + zh]
        rows = jnp.concatenate([rows[:, :HD], rows[:, HD:]], axis=0)
        rows = nn(rows, w.get()[...])
        total = rows if total is None else total + rows
    out_ref[...] = total.astype(BF16)


def total_body(parts, out_ref):
    ref = parts.get()
    out_ref[...] = sum(ref[i].astype(F32) for i in range(4)).astype(BF16)


def behind(pair_kv, distance):
    return lax.ppermute(pair_kv, ("x", "y"), [(i, i + distance) for i in range(PAIRS - distance)])


def head_gain(gain, zh):
    rows = gain.get()[...]
    first = jnp.concatenate([rows[0:1], rows[1:2, :64]], axis=1)
    second = jnp.concatenate([rows[1:2, 64:], rows[2:3]], axis=1)
    return jnp.where(zh == 0, first, second)


def local(q, k, v, rates, decay, step, gate, up, down, ttt_gain, attn_gain, proj):
    sds = jax.ShapeDtypeStruct
    pay = sds((PAY, FD), BF16)
    rates = rates.T
    down = jnp.swapaxes(down, 1, 2)
    step = step.reshape(1, 2)
    folded = sds((128, FD), BF16)
    (send,) = call(pack_body, [pay], (k, v, rates, decay), 0, 1_000_000)
    recv = lax.ppermute(send, "zh", [(0, 1), (1, 0)])
    proj_other = lax.ppermute(proj, "c", [(0, 1), (1, 0)])
    mats = sds((3, HD, FD), F32)
    flat = pltpu.VMEM((PAIRS * CHUNK + 64, 128), F32)
    upd, own, own_q, send_q = call(
        first_body,
        [mats, sds((2 * PAY, FD), BF16), folded, folded],
        (k, v, rates, decay, gate, up, down, step, q),
        6_000_000_000,
        3_000_000,
        mine=(4, 5, 6),
        head_rows={1: PAY},
    )
    pair_kv = lax.dynamic_update_slice(own, recv, (PAY, 0))
    pair_kv, proj_other = lax.optimization_barrier((pair_kv, proj_other))
    shifted = lax.ppermute(pair_kv, "x", [(i, i + 1) for i in range(3)])
    w1 = behind(pair_kv, 1)
    even, outgoing = call(
        second_body,
        [mats, sds((PAIRS, CROWS, 128), BF16)],
        (pair_kv, gate, up, down, step, upd),
        6_000_000_000,
        4_000_000,
        scratch=[flat],
        mine=(1, 2, 3),
    )
    even, later_kv, later_w1, send_q = lax.optimization_barrier((even, pair_kv, w1, send_q))
    w2 = behind(later_w1, 1)
    w3 = behind(later_kv, 3)
    recv_q = lax.ppermute(send_q, "zh", [(0, 1), (1, 0)])
    pieces = lax.all_to_all(outgoing, ("x", "y"), 0, 0, tiled=True)
    acc, stat = call(
        attend_first_body,
        [sds((2, BLK, HD), F32), sds((2, BLK, 128), F32)],
        (own_q, recv_q, pair_kv, shifted, w1),
        500_000_000,
        2_000_000,
        600_000,
        scratch=[pltpu.VMEM((2, 5, BLK, BLK), F32)],
    )
    pieces, acc = lax.optimization_barrier((pieces, acc))
    (sums,) = call(scan_body, [sds((PAIRS, CROWS, 128), BF16)], (pieces,), 500_000, 1_000_000, cap=SMALL)
    prefix = lax.all_to_all(sums, ("x", "y"), 0, 0, tiled=True)
    (att,) = call(
        attend_second_body,
        [sds((2, BLK, HD), F32)],
        (own_q, recv_q, w2, w3, acc, stat, attn_gain.reshape(3, 128)),
        500_000_000,
        2_000_000,
        600_000,
        scratch=[pltpu.VMEM((2, 4, BLK, BLK), F32)],
    )
    (mixed,) = call(
        apply_body,
        [sds((4, 64, FD), BF16)],
        (prefix, even, pair_kv, own_q, recv_q, gate, up, down, ttt_gain.reshape(3, 128), att),
        600_000_000,
        5_000_000,
        scratch=[flat],
        mine=(5, 6, 7),
    )
    mixed = lax.all_to_all(mixed, ("c", "zh"), 0, 0, tiled=True)
    own_w = proj.reshape(2, HD, WIDTH)
    other_w = proj_other.reshape(2, HD, WIDTH)
    (partial,) = call(
        project_body,
        [sds((128, WIDTH), BF16)],
        (mixed, own_w, own_w, other_w, other_w),
        600_000_000,
        6_000_000,
        part={1: 0, 2: 1, 3: 0, 4: 1},
    )
    parts = lax.all_to_all(partial.reshape(4, 32, WIDTH), "zl", 0, 0, tiled=True)
    (result,) = call(total_body, [sds((32, WIDTH), BF16)], (parts,), 400_000, 1_000_000, cap=SMALL)
    return result


def solution(mesh):
    fine = Mesh(mesh.devices.reshape(4, 4, 2, 4, 2), ("x", "y", "zh", "zl", "c"))
    seq = ("x", "y", "zh")
    head = ("zl", "c")
    in_specs = (
        P(seq, head),
        P(seq, head),
        P(seq, head),
        P(seq, head),
        P(seq, head),
        P(head),
        P(head, None, None),
        P(head, None, None),
        P(head, None, None),
        P(head),
        P(head),
        P(head, None),
    )
    out_specs = P(("x", "y", "zh", "zl", "c"), None)
    return jax.shard_map(local, mesh=fine, in_specs=in_specs, out_specs=out_specs, check_vma=False)
```

```python
import functools
import math

import jax
import jax.numpy as jnp
from jax import lax
from jax.experimental import pallas as pl
from jax.experimental.pallas import tpu as pltpu
from jax.sharding import Mesh, PartitionSpec as P

F32 = jnp.float32
BF16 = jnp.bfloat16
HD = 192
FD = 384
BLK = 256
WIDTH = 3072
NS_STEPS = 5
PAIRS = 16
CHUNK = 108
CROWS = 112
PAY = 272
COEF = (3.4445, -4.775, 2.0315)
VMEM_CAP = 60 * 1024 * 1024
SMALL = 12 * 1024 * 1024


class Lazy:
    def __init__(self, copy, ref):
        self.copy, self.ref = copy, ref

    def get(self):
        if self.copy is not None:
            self.copy.wait()
            self.copy = None
        return self.ref


def call(body, outs, ins, flops, nbytes, trans=0, scratch=(), mine=(), cap=VMEM_CAP, part=None, head_rows=None):
    part = part or {}
    head_rows = head_rows or {}
    outs = list(outs)
    n_in, n_out = len(ins), len(outs)
    shapes = [a.shape[1:] if i in mine or i in part else a.shape for i, a in enumerate(ins)]

    def kernel(*refs):
        in_refs, out_refs = refs[:n_in], refs[n_in : n_in + n_out]
        rest = refs[n_in + n_out :]
        in_vm, out_vm = rest[:n_in], rest[n_in : n_in + n_out]
        in_sem, out_sem, extra = rest[n_in + n_out], rest[n_in + n_out + 1], rest[n_in + n_out + 2 :]
        zh = lax.axis_index("zh")
        lazy = []
        for i in range(n_in):
            src = in_refs[i]
            if i in mine or i in part:
                src = src.at[part.get(i, zh)]
            copy = pltpu.make_async_copy(src, in_vm[i], in_sem.at[i])
            copy.start()
            lazy.append(Lazy(copy, in_vm[i]))
        copies = []
        for i in range(n_out):
            dst = out_refs[i].at[0 : head_rows[i]] if i in head_rows else out_refs[i]
            copies.append(pltpu.make_async_copy(out_vm[i], dst, out_sem.at[i]))
        body(*lazy, *out_vm, *extra)
        for copy in copies:
            copy.start()
        for item in lazy:
            item.get()
        for copy in copies:
            copy.wait()

    any_spec = pl.BlockSpec(memory_space=pltpu.MemorySpace.HBM)
    return pl.pallas_call(
        kernel,
        out_shape=outs,
        in_specs=[any_spec] * n_in,
        out_specs=[any_spec] * n_out,
        scratch_shapes=[pltpu.VMEM(sh, a.dtype) for sh, a in zip(shapes, ins)]
        + [pltpu.VMEM((head_rows.get(i, o.shape[0]),) + o.shape[1:], o.dtype) for i, o in enumerate(outs)]
        + [pltpu.SemaphoreType.DMA((n_in,)), pltpu.SemaphoreType.DMA((n_out,))]
        + list(scratch),
        compiler_params=pltpu.CompilerParams(vmem_limit_bytes=cap),
        cost_estimate=pl.CostEstimate(flops=flops, bytes_accessed=nbytes, transcendentals=trans),
    )(*ins)


def nn(a, b):
    return lax.dot_general(a, b, (((1,), (0,)), ((), ())), preferred_element_type=F32)


def nt(a, b):
    return lax.dot_general(a, b, (((1,), (1,)), ((), ())), preferred_element_type=F32)


def split(x):
    hi = x.astype(BF16)
    return hi, (x - hi.astype(F32)).astype(BF16)


def nn3(a, b):
    return nn(a[0], b[0]) + (nn(a[0], b[1]) + nn(a[1], b[0]))


def nt3(a, b):
    return nt(a[0], b[0]) + (nt(a[0], b[1]) + nt(a[1], b[0]))


def three(x):
    hi = x.astype(BF16).astype(F32)
    mid = (x - hi).astype(BF16).astype(F32)
    low = x - hi - mid
    row = lax.broadcasted_iota(jnp.int32, x.shape, 0)
    return jnp.where(row == 0, hi, jnp.where(row == 1, mid, jnp.where(row == 2, low, 0.0)))


def pick(ref, who):
    return jnp.where(who == 0, ref[:, :HD], ref[:, HD:])


def one_of(row, who):
    return jnp.where(who == 0, row[0:1], row[1:2])


def fill(out_ref, k, v, rate_row, decay):
    out_ref[0:BLK, 0:HD] = k
    out_ref[0:BLK, HD:] = v
    row = jnp.concatenate([rate_row, jnp.broadcast_to(decay, (1, 128))], axis=1)
    out_ref[BLK:PAY, :] = three(jnp.broadcast_to(row, (16, FD))).astype(BF16)


def fold_queries(out_ref, q):
    out_ref[:, 0:HD] = q[0:128]
    out_ref[:, HD:] = q[128:256]


def pack_body(k, v, r, d, send_ref):
    who = 1 - lax.axis_index("zh")
    fill(
        send_ref,
        pick(k.get(), who),
        pick(v.get(), who),
        one_of(r.get()[...], who),
        jnp.where(who == 0, d.get()[:, 0:1], d.get()[:, 1:2]),
    )


def tail(pay_ref):
    rows = pay_ref[BLK:PAY, :].astype(F32)
    return rows[0:1] + rows[1:2] + rows[2:3]


def queries(ref):
    both = ref[...]
    return jnp.concatenate([both[:, :HD], both[:, HD:]], axis=0)


def orthogonalize(mats):
    norms = [jnp.sqrt(jnp.sum(m * m, keepdims=True)) + 1e-7 for m in mats]
    mats = [m / n for m, n in zip(mats, norms)]
    for _ in range(NS_STEPS):
        parts = [split(x) for x in mats]
        grams = []
        for hi, lo in parts:
            cross = nt(hi, lo)
            grams.append(nt(hi, hi) + (cross + cross.T))
        polys = []
        for gram in grams:
            hi, lo = split(gram)
            cross = nn(hi, lo)
            polys.append(split(COEF[1] * gram + COEF[2] * (nn(hi, hi) + (cross + cross.T))))
        mats = [COEF[0] * x + nn3(p, s) for x, p, s in zip(mats, polys, parts)]
    return mats


def fast_updates(k, v, rate_row, g, u, dt, step):
    kf = k.astype(F32)
    rk = lax.rsqrt(jnp.mean(kf * kf, axis=1, keepdims=True) + 1e-6)
    rate = jnp.broadcast_to(rate_row, (128, BLK)).T[:, 0:1]
    gh, gl = split(g.get()[...])
    pre_gate = rk * (nn(k, gh) + nn(k, gl))
    uh, ul = split(u.get()[...])
    pre_up = rk * (nn(k, uh) + nn(k, ul))
    dh, dl = split(dt.get()[...])
    back = -rate * (nn(v, dh) + nn(v, dl))
    sig = jax.nn.sigmoid(pre_gate)
    act = pre_gate * sig
    mid_h, mid_l = split(-rate * (act * pre_up))
    gate_h, gate_l = split(rk * (back * pre_up * (sig * (1.0 + pre_gate * (1.0 - sig)))))
    up_h, up_l = split(rk * (back * act))
    kt = k.T
    vt = v.T
    grads = [
        nn(kt, gate_h) + nn(kt, gate_l),
        nn(kt, up_h) + nn(kt, up_l),
        nn(vt, mid_h) + nn(vt, mid_l),
    ]
    row = step.get()[...]
    scale = -jnp.where(lax.axis_index("zh") == 0, row[:, 0:1], row[:, 1:2])
    return [scale * x for x in orthogonalize(grads)]


def first_body(k, v, r, d, g, u, dt, step, q, upd_ref, own_ref, query_ref, send_ref):
    zh = lax.axis_index("zh")
    key = pick(k.get(), zh)
    value = pick(v.get(), zh)
    rate_row = one_of(r.get()[...], zh)
    fill(own_ref, key, value, rate_row, jnp.where(zh == 0, d.get()[:, 0:1], d.get()[:, 1:2]))
    for i, x in enumerate(fast_updates(key, value, rate_row, g, u, dt, step)):
        upd_ref[i] = x
    fold_queries(query_ref, pick(q.get(), zh))
    fold_queries(send_ref, pick(q.get(), 1 - zh))


def second_body(pair_kv, g, u, dt, step, upd, even_ref, send_ref, flat_ref):
    pay_ref = pair_kv.get().at[PAY:]
    others = fast_updates(
        pay_ref[0:BLK, 0:HD], pay_ref[0:BLK, HD:], tail(pay_ref)[:, :BLK], g, u, dt, step
    )
    zh = lax.axis_index("zh")
    upd_ref = upd.get()
    mine = tail(pair_kv.get())[:, BLK:]
    theirs = tail(pay_ref)[:, BLK:]
    keep_even = jnp.where(zh == 0, mine, theirs)
    keep_odd = jnp.where(zh == 0, theirs, mine)
    flat_ref[PAIRS * CHUNK :, :] = jnp.zeros((64, 128), F32)
    for i in range(3):
        other = others[i]
        own_upd = upd_ref[i]
        even = jnp.where(zh == 0, own_upd, other)
        odd = jnp.where(zh == 0, other, own_upd)
        even_ref[i] = even
        for j in range(3):
            cols = slice(j * 128, (j + 1) * 128)
            flat_ref[(3 * i + j) * HD : (3 * i + j + 1) * HD, :] = keep_odd * even[:, cols] + odd[:, cols]
    keep = three(jnp.broadcast_to(keep_even * keep_odd, (16, 128)))[0:4]
    for c in range(PAIRS):
        send_ref[c] = jnp.concatenate([flat_ref[c * CHUNK : (c + 1) * CHUNK, :], keep], axis=0).astype(BF16)


def scan_body(pieces, out_ref):
    in_ref = pieces.get()
    run = jnp.zeros((CROWS, 128), F32)
    for j in range(PAIRS):
        out_ref[j] = run.astype(BF16)
        if j < PAIRS - 1:
            here = in_ref[j].astype(F32)
            keep = here[CHUNK : CHUNK + 1] + here[CHUNK + 1 : CHUNK + 2] + here[CHUNK + 2 : CHUNK + 3]
            run = keep * run + here


def scores_of(q, keys, blocks, score_ref, rows_of, pair):
    row = lax.broadcasted_iota(jnp.int32, (BLK, BLK), 0)
    col = lax.broadcasted_iota(jnp.int32, (BLK, BLK), 1)
    top = None
    for n, (o, e, kind) in enumerate(blocks):
        s = nt(q, keys[o][rows_of(e), 0:HD]) * (1.0 / math.sqrt(HD))
        if kind == "oldest":
            s = jnp.where(col > row, s, -1e30)
        if kind == "newest":
            s = jnp.where(col <= row, s, -1e30)
        if o > 0:
            s = s + jnp.where(pair >= o, 0.0, -1e30)
        score_ref[n] = s
        top = s if top is None else jnp.maximum(top, s)
    return jnp.max(top, axis=1, keepdims=True)


def weighted(values, blocks, score_ref, rows_of, top):
    total = None
    acc = None
    for n, (o, e, _) in enumerate(blocks):
        w = jnp.exp(score_ref[n] - top)
        total = w if total is None else total + w
        part = nn(w.astype(BF16), values[o][rows_of(e), HD:])
        acc = part if acc is None else acc + part
    return jnp.sum(total, axis=1, keepdims=True), acc


def window_blocks(parity, offsets):
    blocks = [(o, e) for o in (4, 3, 2, 1, 0) for e in (0, 1)][parity : parity + 9]
    kinds = ["oldest"] + ["inner"] * 7 + ["newest"]
    return [(o, e, kind) for (o, e), kind in zip(blocks, kinds) if o in offsets]


def ordered_rows(zh):
    def rows_of(parity):
        slot = zh if parity == 0 else 1 - zh
        return pl.ds(pl.multiple_of(slot * PAY, 16), BLK)

    return rows_of


def pair_index():
    return lax.axis_index("x") * 4 + lax.axis_index("y")


def attend_first_body(own, recv, pair_kv, shifted, w1, acc_ref, stat_ref, score_ref):
    zh = lax.axis_index("zh")
    q_own = queries(own.get())
    q_recv = queries(recv.get())
    wins = {0: pair_kv.get(), 4: shifted.get(), 1: w1.get()}
    rows_of = ordered_rows(zh)
    lane = lax.broadcasted_iota(jnp.int32, (BLK, 128), 1)
    for parity in range(2):
        q = jnp.where(zh == parity, q_own, q_recv)
        blocks = window_blocks(parity, wins)
        scores = score_ref.at[parity]
        top = scores_of(q, wins, blocks, scores, rows_of, pair_index())
        total, acc = weighted(wins, blocks, scores, rows_of, top)
        acc_ref[parity] = acc
        stat_ref[parity] = jnp.where(lane < 64, top, total)


def attend_second_body(own, recv, w2, w3, acc_in, stat, gain_in, out_ref, score_ref):
    zh = lax.axis_index("zh")
    q_own = queries(own.get())
    q_recv = queries(recv.get())
    wins = {2: w2.get(), 3: w3.get()}
    gain = head_gain(gain_in, zh)
    rows_of = ordered_rows(zh)
    stats = stat.get()
    before = acc_in.get()
    for parity in range(2):
        q = jnp.where(zh == parity, q_own, q_recv)
        blocks = window_blocks(parity, wins)
        scores = score_ref.at[parity]
        old_top = stats[parity, :, 0:1]
        top = jnp.maximum(old_top, scores_of(q, wins, blocks, scores, rows_of, pair_index()))
        total, acc = weighted(wins, blocks, scores, rows_of, top)
        rescale = jnp.exp(old_top - top)
        total = total + rescale * stats[parity, :, 64:65]
        att = (acc + rescale * before[parity]) / total
        norm = lax.rsqrt(jnp.mean(att * att, axis=1, keepdims=True) + 1e-6)
        out_ref[parity] = att * norm * gain


def apply_body(pre, even, pair_kv, q_mine, q_theirs, g, u, dt, gain_in, att, out_ref, flat_ref):
    zh = lax.axis_index("zh")
    pre_ref, even_ref, own_ref, att_ref = [x.get() for x in (pre, even, pair_kv, att)]
    recv_ref = own_ref.at[PAY:]
    for c in range(PAIRS):
        flat_ref[c * CHUNK : (c + 1) * CHUNK, :] = pre_ref[c].astype(F32)[0:CHUNK]
    keep = jnp.where(zh == 0, tail(own_ref)[:, BLK : BLK + 1], tail(recv_ref)[:, BLK : BLK + 1])
    gain = head_gain(gain_in, zh)
    q_own = queries(q_mine.get())
    q_recv = queries(q_theirs.get())
    base = [x.get()[...] for x in (g, u, dt)]
    for parity in range(2):
        q = jnp.where(zh == parity, q_own, q_recv)
        qf = q.astype(F32)
        rq = lax.rsqrt(jnp.mean(qf * qf, axis=1, keepdims=True) + 1e-6)
        mats = []
        for i in range(3):
            state = jnp.concatenate(
                [flat_ref[(3 * i + j) * HD : (3 * i + j + 1) * HD, :] for j in range(3)], axis=1
            )
            if parity == 1:
                state = keep * state + even_ref[i]
            mats.append(split(base[i] + state))
        gate = rq * (nn(q, mats[0][0]) + nn(q, mats[0][1]))
        up = rq * (nn(q, mats[1][0]) + nn(q, mats[1][1]))
        applied = nt3(split(gate * jax.nn.sigmoid(gate) * up), mats[2])
        norm = lax.rsqrt(jnp.mean(applied * applied, axis=1, keepdims=True) + 1e-6)
        mixed = (applied * norm * gain + att_ref[parity]).astype(BF16)
        for c in range(2):
            for z in range(4):
                out_ref[c * 2 + parity, (z % 2) * 32 : (z % 2) * 32 + 32, (z // 2) * HD : (z // 2 + 1) * HD] = mixed[
                    z * 64 + c * 32 : z * 64 + c * 32 + 32
                ]


def project_body(mix, own_a, own_b, other_a, other_b, out_ref):
    core = lax.axis_index("c")
    mix_ref = mix.get()
    total = None
    for zh, w, which in ((0, own_a, core), (1, own_b, core), (0, other_a, 1 - core), (1, other_b, 1 - core)):
        rows = mix_ref[which * 2 + zh]
        rows = jnp.concatenate([rows[:, :HD], rows[:, HD:]], axis=0)
        rows = nn(rows, w.get()[...])
        total = rows if total is None else total + rows
    out_ref[...] = total.astype(BF16)


def total_body(parts, out_ref):
    ref = parts.get()
    out_ref[...] = sum(ref[i].astype(F32) for i in range(4)).astype(BF16)


def behind(pair_kv, distance):
    return lax.ppermute(pair_kv, ("x", "y"), [(i, i + distance) for i in range(PAIRS - distance)])


def head_gain(gain, zh):
    rows = gain.get()[...]
    first = jnp.concatenate([rows[0:1], rows[1:2, :64]], axis=1)
    second = jnp.concatenate([rows[1:2, 64:], rows[2:3]], axis=1)
    return jnp.where(zh == 0, first, second)


def local(q, k, v, rates, decay, step, gate, up, down, ttt_gain, attn_gain, proj):
    sds = jax.ShapeDtypeStruct
    pay = sds((PAY, FD), BF16)
    rates = rates.T
    down = jnp.swapaxes(down, 1, 2)
    step = step.reshape(1, 2)
    folded = sds((128, FD), BF16)
    (send,) = call(pack_body, [pay], (k, v, rates, decay), 0, 1_000_000)
    recv = lax.ppermute(send, "zh", [(0, 1), (1, 0)])
    proj_other = lax.ppermute(proj, "c", [(0, 1), (1, 0)])
    mats = sds((3, HD, FD), F32)
    flat = pltpu.VMEM((PAIRS * CHUNK + 64, 128), F32)
    upd, own, own_q, send_q = call(
        first_body,
        [mats, sds((2 * PAY, FD), BF16), folded, folded],
        (k, v, rates, decay, gate, up, down, step, q),
        6_000_000_000,
        3_000_000,
        mine=(4, 5, 6),
        head_rows={1: PAY},
    )
    pair_kv = lax.dynamic_update_slice(own, recv, (PAY, 0))
    pair_kv, proj_other = lax.optimization_barrier((pair_kv, proj_other))
    shifted = lax.ppermute(pair_kv, "x", [(i, i + 1) for i in range(3)])
    w1 = behind(pair_kv, 1)
    even, outgoing = call(
        second_body,
        [mats, sds((PAIRS, CROWS, 128), BF16)],
        (pair_kv, gate, up, down, step, upd),
        6_000_000_000,
        4_000_000,
        scratch=[flat],
        mine=(1, 2, 3),
    )
    even, later_kv, later_w1 = lax.optimization_barrier((even, pair_kv, w1))
    w2 = behind(later_w1, 1)
    w3 = behind(later_kv, 3)
    recv_q = lax.ppermute(send_q, "zh", [(0, 1), (1, 0)])
    outgoing, recv_q = lax.optimization_barrier((outgoing, recv_q))
    pieces = lax.all_to_all(outgoing, ("x", "y"), 0, 0, tiled=True)
    acc, stat = call(
        attend_first_body,
        [sds((2, BLK, HD), F32), sds((2, BLK, 128), F32)],
        (own_q, recv_q, pair_kv, shifted, w1),
        500_000_000,
        2_000_000,
        600_000,
        scratch=[pltpu.VMEM((2, 5, BLK, BLK), F32)],
    )
    pieces, acc = lax.optimization_barrier((pieces, acc))
    (sums,) = call(scan_body, [sds((PAIRS, CROWS, 128), BF16)], (pieces,), 500_000, 1_000_000, cap=SMALL)
    prefix = lax.all_to_all(sums, ("x", "y"), 0, 0, tiled=True)
    (att,) = call(
        attend_second_body,
        [sds((2, BLK, HD), F32)],
        (own_q, recv_q, w2, w3, acc, stat, attn_gain.reshape(3, 128)),
        500_000_000,
        2_000_000,
        600_000,
        scratch=[pltpu.VMEM((2, 4, BLK, BLK), F32)],
    )
    (mixed,) = call(
        apply_body,
        [sds((4, 64, FD), BF16)],
        (prefix, even, pair_kv, own_q, recv_q, gate, up, down, ttt_gain.reshape(3, 128), att),
        600_000_000,
        5_000_000,
        scratch=[flat],
        mine=(5, 6, 7),
    )
    mixed = lax.all_to_all(mixed, ("c", "zh"), 0, 0, tiled=True)
    own_w = proj.reshape(2, HD, WIDTH)
    other_w = proj_other.reshape(2, HD, WIDTH)
    (partial,) = call(
        project_body,
        [sds((128, WIDTH), BF16)],
        (mixed, own_w, own_w, other_w, other_w),
        600_000_000,
        6_000_000,
        part={1: 0, 2: 1, 3: 0, 4: 1},
    )
    parts = lax.all_to_all(partial.reshape(4, 32, WIDTH), "zl", 0, 0, tiled=True)
    (result,) = call(total_body, [sds((32, WIDTH), BF16)], (parts,), 400_000, 1_000_000, cap=SMALL)
    return result


def solution(mesh):
    fine = Mesh(mesh.devices.reshape(4, 4, 2, 4, 2), ("x", "y", "zh", "zl", "c"))
    seq = ("x", "y", "zh")
    head = ("zl", "c")
    in_specs = (
        P(seq, head),
        P(seq, head),
        P(seq, head),
        P(seq, head),
        P(seq, head),
        P(head),
        P(head, None, None),
        P(head, None, None),
        P(head, None, None),
        P(head),
        P(head),
        P(head, None),
    )
    out_specs = P(("x", "y", "zh", "zl", "c"), None)
    return jax.shard_map(local, mesh=fine, in_specs=in_specs, out_specs=out_specs, check_vma=False)
```

```python
import functools
import math

import jax
import jax.numpy as jnp
from jax import lax
from jax.experimental import pallas as pl
from jax.experimental.pallas import tpu as pltpu
from jax.sharding import Mesh, PartitionSpec as P

F32 = jnp.float32
BF16 = jnp.bfloat16
HD = 192
FD = 384
BLK = 256
WIDTH = 3072
NS_STEPS = 5
PAIRS = 16
CHUNK = 108
CROWS = 112
PAY = 272
COEF = (3.4445, -4.775, 2.0315)
VMEM_CAP = 60 * 1024 * 1024
SMALL = 12 * 1024 * 1024


class Lazy:
    def __init__(self, copy, ref):
        self.copy, self.ref = copy, ref

    def get(self):
        if self.copy is not None:
            self.copy.wait()
            self.copy = None
        return self.ref


def call(body, outs, ins, flops, nbytes, trans=0, scratch=(), mine=(), cap=VMEM_CAP, part=None, head_rows=None):
    part = part or {}
    head_rows = head_rows or {}
    outs = list(outs)
    n_in, n_out = len(ins), len(outs)
    shapes = [a.shape[1:] if i in mine or i in part else a.shape for i, a in enumerate(ins)]

    def kernel(*refs):
        in_refs, out_refs = refs[:n_in], refs[n_in : n_in + n_out]
        rest = refs[n_in + n_out :]
        in_vm, out_vm = rest[:n_in], rest[n_in : n_in + n_out]
        in_sem, out_sem, extra = rest[n_in + n_out], rest[n_in + n_out + 1], rest[n_in + n_out + 2 :]
        zh = lax.axis_index("zh")
        lazy = []
        for i in range(n_in):
            src = in_refs[i]
            if i in mine or i in part:
                src = src.at[part.get(i, zh)]
            copy = pltpu.make_async_copy(src, in_vm[i], in_sem.at[i])
            copy.start()
            lazy.append(Lazy(copy, in_vm[i]))
        copies = []
        for i in range(n_out):
            dst = out_refs[i].at[0 : head_rows[i]] if i in head_rows else out_refs[i]
            copies.append(pltpu.make_async_copy(out_vm[i], dst, out_sem.at[i]))
        body(*lazy, *out_vm, *extra)
        for copy in copies:
            copy.start()
        for item in lazy:
            item.get()
        for copy in copies:
            copy.wait()

    any_spec = pl.BlockSpec(memory_space=pltpu.MemorySpace.HBM)
    return pl.pallas_call(
        kernel,
        out_shape=outs,
        in_specs=[any_spec] * n_in,
        out_specs=[any_spec] * n_out,
        scratch_shapes=[pltpu.VMEM(sh, a.dtype) for sh, a in zip(shapes, ins)]
        + [pltpu.VMEM((head_rows.get(i, o.shape[0]),) + o.shape[1:], o.dtype) for i, o in enumerate(outs)]
        + [pltpu.SemaphoreType.DMA((n_in,)), pltpu.SemaphoreType.DMA((n_out,))]
        + list(scratch),
        compiler_params=pltpu.CompilerParams(vmem_limit_bytes=cap),
        cost_estimate=pl.CostEstimate(flops=flops, bytes_accessed=nbytes, transcendentals=trans),
    )(*ins)


def nn(a, b):
    return lax.dot_general(a, b, (((1,), (0,)), ((), ())), preferred_element_type=F32)


def nt(a, b):
    return lax.dot_general(a, b, (((1,), (1,)), ((), ())), preferred_element_type=F32)


def split(x):
    hi = x.astype(BF16)
    return hi, (x - hi.astype(F32)).astype(BF16)


def nn3(a, b):
    return nn(a[0], b[0]) + (nn(a[0], b[1]) + nn(a[1], b[0]))


def nt3(a, b):
    return nt(a[0], b[0]) + (nt(a[0], b[1]) + nt(a[1], b[0]))


def three(x):
    hi = x.astype(BF16).astype(F32)
    mid = (x - hi).astype(BF16).astype(F32)
    low = x - hi - mid
    row = lax.broadcasted_iota(jnp.int32, x.shape, 0)
    return jnp.where(row == 0, hi, jnp.where(row == 1, mid, jnp.where(row == 2, low, 0.0)))


def pick(ref, who):
    return jnp.where(who == 0, ref[:, :HD], ref[:, HD:])


def one_of(row, who):
    return jnp.where(who == 0, row[0:1], row[1:2])


def fill(out_ref, k, v, rate_row, decay):
    out_ref[0:BLK, 0:HD] = k
    out_ref[0:BLK, HD:] = v
    row = jnp.concatenate([rate_row, jnp.broadcast_to(decay, (1, 128))], axis=1)
    out_ref[BLK:PAY, :] = three(jnp.broadcast_to(row, (16, FD))).astype(BF16)


def fold_queries(out_ref, q):
    out_ref[:, 0:HD] = q[0:128]
    out_ref[:, HD:] = q[128:256]


def pack_body(k, v, r, d, send_ref):
    who = 1 - lax.axis_index("zh")
    fill(
        send_ref,
        pick(k.get(), who),
        pick(v.get(), who),
        one_of(r.get()[...], who),
        jnp.where(who == 0, d.get()[:, 0:1], d.get()[:, 1:2]),
    )


def tail(pay_ref):
    rows = pay_ref[BLK:PAY, :].astype(F32)
    return rows[0:1] + rows[1:2] + rows[2:3]


def queries(ref):
    both = ref[...]
    return jnp.concatenate([both[:, :HD], both[:, HD:]], axis=0)


def orthogonalize(mats):
    norms = [jnp.sqrt(jnp.sum(m * m, keepdims=True)) + 1e-7 for m in mats]
    mats = [m / n for m, n in zip(mats, norms)]
    for _ in range(NS_STEPS):
        parts = [split(x) for x in mats]
        grams = []
        for hi, lo in parts:
            cross = nt(hi, lo)
            grams.append(nt(hi, hi) + (cross + cross.T))
        polys = []
        for gram in grams:
            hi, lo = split(gram)
            cross = nn(hi, lo)
            polys.append(split(COEF[1] * gram + COEF[2] * (nn(hi, hi) + (cross + cross.T))))
        mats = [COEF[0] * x + nn3(p, s) for x, p, s in zip(mats, polys, parts)]
    return mats


def fast_updates(k, v, rate_row, g, u, dt, step):
    kf = k.astype(F32)
    rk = lax.rsqrt(jnp.mean(kf * kf, axis=1, keepdims=True) + 1e-6)
    rate = jnp.broadcast_to(rate_row, (128, BLK)).T[:, 0:1]
    gh, gl = split(g.get()[...])
    pre_gate = rk * (nn(k, gh) + nn(k, gl))
    uh, ul = split(u.get()[...])
    pre_up = rk * (nn(k, uh) + nn(k, ul))
    dh, dl = split(dt.get()[...])
    back = -rate * (nn(v, dh) + nn(v, dl))
    sig = jax.nn.sigmoid(pre_gate)
    act = pre_gate * sig
    mid_h, mid_l = split(-rate * (act * pre_up))
    gate_h, gate_l = split(rk * (back * pre_up * (sig * (1.0 + pre_gate * (1.0 - sig)))))
    up_h, up_l = split(rk * (back * act))
    kt = k.T
    vt = v.T
    grads = [
        nn(kt, gate_h) + nn(kt, gate_l),
        nn(kt, up_h) + nn(kt, up_l),
        nn(vt, mid_h) + nn(vt, mid_l),
    ]
    row = step.get()[...]
    scale = -jnp.where(lax.axis_index("zh") == 0, row[:, 0:1], row[:, 1:2])
    return [scale * x for x in orthogonalize(grads)]


def first_body(k, v, r, d, g, u, dt, step, q, upd_ref, own_ref, query_ref, send_ref):
    zh = lax.axis_index("zh")
    key = pick(k.get(), zh)
    value = pick(v.get(), zh)
    rate_row = one_of(r.get()[...], zh)
    fill(own_ref, key, value, rate_row, jnp.where(zh == 0, d.get()[:, 0:1], d.get()[:, 1:2]))
    for i, x in enumerate(fast_updates(key, value, rate_row, g, u, dt, step)):
        upd_ref[i] = x
    fold_queries(query_ref, pick(q.get(), zh))
    fold_queries(send_ref, pick(q.get(), 1 - zh))


def second_body(pair_kv, g, u, dt, step, upd, even_ref, send_ref, flat_ref):
    pay_ref = pair_kv.get().at[PAY:]
    others = fast_updates(
        pay_ref[0:BLK, 0:HD], pay_ref[0:BLK, HD:], tail(pay_ref)[:, :BLK], g, u, dt, step
    )
    zh = lax.axis_index("zh")
    upd_ref = upd.get()
    mine = tail(pair_kv.get())[:, BLK:]
    theirs = tail(pay_ref)[:, BLK:]
    keep_even = jnp.where(zh == 0, mine, theirs)
    keep_odd = jnp.where(zh == 0, theirs, mine)
    flat_ref[PAIRS * CHUNK :, :] = jnp.zeros((64, 128), F32)
    for i in range(3):
        other = others[i]
        own_upd = upd_ref[i]
        even = jnp.where(zh == 0, own_upd, other)
        odd = jnp.where(zh == 0, other, own_upd)
        even_ref[i] = even
        for j in range(3):
            cols = slice(j * 128, (j + 1) * 128)
            flat_ref[(3 * i + j) * HD : (3 * i + j + 1) * HD, :] = keep_odd * even[:, cols] + odd[:, cols]
    keep = three(jnp.broadcast_to(keep_even * keep_odd, (16, 128)))[0:4]
    for c in range(PAIRS):
        send_ref[c] = jnp.concatenate([flat_ref[c * CHUNK : (c + 1) * CHUNK, :], keep], axis=0).astype(BF16)


def scan_body(pieces, out_ref):
    in_ref = pieces.get()
    run = jnp.zeros((CROWS, 128), F32)
    for j in range(PAIRS):
        out_ref[j] = run.astype(BF16)
        if j < PAIRS - 1:
            here = in_ref[j].astype(F32)
            keep = here[CHUNK : CHUNK + 1] + here[CHUNK + 1 : CHUNK + 2] + here[CHUNK + 2 : CHUNK + 3]
            run = keep * run + here


def scores_of(q, keys, blocks, score_ref, rows_of, pair):
    row = lax.broadcasted_iota(jnp.int32, (BLK, BLK), 0)
    col = lax.broadcasted_iota(jnp.int32, (BLK, BLK), 1)
    top = None
    for n, (o, e, kind) in enumerate(blocks):
        s = nt(q, keys[o][rows_of(e), 0:HD]) * (1.0 / math.sqrt(HD))
        if kind == "oldest":
            s = jnp.where(col > row, s, -1e30)
        if kind == "newest":
            s = jnp.where(col <= row, s, -1e30)
        if o > 0:
            s = s + jnp.where(pair >= o, 0.0, -1e30)
        score_ref[n] = s
        top = s if top is None else jnp.maximum(top, s)
    return jnp.max(top, axis=1, keepdims=True)


def weighted(values, blocks, score_ref, rows_of, top):
    total = None
    acc = None
    for n, (o, e, _) in enumerate(blocks):
        w = jnp.exp(score_ref[n] - top)
        total = w if total is None else total + w
        part = nn(w.astype(BF16), values[o][rows_of(e), HD:])
        acc = part if acc is None else acc + part
    return jnp.sum(total, axis=1, keepdims=True), acc


def window_blocks(parity, offsets):
    blocks = [(o, e) for o in (4, 3, 2, 1, 0) for e in (0, 1)][parity : parity + 9]
    kinds = ["oldest"] + ["inner"] * 7 + ["newest"]
    return [(o, e, kind) for (o, e), kind in zip(blocks, kinds) if o in offsets]


def ordered_rows(zh):
    def rows_of(parity):
        slot = zh if parity == 0 else 1 - zh
        return pl.ds(pl.multiple_of(slot * PAY, 16), BLK)

    return rows_of


def pair_index():
    return lax.axis_index("x") * 4 + lax.axis_index("y")


def attend_first_body(own, recv, pair_kv, shifted, w1, w3, acc_ref, stat_ref, score_ref):
    zh = lax.axis_index("zh")
    q_own = queries(own.get())
    q_recv = queries(recv.get())
    wins = {0: pair_kv.get(), 4: shifted.get(), 1: w1.get(), 3: w3.get()}
    rows_of = ordered_rows(zh)
    lane = lax.broadcasted_iota(jnp.int32, (BLK, 128), 1)
    for parity in range(2):
        q = jnp.where(zh == parity, q_own, q_recv)
        blocks = window_blocks(parity, wins)
        scores = score_ref.at[parity]
        top = scores_of(q, wins, blocks, scores, rows_of, pair_index())
        total, acc = weighted(wins, blocks, scores, rows_of, top)
        acc_ref[parity] = acc
        stat_ref[parity] = jnp.where(lane < 64, top, total)


def attend_second_body(own, recv, w2, acc_in, stat, gain_in, out_ref, score_ref):
    zh = lax.axis_index("zh")
    q_own = queries(own.get())
    q_recv = queries(recv.get())
    wins = {2: w2.get()}
    gain = head_gain(gain_in, zh)
    rows_of = ordered_rows(zh)
    stats = stat.get()
    before = acc_in.get()
    for parity in range(2):
        q = jnp.where(zh == parity, q_own, q_recv)
        blocks = window_blocks(parity, wins)
        scores = score_ref.at[parity]
        old_top = stats[parity, :, 0:1]
        top = jnp.maximum(old_top, scores_of(q, wins, blocks, scores, rows_of, pair_index()))
        total, acc = weighted(wins, blocks, scores, rows_of, top)
        rescale = jnp.exp(old_top - top)
        total = total + rescale * stats[parity, :, 64:65]
        att = (acc + rescale * before[parity]) / total
        norm = lax.rsqrt(jnp.mean(att * att, axis=1, keepdims=True) + 1e-6)
        out_ref[parity] = att * norm * gain


def apply_body(pre, even, pair_kv, q_mine, q_theirs, g, u, dt, gain_in, att, out_ref, flat_ref):
    zh = lax.axis_index("zh")
    pre_ref, even_ref, own_ref, att_ref = [x.get() for x in (pre, even, pair_kv, att)]
    recv_ref = own_ref.at[PAY:]
    for c in range(PAIRS):
        flat_ref[c * CHUNK : (c + 1) * CHUNK, :] = pre_ref[c].astype(F32)[0:CHUNK]
    keep = jnp.where(zh == 0, tail(own_ref)[:, BLK : BLK + 1], tail(recv_ref)[:, BLK : BLK + 1])
    gain = head_gain(gain_in, zh)
    q_own = queries(q_mine.get())
    q_recv = queries(q_theirs.get())
    base = [x.get()[...] for x in (g, u, dt)]
    for parity in range(2):
        q = jnp.where(zh == parity, q_own, q_recv)
        qf = q.astype(F32)
        rq = lax.rsqrt(jnp.mean(qf * qf, axis=1, keepdims=True) + 1e-6)
        mats = []
        for i in range(3):
            state = jnp.concatenate(
                [flat_ref[(3 * i + j) * HD : (3 * i + j + 1) * HD, :] for j in range(3)], axis=1
            )
            if parity == 1:
                state = keep * state + even_ref[i]
            mats.append(split(base[i] + state))
        gate = rq * (nn(q, mats[0][0]) + nn(q, mats[0][1]))
        up = rq * (nn(q, mats[1][0]) + nn(q, mats[1][1]))
        applied = nt3(split(gate * jax.nn.sigmoid(gate) * up), mats[2])
        norm = lax.rsqrt(jnp.mean(applied * applied, axis=1, keepdims=True) + 1e-6)
        mixed = (applied * norm * gain + att_ref[parity]).astype(BF16)
        for c in range(2):
            for z in range(4):
                out_ref[c * 2 + parity, (z % 2) * 32 : (z % 2) * 32 + 32, (z // 2) * HD : (z // 2 + 1) * HD] = mixed[
                    z * 64 + c * 32 : z * 64 + c * 32 + 32
                ]


def project_body(mix, own_a, own_b, other_a, other_b, out_ref):
    core = lax.axis_index("c")
    mix_ref = mix.get()
    total = None
    for zh, w, which in ((0, own_a, core), (1, own_b, core), (0, other_a, 1 - core), (1, other_b, 1 - core)):
        rows = mix_ref[which * 2 + zh]
        rows = jnp.concatenate([rows[:, :HD], rows[:, HD:]], axis=0)
        rows = nn(rows, w.get()[...])
        total = rows if total is None else total + rows
    out_ref[...] = total.astype(BF16)


def total_body(parts, out_ref):
    ref = parts.get()
    out_ref[...] = sum(ref[i].astype(F32) for i in range(4)).astype(BF16)


def behind(pair_kv, distance):
    return lax.ppermute(pair_kv, ("x", "y"), [(i, i + distance) for i in range(PAIRS - distance)])


def head_gain(gain, zh):
    rows = gain.get()[...]
    first = jnp.concatenate([rows[0:1], rows[1:2, :64]], axis=1)
    second = jnp.concatenate([rows[1:2, 64:], rows[2:3]], axis=1)
    return jnp.where(zh == 0, first, second)


def local(q, k, v, rates, decay, step, gate, up, down, ttt_gain, attn_gain, proj):
    sds = jax.ShapeDtypeStruct
    pay = sds((PAY, FD), BF16)
    rates = rates.T
    down = jnp.swapaxes(down, 1, 2)
    step = step.reshape(1, 2)
    folded = sds((128, FD), BF16)
    (send,) = call(pack_body, [pay], (k, v, rates, decay), 0, 1_000_000)
    recv = lax.ppermute(send, "zh", [(0, 1), (1, 0)])
    proj_other = lax.ppermute(proj, "c", [(0, 1), (1, 0)])
    mats = sds((3, HD, FD), F32)
    flat = pltpu.VMEM((PAIRS * CHUNK + 64, 128), F32)
    upd, own, own_q, send_q = call(
        first_body,
        [mats, sds((2 * PAY, FD), BF16), folded, folded],
        (k, v, rates, decay, gate, up, down, step, q),
        6_000_000_000,
        3_000_000,
        mine=(4, 5, 6),
        head_rows={1: PAY},
    )
    pair_kv = lax.dynamic_update_slice(own, recv, (PAY, 0))
    pair_kv, proj_other = lax.optimization_barrier((pair_kv, proj_other))
    shifted = lax.ppermute(pair_kv, "x", [(i, i + 1) for i in range(3)])
    w1 = behind(pair_kv, 1)
    w3 = behind(pair_kv, 3)
    even, outgoing = call(
        second_body,
        [mats, sds((PAIRS, CROWS, 128), BF16)],
        (pair_kv, gate, up, down, step, upd),
        6_000_000_000,
        4_000_000,
        scratch=[flat],
        mine=(1, 2, 3),
    )
    even, later_w1 = lax.optimization_barrier((even, w1))
    w2 = behind(later_w1, 1)
    recv_q = lax.ppermute(send_q, "zh", [(0, 1), (1, 0)])
    outgoing, recv_q = lax.optimization_barrier((outgoing, recv_q))
    pieces = lax.all_to_all(outgoing, ("x", "y"), 0, 0, tiled=True)
    acc, stat = call(
        attend_first_body,
        [sds((2, BLK, HD), F32), sds((2, BLK, 128), F32)],
        (own_q, recv_q, pair_kv, shifted, w1, w3),
        500_000_000,
        2_000_000,
        600_000,
        scratch=[pltpu.VMEM((2, 7, BLK, BLK), F32)],
    )
    pieces, acc = lax.optimization_barrier((pieces, acc))
    (sums,) = call(scan_body, [sds((PAIRS, CROWS, 128), BF16)], (pieces,), 500_000, 1_000_000, cap=SMALL)
    prefix = lax.all_to_all(sums, ("x", "y"), 0, 0, tiled=True)
    (att,) = call(
        attend_second_body,
        [sds((2, BLK, HD), F32)],
        (own_q, recv_q, w2, acc, stat, attn_gain.reshape(3, 128)),
        500_000_000,
        2_000_000,
        600_000,
        scratch=[pltpu.VMEM((2, 2, BLK, BLK), F32)],
    )
    (mixed,) = call(
        apply_body,
        [sds((4, 64, FD), BF16)],
        (prefix, even, pair_kv, own_q, recv_q, gate, up, down, ttt_gain.reshape(3, 128), att),
        600_000_000,
        5_000_000,
        scratch=[flat],
        mine=(5, 6, 7),
    )
    mixed = lax.all_to_all(mixed, ("c", "zh"), 0, 0, tiled=True)
    own_w = proj.reshape(2, HD, WIDTH)
    other_w = proj_other.reshape(2, HD, WIDTH)
    (partial,) = call(
        project_body,
        [sds((128, WIDTH), BF16)],
        (mixed, own_w, own_w, other_w, other_w),
        600_000_000,
        6_000_000,
        part={1: 0, 2: 1, 3: 0, 4: 1},
    )
    parts = lax.all_to_all(partial.reshape(4, 32, WIDTH), "zl", 0, 0, tiled=True)
    (result,) = call(total_body, [sds((32, WIDTH), BF16)], (parts,), 400_000, 1_000_000, cap=SMALL)
    return result


def solution(mesh):
    fine = Mesh(mesh.devices.reshape(4, 4, 2, 4, 2), ("x", "y", "zh", "zl", "c"))
    seq = ("x", "y", "zh")
    head = ("zl", "c")
    in_specs = (
        P(seq, head),
        P(seq, head),
        P(seq, head),
        P(seq, head),
        P(seq, head),
        P(head),
        P(head, None, None),
        P(head, None, None),
        P(head, None, None),
        P(head),
        P(head),
        P(head, None),
    )
    out_specs = P(("x", "y", "zh", "zl", "c"), None)
    return jax.shard_map(local, mesh=fine, in_specs=in_specs, out_specs=out_specs, check_vma=False)
```
